32 devices in a mesh: dp: 8 (over z, y), fsdp: 4 (over x, core).
Axes of the slice: x: 2, y: 2, z: 4, core: 2. Of those that a mesh axis runs over, the one named last changes fastest.
Arguments:
- patches: bfloat16 [128, 324, 768], P(('dp', 'fsdp')), may hold values from -6 to 6
- groups: int32 [128], P(('dp', 'fsdp')), may hold values from 0 to 2, as said below
- labels: int32 [128], P(('dp', 'fsdp')), may hold values from 0 to 999
- wide_w: float32 [3, 192, 1536], P(None, None, ('dp', 'fsdp')), may hold values from -0.4375 to 0.4375
- down_w: float32 [3, 768, 192], P(None, ('dp', 'fsdp')), may hold values from -0.21875 to 0.21875
- plain: float32 [409408], P(('dp', 'fsdp'))
- wide_mom: float32 [3, 192, 1536], P(None, None, ('dp', 'fsdp')), may hold values from -9.1552734e-05 to 9.1552734e-05
- down_mom: float32 [3, 768, 192], P(None, ('dp', 'fsdp')), may hold values from -9.1552734e-05 to 9.1552734e-05
- plain_first: float32 [409408], P(('dp', 'fsdp')), may hold values from -9.1552734e-05 to 9.1552734e-05
- plain_second: float32 [409408], P(('dp', 'fsdp')), may hold values from 5.7586705e-12 to 2.3034681e-10
- basis_plain: float32 [64, 409408], P(None, ('dp', 'fsdp')), may hold values from -1 to 1, as said below
Outputs:
- loss_sum: float32 [], replicated
- removed_norm: float32 [], replicated
- grad_norm: float32 [], replicated
- wide_new: float32 [3, 192, 1536], P(None, None, ('dp', 'fsdp'))
- wide_mom_new: float32 [3, 192, 1536], P(None, None, ('dp', 'fsdp'))
- wide_copy: bfloat16 [3, 192, 1536], P(None, None, ('dp', 'fsdp'))
- down_new: float32 [3, 768, 192], P(None, ('dp', 'fsdp'))
- down_mom_new: float32 [3, 768, 192], P(None, ('dp', 'fsdp'))
- down_copy: bfloat16 [3, 768, 192], P(None, ('dp', 'fsdp'))
- plain_new: float32 [409408], P(('dp', 'fsdp'))
- plain_first_new: float32 [409408], P(('dp', 'fsdp'))
- plain_second_new: float32 [409408], P(('dp', 'fsdp'))
- plain_copy: bfloat16 [409408], P(('dp', 'fsdp'))
The draws below stay inside these ranges and needn't reach their ends.
Inputs may be any that keep to these rules, and one draw needn't show every extreme that they name: `groups`: 0 for images of 101 tokens, 1 for 197, 2 for 325; every group occurs. `basis_plain`: the rows are orthonormal; every entry outside the final gain, the final shift and the head bias is zero.
All inputs are finite; a program needn't handle non-finite values.
Results may differ from the reference program's by a relative error of at most 0.01.
Values may be sent and summed in bfloat16 or wider, within the bound.
No kernel may reach another device: no remote copies, remote signals or barrier semaphores. Data moves between devices by JAX's collectives and lax.ppermute only.
A program may use at most 128 MiB of HBM per device.

```python
import math
import jax
import jax.numpy as jnp
from jax import lax

D = 192
HEADS = 3
HD = 64
FF = 768
PATCH_DIM = 768
CLASSES = 1000
LAYERS = 3
SEQ = 325
LEN_MID = 197
LEN_SHORT = 101
BASIS = 64
STEP = 10
IMG_DEV = 4
IMAGES = 128
WIDE = 1536
PLAIN = 409408
PTOTAL = 1736512


def draw_plain(key, part):
    key = jax.random.fold_in(key, 5)
    layout = [(PATCH_DIM * D, 1.0 / PATCH_DIM ** 0.5, 0.0), (D * CLASSES, 2.0 / D ** 0.5, 0.0), (D, 1.0, 0.0), (D, 0.2, 0.0), (SEQ * D, 0.5, 0.0)]
    per_layer = [(D, 0.2, 1.0), (D, 0.2, 0.0), (D, 0.2, 0.0), (D, 0.2, 1.0), (D, 0.2, 0.0), (D, 0.2, 0.0), (FF, 0.2, 0.0)]
    layout = layout + per_layer * LAYERS + [(D, 0.2, 1.0), (D, 0.2, 0.0), (CLASSES, 0.5, 0.0)]
    used_entries = sum([entry[0] for entry in layout])
    layout = layout + [(PLAIN - used_entries, 0.1, 0.0)]
    scales = jnp.concatenate([jnp.full((entry[0],), entry[1], jnp.float32) for entry in layout])
    shifts = jnp.concatenate([jnp.full((entry[0],), entry[2], jnp.float32) for entry in layout])
    noise = jax.random.normal(key, (PLAIN,), jnp.float32)
    return noise * scales + shifts


def draw_groups(key, part):
    key = jax.random.fold_in(key, 7)
    holders = IMAGES // IMG_DEV
    spread = jax.random.randint(key, (IMAGES,), 0, 2 * holders)
    holder = jnp.arange(IMAGES, dtype=jnp.int32) // IMG_DEV
    chosen = jnp.minimum((holder + spread) // holders, 2)
    chosen = chosen.at[0].set(0).at[IMAGES - 1].set(2)
    return chosen.astype(jnp.int32)


def draw_basis_plain(key, part):
    key = jax.random.fold_in(key, 11)
    block_width = 2 * D + CLASSES
    block_start = PATCH_DIM * D + D * CLASSES + 2 * D + SEQ * D + LAYERS * (6 * D + FF)
    source = jax.random.normal(key, (BASIS, block_width), jnp.float32)
    finished = []
    for row_number in range(BASIS):
        vector = source[row_number]
        for sweep in range(2):
            if finished:
                stacked = jnp.stack(finished)
                inner = jnp.dot(stacked, vector, precision=lax.Precision.HIGHEST)
                vector = vector - jnp.dot(inner, stacked, precision=lax.Precision.HIGHEST)
        vector = vector / jnp.sqrt(jnp.sum(vector * vector))
        finished.append(vector)
    block = jnp.stack(finished)
    before = jnp.zeros((BASIS, block_start), jnp.float32)
    after = jnp.zeros((BASIS, PLAIN - block_start - block_width), jnp.float32)
    return jnp.concatenate([before, block, after], 1)


def touch_ends(drawn, own_key, low, largest):
    longest = drawn.shape.index(max(drawn.shape))
    spots = []
    for shift in (0, 1):
        where = [jax.random.randint(jax.random.fold_in(own_key, axis), (), 0, length) for axis, length in enumerate(drawn.shape)]
        where[longest] = (where[longest] + shift) % drawn.shape[longest]
        spots.append(tuple(where))
    return drawn.at[spots[0]].set(low).at[spots[1]].set(largest)


def shard_levels(rng, extent, split, low, largest):
    factor_of = 1.0
    for dim, shards_of in split:
        heights = jax.random.uniform(jax.random.fold_in(jax.random.fold_in(rng, 6), dim), (shards_of,), jnp.float32, low / len(split), largest / len(split))
        factor_of = factor_of * jnp.repeat(jnp.exp(heights), extent[dim] // shards_of).reshape((-1,) + (1,) * (len(extent) - 1 - dim))
    return factor_of


def gaussian(key, dims, scale, limit, cuts=(), held_as=jnp.bfloat16):
    level = shard_levels(key, dims, cuts, -0.22, 0.18) if cuts else 1.0
    values = jax.random.normal(key, dims, jnp.float32) * scale * level
    return jnp.minimum(jnp.maximum(values, -limit), limit).astype(held_as)


def setup_inputs(seed: int = 0) -> dict:
    keys = jax.random.split(jax.random.key(seed), 12)
    patches = gaussian(keys[0], (IMAGES, SEQ - 1, PATCH_DIM), 1.0, 6.0, ((0, 32),))
    groups = draw_groups(jax.random.fold_in(keys[11], 71), 0)
    labels = touch_ends(jax.random.randint(keys[2], (IMAGES,), 0, CLASSES), jax.random.fold_in(keys[2], 1), 0, CLASSES - 1).astype(jnp.int32)
    wide_w = gaussian(keys[3], (LAYERS, D, WIDE), D ** -0.5, 0.4375, ((2, 32),), jnp.float32)
    down_w = gaussian(keys[4], (LAYERS, FF, D), FF ** -0.5, 0.21875, ((1, 32),), jnp.float32)
    plain = draw_plain(jax.random.fold_in(keys[11], 71), 0)
    wide_mom = gaussian(keys[6], (LAYERS, D, WIDE), (0.02 / PTOTAL ** 0.5), 9.1552734375e-05, ((2, 32),), jnp.float32)
    down_mom = gaussian(keys[7], (LAYERS, FF, D), (0.02 / PTOTAL ** 0.5), 9.1552734375e-05, ((1, 32),), jnp.float32)
    plain_first = gaussian(keys[8], (PLAIN,), (0.02 / PTOTAL ** 0.5), 9.1552734375e-05, ((0, 32),), jnp.float32)
    plain_second = jnp.clip(jnp.exp(math.log(2.303468110698148e-10) - 3.6888794 * jax.random.uniform(keys[9], (PLAIN,), jnp.float32) ** shard_levels(keys[9], (PLAIN,), ((0, 32),), -0.2, 0.2)), 5.758670450217718e-12, 2.303468110698148e-10)
    basis_plain = draw_basis_plain(jax.random.fold_in(keys[11], 71), 0)
    return dict(patches=patches, groups=groups, labels=labels, wide_w=wide_w, down_w=down_w, plain=plain, wide_mom=wide_mom, down_mom=down_mom, plain_first=plain_first, plain_second=plain_second, basis_plain=basis_plain)


@jax.custom_vjp
def low(v):
    return lax.optimization_barrier(v.astype(jnp.bfloat16)).astype(jnp.float32)

@jax.custom_vjp
def low_back(v):
    return v

def low_keep(v):
    return (low(v), None)

def low_pass(kept, grad):
    return (grad,)

def back_keep(v):
    return (v, None)

def back_low(kept, grad):
    return (low(grad),)
low.defvjp(low_keep, low_pass)
low_back.defvjp(back_keep, back_low)
HIGH = lax.Precision.HIGHEST
NORM_EPS = 1e-06
CLIP_AT = 0.02
MUON_RATE = 0.3
ADAM_RATE = 0.05
BETA_ONE = 0.5
BETA_TWO = 0.95
DECAY_RATE = 0.01
ADAM_EPS = 1e-08
SHAPE_EPS = 1e-07
MASKED = -1e+30

def pieces(flat_params):
    layout = [('patch_w', PATCH_DIM * D, (PATCH_DIM, D)), ('head_w', D * CLASSES, (D, CLASSES)), ('cls_token', D, (D,)), ('patch_b', D, (D,)), ('position', SEQ * D, (SEQ, D)), ('layer_vec', LAYERS * (6 * D + FF), (LAYERS, 6 * D + FF)), ('final', 2 * D, (2, D)), ('head_b', CLASSES, (CLASSES,))]
    found = {}
    offset = 0
    for entry_name, entry_size, entry_shape in layout:
        found[entry_name] = flat_params[offset:offset + entry_size].reshape(entry_shape)
        offset += entry_size
    return found

def normalize(stream, gain, shift):
    average = lax.optimization_barrier(jnp.mean(stream, -1, keepdims=True))
    centered = stream - average
    variance = lax.optimization_barrier(jnp.mean(centered * centered, -1, keepdims=True))
    return centered * lax.rsqrt(variance + NORM_EPS) * gain + shift

def matmul(left, right):
    return low_back(jnp.einsum('...i,ij->...j', low(left), low(right), precision=HIGH))

def layer_apply(stream, wide, down, vectors, key_valid):
    first_gain, first_shift, out_bias, second_gain, second_shift, down_bias = vectors[:6 * D].reshape(6, D)
    up_bias = vectors[6 * D:]
    batch_size = stream.shape[0]
    projected = matmul(normalize(stream, first_gain, first_shift), wide[:, :3 * D])
    queries = low(projected[..., :D] * HD ** (-0.5)).reshape(batch_size, SEQ, HEADS, HD)
    key_rows = low(projected[..., D:2 * D]).reshape(batch_size, SEQ, HEADS, HD)
    value_rows = low(projected[..., 2 * D:]).reshape(batch_size, SEQ, HEADS, HD)
    scores = low_back(jnp.einsum('bqhd,bkhd->bhqk', queries, key_rows, precision=HIGH))
    scores = jnp.where(key_valid[:, None, None, :] > 0, scores, MASKED)
    attention = jax.nn.softmax(scores, -1)
    mixture = low_back(jnp.einsum('bhqk,bkhd->bqhd', low(attention), value_rows, precision=HIGH)).reshape(batch_size, SEQ, D)
    middle = stream + matmul(mixture, wide[:, 3 * D:4 * D]) + out_bias
    active = jax.nn.gelu(matmul(normalize(middle, second_gain, second_shift), wide[:, 4 * D:]) + up_bias, approximate=True)
    return middle + matmul(active, down) + down_bias

def block_loss(weights, image_block):
    wide_w, down_w, plain = weights
    patches, key_valid, labels = image_block
    found = pieces(plain)
    embedded = matmul(patches, found['patch_w']) + found['patch_b']
    batch_size = patches.shape[0]
    leading = jnp.broadcast_to(found['cls_token'], (batch_size, 1, D))
    stream = jnp.concatenate([leading, embedded], 1) + found['position']
    for layer_index in range(LAYERS):
        stream = layer_apply(stream, wide_w[layer_index], down_w[layer_index], found['layer_vec'][layer_index], key_valid)
    final_normed = normalize(stream[:, 0], found['final'][0], found['final'][1])
    logits = matmul(final_normed, found['head_w']) + found['head_b']
    log_probs = jax.nn.log_softmax(logits, -1)
    onehot = (labels[:, None] == jnp.arange(CLASSES)[None, :]).astype(jnp.float32)
    return -jnp.sum(log_probs * onehot)

def total_loss(wide_w, down_w, plain, patches, key_valid, labels):
    blocks = (patches.reshape(IMAGES // 8, 8, SEQ - 1, PATCH_DIM), key_valid.reshape(IMAGES // 8, 8, SEQ), labels.reshape(IMAGES // 8, 8))
    checked = jax.checkpoint(block_loss)

    def accumulate(running, image_block):
        return (running + checked((wide_w, down_w, plain), image_block), None)
    running, unused = lax.scan(accumulate, jnp.zeros((), jnp.float32), blocks)
    return running

def orthogonalize(matrix):
    height, breadth = matrix.shape
    iterate = matrix.T if height > breadth else matrix
    iterate = iterate / (jnp.sqrt(jnp.sum(iterate * iterate)) + SHAPE_EPS)
    for iteration in range(5):
        gram_matrix = jnp.dot(iterate, iterate.T, precision=HIGH)
        polynomial = -4.775 * gram_matrix + 2.0315 * jnp.dot(gram_matrix, gram_matrix, precision=HIGH)
        iterate = 3.4445 * iterate + jnp.dot(polynomial, iterate, precision=HIGH)
    iterate = iterate.T if height > breadth else iterate
    return iterate * (MUON_RATE * 0.2 * max(height, breadth) ** 0.5)

def muon_updates(wide_all, down_all):
    wide_list = []
    down_list = []
    for layer_index in range(LAYERS):
        segments = [orthogonalize(wide_all[layer_index, :, column_start:column_stop]) for column_start, column_stop in ((0, 3 * D), (3 * D, 4 * D), (4 * D, 4 * D + FF))]
        wide_list.append(jnp.concatenate(segments, 1))
        down_list.append(orthogonalize(down_all[layer_index]))
    return (jnp.stack(wide_list), jnp.stack(down_list))

def reference(patches, groups, labels, wide_w, down_w, plain, wide_mom, down_mom, plain_first, plain_second, basis_plain):
    length = jnp.where(groups == 0, LEN_SHORT, jnp.where(groups == 1, LEN_MID, SEQ)).astype(jnp.int32)
    key_valid = (jnp.arange(SEQ, dtype=jnp.int32)[None, :] < length[:, None]).astype(jnp.int32)
    patch_float = patches.astype(jnp.float32)

    def loss_of(wide_value, down_value, plain_value):
        return total_loss(wide_value, down_value, plain_value, patch_float, key_valid, labels)
    loss_sum, pull = jax.vjp(loss_of, wide_w, down_w, plain)
    wide_grad, down_grad, plain_grad = pull(jnp.float32(1.0 / IMAGES))
    coefficients = jnp.einsum('kp,p->k', basis_plain, plain_grad, precision=HIGH)
    removed_norm = jnp.sqrt(jnp.sum(coefficients * coefficients))
    plain_grad = plain_grad - jnp.einsum('kp,k->p', basis_plain, coefficients, precision=HIGH)
    square_sum = jnp.sum(wide_grad * wide_grad) + jnp.sum(down_grad * down_grad) + jnp.sum(plain_grad * plain_grad)
    grad_norm = jnp.sqrt(square_sum)
    factor = CLIP_AT / jnp.maximum(grad_norm, CLIP_AT)
    wide_grad = wide_grad * factor
    down_grad = down_grad * factor
    plain_grad = plain_grad * factor
    wide_mom_new = BETA_ONE * wide_mom + wide_grad
    down_mom_new = BETA_ONE * down_mom + down_grad
    wide_update, down_update = muon_updates(wide_mom_new, down_mom_new)
    wide_new = wide_w - wide_update
    down_new = down_w - down_update
    first_new = BETA_ONE * plain_first + (1.0 - BETA_ONE) * plain_grad
    second_new = BETA_TWO * plain_second + (1.0 - BETA_TWO) * plain_grad * plain_grad
    first_hat = first_new / (1.0 - BETA_ONE ** STEP)
    second_hat = second_new / (1.0 - BETA_TWO ** STEP)
    plain_new = plain - ADAM_RATE * (first_hat / (jnp.sqrt(second_hat) + ADAM_EPS) + DECAY_RATE * plain)
    return (loss_sum, removed_norm, grad_norm, wide_new, wide_mom_new, wide_new.astype(jnp.bfloat16), down_new, down_mom_new, down_new.astype(jnp.bfloat16), plain_new, first_new, second_new, plain_new.astype(jnp.bfloat16))
```

```python
import functools
import math

import jax
import jax.numpy as jnp
from jax import lax
from jax.experimental import pallas as pl
from jax.experimental.pallas import tpu as pltpu
from jax.sharding import PartitionSpec as P

D = 192
HEADS = 3
HD = 64
FF = 768
PATCH_DIM = 768
CLASSES = 1000
CLASSES_PAD = 1024
LAYERS = 3
SEQ = 325
PATCHES = SEQ - 1
LEN_MID = 197
LEN_SHORT = 101
BASIS = 64
STEP = 10
WIDE = 1536
ROWS_OUT = WIDE + FF

HEAD_AT = PATCH_DIM * D
CLS_AT = HEAD_AT + D * CLASSES
PATCH_B_AT = CLS_AT + D
POS_AT = PATCH_B_AT + D
VEC_AT = POS_AT + SEQ * D
VEC_LAYER = 6 * D + FF
FINAL_AT = VEC_AT + LAYERS * VEC_LAYER
HEAD_B_AT = FINAL_AT + 2 * D
USED = HEAD_B_AT + CLASSES
HEAD_ROWS = D * CLASSES // 128
BLOCK_PAD = 2 * D + CLASSES_PAD
PATCH_ROWS = HEAD_AT // 128
TAIL_ROW = CLS_AT // 128
TAIL_ROWS = FINAL_AT // 128 + 1 - TAIL_ROW

PACKED = ROWS_OUT * 3 // 2
MIDDLE_ROWS = 4096
FIRST_ROWS = 5632

TQ = 336
TK = 384
CLS_ROW = PATCHES

NORM_EPS = 1e-06
CLIP_AT = 0.02
MUON_RATE = 0.3
ADAM_RATE = 0.05
BETA_ONE = 0.5
BETA_TWO = 0.95
DECAY_RATE = 0.01
ADAM_EPS = 1e-08
SHAPE_EPS = 1e-07
MASKED = -1e30
GELU_C = math.sqrt(2.0 / math.pi)
GELU_K = 0.044715

F32 = jnp.float32
BF = jnp.bfloat16
AXES = ("dp", "fsdp")
NN = (((1,), (0,)), ((), ()))
NT = (((1,), (1,)), ((), ()))
TN = (((0,), (0,)), ((), ()))
VMEM_LIMIT = 60 * 1024 * 1024


def dot(a, b, how):
    return lax.dot_general(a, b, how, preferred_element_type=F32)


def lanes(shape):
    return lax.broadcasted_iota(jnp.int32, shape, len(shape) - 1)


def head_mask(h):
    lane = lanes((1, D))
    return jnp.where((lane >= h * HD) & (lane < (h + 1) * HD), 1.0, 0.0)


def norm_stats(x):
    mean = jnp.mean(x, -1, keepdims=True)
    centered = x - mean
    var = jnp.mean(centered * centered, -1, keepdims=True)
    rstd = lax.rsqrt(var + NORM_EPS)
    return centered * rstd, rstd


def norm_back(dn, xhat, rstd, gain):
    scaled = dn * gain
    m1 = jnp.mean(scaled, -1, keepdims=True)
    m2 = jnp.mean(scaled * xhat, -1, keepdims=True)
    return rstd * (scaled - m1 - xhat * m2)


def colsum(x):
    return jnp.sum(x, 0, keepdims=True)


def key_mask(length, rows):
    key = lanes((rows, TK))
    return ((key < length - 1) | (key == CLS_ROW)).astype(F32)


def softmax_rows(scores):
    top = jnp.max(scores, -1, keepdims=True)
    e = jnp.exp(scores - top)
    return e / jnp.sum(e, -1, keepdims=True)


def merge(a, b, shift):
    if shift == 0:
        return a
    lane = lanes(a.shape)
    return jnp.where(
        lane < 128 - shift, pltpu.roll(a, 128 - shift, 1), pltpu.roll(b, 128 - shift, 1)
    )


def flat_vec(flat, at, n):
    blocks = []
    for j in range(-(-n // 128)):
        q, r = divmod(at + 128 * j, 128)
        blocks.append(merge(flat[q : q + 1, :], flat[q + 1 : q + 2, :], r))
    row = blocks[0] if len(blocks) == 1 else jnp.concatenate(blocks, 1)
    return row[:, :n]


def unpack_flat(blocks, flat, tmp, devices, share):
    rows = blocks.shape[1]
    lane = lanes((rows, 128))
    for d in range(devices):
        q, r = divmod(d * share, 128)
        block = blocks[d]
        if r == 0:
            flat[q : q + rows, :] = block
            continue
        slot = d % 4
        tmp[slot, 8 : 8 + rows, :] = pltpu.roll(block, r, 1)
        tmp[slot, 7:8, :] = flat[q : q + 1, :]
        flat[q : q + rows, :] = jnp.where(
            lane >= r, tmp[slot, 8 : 8 + rows, :], tmp[slot, 7 : 7 + rows, :]
        )


def unpack_pairs(flat, row, pairs, out, out_at):
    a = flat[pl.ds(row, pairs, stride=3), :]
    b = flat[pl.ds(row + 1, pairs, stride=3), :]
    c = flat[pl.ds(row + 2, pairs, stride=3), :]
    out[0, pl.ds(out_at, pairs, stride=2), :] = a
    out[1, pl.ds(out_at, pairs, stride=2), :] = b
    out[0, pl.ds(out_at + 1, pairs, stride=2), :] = merge(b, c, 64)
    out[1, pl.ds(out_at + 1, pairs, stride=2), :] = pltpu.roll(c, 64, 1)


def rows192(ref, at, n):
    return jnp.concatenate([ref[0, at : at + n, :], ref[1, at : at + n, 0:64]], 1)


def pack_pairs(src, src_at, flat, row, pairs):
    a = src[0, pl.ds(src_at, pairs, stride=2), :]
    b = src[1, pl.ds(src_at, pairs, stride=2), :]
    c = src[0, pl.ds(src_at + 1, pairs, stride=2), :]
    e = src[1, pl.ds(src_at + 1, pairs, stride=2), :]
    lane = lanes(a.shape)
    c = pltpu.roll(c, 64, 1)
    flat[pl.ds(row, pairs, stride=3), :] = a
    flat[pl.ds(row + 1, pairs, stride=3), :] = jnp.where(lane < 64, b, c)
    flat[pl.ds(row + 2, pairs, stride=3), :] = jnp.where(lane < 64, c, pltpu.roll(e, 64, 1))


def unpack_head(flat, out):
    lane = lanes((12, 128))
    for rho in range(16):
        for k in range(8):
            q, r = divmod(1000 * rho + 128 * k, 128)
            a = flat[pl.ds(HEAD_AT // 128 + q, 12, stride=125), :]
            b = flat[pl.ds(HEAD_AT // 128 + q + 1, 12, stride=125), :]
            block = merge(a, b, r)
            if k == 7:
                block = jnp.where(lane < CLASSES - 896, block, 0.0)
            out[k, pl.ds(rho, 12, stride=16), :] = block


def pack_head(src, out):
    lane = lanes((12, 128))
    for j in range(125):
        rho, c = divmod(128 * j, 1000)
        k, s = divmod(c, 128)
        a = src[k, pl.ds(rho, 12, stride=16), :]
        if s:
            b = a
            if k < 7:
                b = src[k + 1, pl.ds(rho, 12, stride=16), :]
            a = merge(a, b, s)
        left = 1000 - c
        if left < 128:
            nxt = src[0, pl.ds(rho + 1, 12, stride=16), :]
            a = jnp.where(lane < left, a, pltpu.roll(nxt, left, 1))
        out[pl.ds(j, 12, stride=125), :] = a


FACTOR_FLOW = 24
FACTOR_DLOGITS = 26
FACTOR_BLOCKS = 34
EXACT = 13
EXACT_ROWS = 16


def put_factor(ref, block, value, images):
    for k in range(-(-value.shape[1] // 128)):
        part = value[0:images, 128 * k : 128 * (k + 1)].astype(F32)
        at = EXACT_ROWS + (block + k) * images
        ref[at : at + images, 0 : part.shape[1]] = part


def put_entries(ref, shift_rows, at, row, n):
    lane = lanes((1, 128))
    done = 0
    while done < n:
        q, r = divmod(at + done, 128)
        q = q + shift_rows
        take = min(128 - r, n - done)
        block, off = divmod(done, 128)
        piece = row[:, 128 * block : 128 * (block + 1)]
        if off + take > 128:
            piece = merge(piece, row[:, 128 * (block + 1) : 128 * (block + 2)], off)
            off = 0
        shift = (r - off) % 128
        if shift:
            piece = pltpu.roll(piece, shift, 1)
        if take < 128:
            piece = jnp.where((lane >= r) & (lane < r + take), piece, ref[q : q + 1, :])
        ref[q : q + 1, :] = piece
        done += take


def image_rows(i):
    return pl.ds(pl.multiple_of(i * TQ, 16), TQ)


def length_of(group):
    return jnp.where(group == 0, LEN_SHORT, jnp.where(group == 1, LEN_MID, SEQ))


def layer_vectors(flat, l):
    at = VEC_AT + l * VEC_LAYER
    six = [flat_vec(flat, at + k * D, D) for k in range(6)]
    return six, flat_vec(flat, at + 6 * D, FF)


def store_layer_grads(ref, parts):
    tails = []
    for at, g in parts:
        ref[at : at + g.shape[0], :] = g[:, 0:128]
        tails.append((at, g))
    half = ROWS_OUT // 2
    for at, g in tails:
        n = g.shape[0]
        low = max(0, min(n, half - at))
        if low > 0:
            ref[ROWS_OUT + at : ROWS_OUT + at + low, 0:64] = g[:low, 128:192]
        if low < n:
            start = at + low - half
            ref[ROWS_OUT + start : ROWS_OUT + start + n - low, 64:128] = g[low:, 128:192]


def half_rows(rows):
    return -(-rows // 8) * 8, -(-rows // 16) * 8


def unpack_weights(blocks, layers, column_width, row_width, asm, wt, dn):
    devices = blocks.shape[0]
    per_layer = column_width + row_width
    a_rows, h = half_rows(layers * per_layer)
    for l in range(layers):
        for d in range(devices):
            block = blocks[d].astype(F32)
            for at, n, to in (
                (l * per_layer, column_width, d * column_width),
                (l * per_layer + column_width, row_width, WIDE + d * row_width),
            ):
                asm[to : to + n, 0:128] = block[at : at + n]
                low = max(0, min(n, h - at))
                if low:
                    asm[to : to + low, 128:192] = block[a_rows + at : a_rows + at + low, 0:64]
                if low < n:
                    start = a_rows + at + low - h
                    asm[to + low : to + n, 128:192] = block[start : start + n - low, 64:128]
        wt[l] = asm[0:WIDE, :].astype(BF)
        dn[l] = asm[WIDE:ROWS_OUT, :].astype(BF)


def layer_forward(images, l, info, flat, wt, dn, gains, xin, xout, saved):
    mid, qs, ks, vs, mixs, acts, gps = saved
    masks = [head_mask(h).astype(BF) for h in range(HEADS)]
    (gain1, shift1, out_bias, gain2, shift2, down_bias), up_bias = layer_vectors(flat, l)
    for k, value in enumerate((gain1, shift1, gain2, shift2)):
        gains[k : k + 1, :] = value

    def layer(i, carry):
        rows = image_rows(i)
        x = xin[rows, :]
        xhat, _ = norm_stats(x)
        n1 = (xhat * gain1 + shift1).astype(BF)
        q = (dot(n1, wt[0, 0:D, :], NT) * HD ** (-0.5)).astype(BF)
        k = dot(n1, wt[0, D : 2 * D, :], NT).astype(BF)
        v = dot(n1, wt[0, 2 * D : 3 * D, :], NT).astype(BF)
        qs[rows, :] = q
        ks[i, 0:TQ, :] = k
        vs[i, 0:TQ, :] = v
        ks[i, TQ:TK, :] = jnp.zeros((TK - TQ, D), BF)
        vs[i, TQ:TK, :] = jnp.zeros((TK - TQ, D), BF)
        valid = key_mask(length_of(info[i]), 1)
        kk = ks[i]
        vv = vs[i]
        mix = None
        for h in range(HEADS):
            s = dot(q * masks[h], kk, NT)
            s = jnp.where(valid > 0, s, MASKED)
            p = softmax_rows(s).astype(BF)
            part = dot(p, vv * masks[h], NN)
            mix = part if mix is None else mix + part
        mix = mix.astype(BF)
        mixs[rows, :] = mix
        middle = x + dot(mix, wt[0, 3 * D : 4 * D, :], NT) + out_bias
        mid[rows, :] = middle
        xhat2, _ = norm_stats(middle)
        n2 = (xhat2 * gain2 + shift2).astype(BF)
        up = dot(n2, wt[0, 4 * D : WIDE, :], NT) + up_bias
        t = jnp.tanh(GELU_C * (up + GELU_K * (up * up * up)))
        half = 0.5 * (1.0 + t)
        act = (up * half).astype(BF)
        gps[rows, :] = half + 0.5 * up * (1.0 - t * t) * (
            GELU_C * (1.0 + 3.0 * GELU_K * (up * up))
        )
        acts[rows, :] = act
        xout[rows, :] = middle + dot(act, dn[0], NN) + down_bias
        return carry

    lax.fori_loop(0, images, layer, 0)


def start_kernel(devices, share, images, column_width, row_width, n_pieces, tops, info, where, *refs):
    pieces, top_pieces = refs[:n_pieces], refs[n_pieces : 2 * n_pieces]
    patches = refs[2 * n_pieces]
    x0, mid, qs, ks, vs, mixs, acts, gps, x1, gains, wt, dn, flat = refs[
        2 * n_pieces + 1 : 2 * n_pieces + 14
    ]
    blocks, weights, asm, tmp, pw, pos = refs[2 * n_pieces + 14 :]
    inner = pieces[0].shape[0]
    rows = blocks.shape[1]
    for k in range(n_pieces):
        for j in range(inner):
            d = where[k * inner + j]
            blocks[d] = pieces[k][j, 0:rows, :].astype(F32)
            weights[d] = pieces[k][j, rows:, :]
    top_inner = top_pieces[0].shape[0]
    for k in range(n_pieces):
        for j in range(top_inner):
            d = where[n_pieces * inner + k * top_inner + j]
            blocks[d] = blocks[d] + top_pieces[k][j].astype(F32)
    unpack_flat(blocks, flat, tmp, devices, share)
    unpack_weights(weights, 1, column_width, row_width, asm, wt, dn)
    unpack_pairs(flat, 0, PATCH_DIM // 2, pw, 0)
    unpack_pairs(flat, POS_AT // 128, SEQ // 2, pos, 7)
    last = flat_vec(flat, POS_AT + (SEQ - 1) * D, D)
    pos[0, 7 + SEQ - 1 : 7 + SEQ, :] = last[:, 0:128]
    pos[1, 7 + SEQ - 1 : 7 + SEQ, 0:64] = last[:, 128:192]
    cls = flat_vec(flat, CLS_AT, D)
    patch_b = flat_vec(flat, PATCH_B_AT, D)
    patch_low = rows192(pw, 0, PATCH_DIM).astype(BF)

    def embed(i, carry):
        base = pl.multiple_of(i * TQ, 16)
        e = dot(patches[i], patch_low, NN) + patch_b + rows192(pos, 8, PATCHES)
        x0[pl.ds(base, 320), :] = e[0:320]
        tail = jnp.concatenate(
            [e[320:324], cls + rows192(pos, 7, 1), jnp.zeros((TQ - SEQ, D), F32)], 0
        )
        x0[pl.ds(base + 320, 16), :] = tail
        return carry

    lax.fori_loop(0, images, embed, 0)
    layer_forward(
        images, 0, info, flat, wt, dn, gains, x0, x1, (mid, qs, ks, vs, mixs, acts, gps)
    )


def forward_kernel(
    total_images,
    images,
    column_width,
    row_width,
    n_pieces,
    info,
    where,
    flat,
    x1,
    *refs,
):
    pieces = refs[:n_pieces]
    mid, qs, ks, vs, mixs, acts, gps, gains, gstream, kv, factors, small, wt_all, dn_all = refs[
        n_pieces : n_pieces + 14
    ]
    (
        weights,
        asm,
        hw,
        n1buf,
        kbuf,
        vbuf,
        dkbuf,
        dvbuf,
        clsbuf,
        qcls,
        mixcls,
        dmixcls,
        dqcls,
        midgrad,
        n1low,
    ) = refs[n_pieces + 14 :]
    inner = pieces[0].shape[0]
    for k in range(n_pieces):
        for j in range(inner):
            weights[where[k * inner + j]] = pieces[k][j]
    unpack_weights(weights, 2, column_width, row_width, asm, wt_all, dn_all)
    unpack_head(flat, hw)
    factors[...] = jnp.zeros_like(factors)
    layer_forward(
        images,
        1,
        info,
        flat,
        wt_all,
        dn_all,
        gains,
        x1,
        n1buf,
        (mid, qs, ks, vs, mixs, acts, gps),
    )
    wt, dn = wt_all.at[1], dn_all.at[1]

    l = 2
    x2 = n1buf
    (gain1, shift1, out_bias, gain2, shift2, down_bias), up_bias = layer_vectors(flat, l)
    wk = wt[D : 2 * D, :]
    wv = wt[2 * D : 3 * D, :]
    clsbuf[...] = jnp.zeros_like(clsbuf)
    mixcls[...] = jnp.zeros_like(mixcls)
    kbuf[:, TQ:TK, :] = jnp.zeros((images, TK - TQ, D), BF)
    vbuf[:, TQ:TK, :] = jnp.zeros((images, TK - TQ, D), BF)

    def keys(i, carry):
        rows = image_rows(i)
        xhat, _ = norm_stats(x2[rows, :])
        n1 = (xhat * gain1 + shift1).astype(BF)
        kbuf[i, 0:TQ, :] = dot(n1, wk, NT).astype(BF)
        vbuf[i, 0:TQ, :] = dot(n1, wv, NT).astype(BF)
        clsbuf[pl.ds(i, 1), :] = x2[pl.ds(i * TQ + CLS_ROW, 1), :]
        return carry

    lax.fori_loop(0, images, keys, 0)
    xc = clsbuf[...]
    xhat1c, rstd1c = norm_stats(xc)
    n1c = (xhat1c * gain1 + shift1).astype(BF)
    qc = (dot(n1c, wt[0:D, :], NT) * HD ** (-0.5)).astype(BF)
    qcls[...] = qc.astype(F32)
    mask3 = jnp.concatenate([head_mask(h) for h in range(HEADS)] + [jnp.zeros((13, D), F32)], 0)

    def cls_probs(i):
        q3 = (qcls[pl.ds(i, 1), :] * mask3).astype(BF)
        s = dot(q3, kbuf[i], NT)
        s = jnp.where(key_mask(length_of(info[i]), 1) > 0, s, MASKED)
        return q3, softmax_rows(s)

    def attend(i, carry):
        q3, p = cls_probs(i)
        m = dot(p.astype(BF), vbuf[i], NN)
        mixcls[pl.ds(i, 1), :] = colsum(m * mask3)
        return carry

    lax.fori_loop(0, images, attend, 0)
    mixc = mixcls[...].astype(BF)
    midc = xc + dot(mixc, wt[3 * D : 4 * D, :], NT) + out_bias
    xhat2c, rstd2c = norm_stats(midc)
    n2c = (xhat2c * gain2 + shift2).astype(BF)
    upc = dot(n2c, wt[4 * D : WIDE, :], NT) + up_bias
    tc = jnp.tanh(GELU_C * (upc + GELU_K * (upc * upc * upc)))
    halfc = 0.5 * (1.0 + tc)
    actc = (upc * halfc).astype(BF)
    gpc = halfc + 0.5 * upc * (1.0 - tc * tc) * (GELU_C * (1.0 + 3.0 * GELU_K * (upc * upc)))
    outc = midc + dot(actc, dn[...], NN) + down_bias

    fgain = flat_vec(flat, FINAL_AT, D)
    fshift = flat_vec(flat, FINAL_AT + D, D)
    head_b = jnp.concatenate(
        [flat_vec(flat, HEAD_B_AT, CLASSES), jnp.zeros((1, CLASSES_PAD - CLASSES), F32)], 1
    )
    row16 = lax.broadcasted_iota(jnp.int32, (16, 1), 0)
    real = (row16 < images).astype(F32)
    xhatf, rstdf = norm_stats(outc)
    flow = (xhatf * fgain + fshift).astype(BF)
    head_low = jnp.concatenate([hw[k] for k in range(8)], 1).astype(BF)
    cls_lane = lanes((16, CLASSES_PAD))
    logits = dot(flow, head_low, NN) + head_b
    logits = jnp.where(cls_lane < CLASSES, logits, MASKED)
    top = jnp.max(logits, -1, keepdims=True)
    e = jnp.exp(logits - top)
    total = jnp.sum(e, -1, keepdims=True)
    labels = jnp.zeros((16, 1), jnp.int32)
    for i in range(images):
        labels = jnp.where(row16 == i, info[images + i], labels)
    onehot = (cls_lane == labels).astype(F32)
    picked = jnp.sum(jnp.where(cls_lane == labels, logits, 0.0), -1, keepdims=True)
    loss = jnp.sum((top + jnp.log(total) - picked) * real, 0, keepdims=True)
    dlogits = (e / total - onehot) * (real / total_images)
    dlow = dlogits.astype(BF)
    dflow = dot(dlow, head_low, NT)
    put_factor(factors, FACTOR_FLOW, flow, images)
    put_factor(factors, FACTOR_DLOGITS, dlow, images)
    small[...] = jnp.zeros_like(small)
    exact = [jnp.broadcast_to(loss, (1, 128))]
    head_bias_grad = colsum(dlogits)
    exact += [head_bias_grad[:, 128 * k : 128 * (k + 1)] for k in range(8)]
    for value in (colsum(dflow * xhatf), colsum(dflow)):
        value = jnp.concatenate([value, jnp.zeros((1, 64), F32)], 1)
        exact += [value[:, 0:128], value[:, 128:256]]
    for k, value in enumerate(exact):
        factors[k : k + 1, :] = value
    gout = norm_back(dflow, xhatf, rstdf, fgain) * real

    ol = gout.astype(BF)
    dact = dot(ol, dn[...], NT)
    dup = dact * gpc * real
    ul = dup.astype(BF)
    dn2 = dot(ul, wt[4 * D : WIDE, :], NN)
    dmid = norm_back(dn2, xhat2c, rstd2c, gain2) + gout
    ml = dmid.astype(BF)
    small[4:5, 0:FF] = colsum(dup)
    small[10:11, 0:D] = colsum(dmid)
    small[11:12, 0:D] = colsum(dn2 * xhat2c)
    small[12:13, 0:D] = colsum(dn2)
    small[13:14, 0:D] = colsum(gout)
    dmixcls[...] = dot(ml, wt[3 * D : 4 * D, :], NN).astype(BF).astype(F32)
    dqcls[...] = jnp.zeros_like(dqcls)

    def attend_back(i, carry):
        q3, p = cls_probs(i)
        dm3 = (dmixcls[pl.ds(i, 1), :] * mask3).astype(BF)
        dp = dot(dm3, vbuf[i], NT)
        dv = dot(p.astype(BF), dm3, TN)
        ds = (p * (dp - jnp.sum(p * dp, -1, keepdims=True))).astype(BF)
        dq = dot(ds, kbuf[i], NN)
        dk = dot(ds, q3, TN)
        rows = image_rows(i)
        dkbuf[rows, :] = dk[0:TQ].astype(BF)
        dvbuf[rows, :] = dv[0:TQ].astype(BF)
        dqcls[pl.ds(i, 1), :] = colsum(dq * mask3) * HD ** (-0.5)
        return carry

    lax.fori_loop(0, images, attend_back, 0)
    dql = dqcls[...].astype(BF)
    dn1c = dot(dql, wt[0:D, :], NN)
    midgrad[...] = dmid
    dqcls[...] = dn1c
    for k, value in enumerate((ol, n2c, ml, mixc, dql, n1c)):
        put_factor(factors, 2 * k, value, images)
    for k, value in enumerate((actc, ul)):
        put_factor(factors, 12 + 6 * k, value, images)

    def stream_back(i, carry):
        dgain, dshift = carry
        rows = image_rows(i)
        base = pl.multiple_of(i * TQ, 16)
        xhat, rstd = norm_stats(x2[rows, :])
        n1low[rows, :] = (xhat * gain1 + shift1).astype(BF)
        dkl = dkbuf[rows, :]
        dvl = dvbuf[rows, :]
        dn1 = dot(dkl, wk, NN) + dot(dvl, wv, NN)
        at_cls = lax.broadcasted_iota(jnp.int32, (TQ, 1), 0) == CLS_ROW
        dn1 = dn1 + jnp.where(at_cls, dqcls[pl.ds(i, 1), :], 0.0)
        gin = norm_back(dn1, xhat, rstd, gain1)
        gstream[rows, :] = gin + jnp.where(at_cls, midgrad[pl.ds(i, 1), :], 0.0)
        return (dgain + colsum(dn1 * xhat), dshift + colsum(dn1))

    zero_row = jnp.zeros((1, D), F32)
    dgain, dshift = lax.fori_loop(0, images, stream_back, (zero_row, zero_row))
    dwk = dot(dkbuf[...], n1low[...], TN)
    dwv = dot(dvbuf[...], n1low[...], TN)
    small[8:9, 0:D] = dgain
    small[9:10, 0:D] = dshift
    kv[0:D, :] = dwk[:, 0:128]
    kv[D : 2 * D, :] = dwv[:, 0:128]
    kv[2 * D :, 0:64] = dwk[:, 128:192]
    kv[2 * D :, 64:128] = dwv[:, 128:192]


def layer_back(
    images,
    info,
    x,
    mid,
    qs,
    ks,
    vs,
    mixs,
    acts,
    gps,
    gains_shifts,
    gout,
    wt,
    dn,
    gin,
    gt,
    vec,
    upb,
    olbuf,
    ulbuf,
    n2buf,
    mlbuf,
    n1buf,
    dqbuf,
    dkbuf,
    dvbuf,
):
    gain1, shift1, gain2, shift2 = gains_shifts
    masks = [head_mask(h).astype(BF) for h in range(HEADS)]
    vec[...] = jnp.zeros_like(vec)
    upb[...] = jnp.zeros_like(upb)

    def body(i, carry):
        rows = image_rows(i)
        go = gout[rows, :]
        ol = go.astype(BF)
        olbuf[rows, :] = ol
        dact = dot(ol, dn[0], NT)
        dup = dact * gps[rows, :]
        ul = dup.astype(BF)
        ulbuf[rows, :] = ul
        dn2 = dot(ul, wt[0, 4 * D : WIDE, :], NN)
        xhat2, rstd2 = norm_stats(mid[rows, :])
        n2buf[rows, :] = (xhat2 * gain2 + shift2).astype(BF)
        dmid = norm_back(dn2, xhat2, rstd2, gain2) + go
        ml = dmid.astype(BF)
        mlbuf[rows, :] = ml
        upb[0:1, :] += colsum(dup)
        vec[2:3, :] += colsum(dmid)
        vec[3:4, :] += colsum(dn2 * xhat2)
        vec[4:5, :] += colsum(dn2)
        vec[5:6, :] += colsum(go)
        dmix = dot(ml, wt[0, 3 * D : 4 * D, :], NN).astype(BF)
        valid = key_mask(length_of(info[i]), 1)
        q = qs[rows, :]
        kk = ks[i]
        vv = vs[i]
        dq = dk = dv = None
        for h in range(HEADS):
            qh = q * masks[h]
            dmh = dmix * masks[h]
            s = dot(qh, kk, NT)
            s = jnp.where(valid > 0, s, MASKED)
            p = softmax_rows(s)
            dp = dot(dmh, vv, NT)
            t = p * dp
            ds = (t - p * jnp.sum(t, -1, keepdims=True)).astype(BF)
            dv_h = dot(p.astype(BF), dmh, TN)
            dq_h = dot(ds, kk * masks[h], NN)
            dk_h = dot(ds, qh, TN)
            dq, dk, dv = (dq_h, dk_h, dv_h) if dq is None else (dq + dq_h, dk + dk_h, dv + dv_h)
        dql = (dq * HD ** (-0.5)).astype(BF)
        dkl = dk[0:TQ].astype(BF)
        dvl = dv[0:TQ].astype(BF)
        dqbuf[rows, :] = dql
        dkbuf[rows, :] = dkl
        dvbuf[rows, :] = dvl
        dn1 = (
            dot(dql, wt[0, 0:D, :], NN)
            + dot(dkl, wt[0, D : 2 * D, :], NN)
            + dot(dvl, wt[0, 2 * D : 3 * D, :], NN)
        )
        xhat1, rstd1 = norm_stats(x[rows, :])
        n1buf[rows, :] = (xhat1 * gain1 + shift1).astype(BF)
        vec[0:1, :] += colsum(dn1 * xhat1)
        vec[1:2, :] += colsum(dn1)
        gin[rows, :] = norm_back(dn1, xhat1, rstd1, gain1) + dmid
        return carry

    lax.fori_loop(0, images, body, 0)
    store_layer_grads(
        gt,
        [
            (0, dot(dqbuf[...], n1buf[...], TN)),
            (D, dot(dkbuf[...], n1buf[...], TN)),
            (2 * D, dot(dvbuf[...], n1buf[...], TN)),
            (3 * D, dot(mlbuf[...], mixs[...], TN)),
            (4 * D, dot(ulbuf[...], n2buf[...], TN)),
            (WIDE, dot(acts[...], olbuf[...], TN)),
        ],
    )


def share_halves(gt, keep, send, mine):
    half = keep.shape[0]
    keep[...] = gt[pl.ds(pl.multiple_of(mine * half, 8), half), :]
    send[...] = gt[pl.ds(pl.multiple_of((1 - mine) * half, 8), half), :]


def middle_kernel(images, info, *refs):
    (x, mid, qs, ks, vs, mixs, acts, gps, gains, gout, wt, dn, kv) = refs[:13]
    (gin, keep, send, vec, upb, gt) = refs[13:19]
    gs = tuple(gains[k : k + 1, :] for k in range(4))
    layer_back(
        images, info, x, mid, qs, ks, vs, mixs, acts, gps, gs, gout, wt, dn, gin, gt, vec, upb,
        *refs[19:],
    )
    gt[PACKED : PACKED + 3 * D, :] = kv[...]
    gt[PACKED + 3 * D :, :] = jnp.zeros((MIDDLE_ROWS - PACKED - 3 * D, 128), F32)
    share_halves(gt, keep, send, info[2 * images])


def first_kernel(images, info, *refs):
    (x, mid, qs, ks, vs, mixs, acts, gps, gains, gout, wt, dn) = refs[:12]
    (patches, small, vec1, upb1, keep, send) = refs[12:18]
    (gt, gin, vec, upb, pgrad, posgrad) = refs[18:24]
    gs = tuple(gains[k : k + 1, :] for k in range(4))
    layer_back(
        images, info, x, mid, qs, ks, vs, mixs, acts, gps, gs, gout, wt, dn, gin, gt, vec, upb,
        *refs[24:],
    )

    def pos_rows(at):
        return jnp.concatenate([posgrad[0, at : at + 1, :], posgrad[1, at : at + 1, :]], 1)

    pgrad[...] = jnp.zeros_like(pgrad)
    posgrad[...] = jnp.zeros_like(posgrad)

    def embed_back(i, carry):
        base = pl.multiple_of(i * TQ, 16)
        g = gin[image_rows(i), :]
        posgrad[0, 8 : 8 + TQ, :] += g[:, 0:128]
        posgrad[1, 8 : 8 + TQ, 0:64] += g[:, 128:192]
        gl = g.astype(BF)[0:PATCHES]
        pg = dot(patches[i], gl, TN)
        pgrad[0] += pg[:, 0:128]
        pgrad[1, :, 0:64] += pg[:, 128:192]
        return carry

    lax.fori_loop(0, images, embed_back, 0)
    cls_row = pos_rows(8 + CLS_ROW)
    patch_b = jnp.concatenate([colsum(posgrad[k, 8 : 8 + PATCHES, :]) for k in range(2)], 1)
    posgrad[0, 7:8, :] = cls_row[:, 0:128]
    posgrad[1, 7:8, :] = cls_row[:, 128:256]
    base = PACKED + PATCH_ROWS
    gt[base:, :] = jnp.zeros((FIRST_ROWS - base, 128), F32)
    pack_pairs(pgrad, 0, gt, PACKED, PATCH_DIM // 2)
    pack_pairs(posgrad, 7, gt, base + POS_AT // 128 - TAIL_ROW, SEQ // 2)
    put = functools.partial(put_entries, gt, base - TAIL_ROW)
    put(CLS_AT, cls_row, D)
    put(PATCH_B_AT, patch_b, D)
    put(POS_AT + (SEQ - 1) * D, pos_rows(7 + SEQ - 1), D)
    for layer in range(LAYERS):
        at = VEC_AT + layer * VEC_LAYER
        for k in range(6):
            if layer == 2:
                row = small[8 + k : 9 + k, 0:256]
            elif layer == 1:
                row = vec1[k : k + 1, :]
            else:
                row = vec[k : k + 1, :]
            if layer < 2:
                row = jnp.concatenate([row, jnp.zeros((1, 64), F32)], 1)
            put(at + k * D, row, D)
        row = small[4:5, 0:FF] if layer == 2 else (upb1 if layer == 1 else upb)[0:1, :]
        put(at + 6 * D, row, FF)
    share_halves(gt, keep, send, info[2 * images])


def parts(a):
    high = a.astype(BF)
    return high, (a - high.astype(F32)).astype(BF)


def parts_dot(a, b, how):
    return dot(a[0], b[0], how) + (dot(a[0], b[1], how) + dot(a[1], b[0], how))


def split_dot(a, b, how):
    return parts_dot(parts(a), parts(b), how)


def own_rows(ref, l, at, width):
    if width % 8 == 0:
        return ref[l, pl.ds(pl.multiple_of(at, 8), width), :]
    rows = -(-(width + 7) // 8) * 8
    base = pl.multiple_of((at // 8) * 8, 8)
    x = ref[l, pl.ds(base, rows), :]
    return pltpu.roll(x, lax.rem(rows - (at - base), rows), 0)[:width]


def coefficient_kernel(devices, gathered, basis, exact, extra):
    total = gathered[0]
    for d in range(1, devices):
        total = total + gathered[d]
    exact[...] = total
    c = split_dot(jnp.broadcast_to(block_row(exact), (8, BLOCK_PAD)), basis[...], NT)[0:1, :]
    extra[...] = jnp.zeros_like(extra)
    for k in range(3):
        high = c.astype(BF).astype(F32)
        extra[k : k + 1, 0:BASIS] = high
        c = c - high


def late_kernel(devices, images, gathered, g2, headflat, hg):
    rows = gathered.shape[0] // devices

    def factor(block, count):
        columns = []
        for b in range(block, block + count):
            parts = [
                gathered[pl.ds(EXACT_ROWS + b * images + i, devices, stride=rows), :]
                for i in range(images)
            ]
            columns.append(jnp.concatenate(parts, 0))
        return jnp.concatenate(columns, 1).astype(BF)

    ol, n2, ml, mix, dq, n1 = [factor(2 * k, 2)[:, 0:D] for k in range(6)]
    act, ul = factor(12, 6), factor(18, 6)
    g2[0:D, :] = dot(dq, n1, TN)
    g2[3 * D : 4 * D, :] = dot(ml, mix, TN)
    g2[4 * D : WIDE, :] = dot(ul, n2, TN)
    g2[WIDE:, :] = dot(act, ol, TN)
    flow = factor(FACTOR_FLOW, 2)[:, 0:D]
    for k in range(8):
        hg[k] = dot(flow, factor(FACTOR_DLOGITS + k, 1), TN)
    pack_head(hg, headflat)


def block_row(exact):
    pieces = [
        jnp.concatenate([exact[at : at + 1, :], exact[at + 1 : at + 2, 0:64]], 1) for at in (9, 11)
    ]
    pieces += [exact[1 + k : 2 + k, :] for k in range(8)]
    return jnp.concatenate(pieces, 1)


def unpack_layer(src, out, l, which):
    half = ROWS_OUT // 2
    for c in range(18):
        out[l, c * 128 : (c + 1) * 128, 0:128] = src[c * 128 : (c + 1) * 128, :].astype(F32)
    for c in range(9):
        g = src[ROWS_OUT + c * 128 : ROWS_OUT + (c + 1) * 128, :].astype(F32)
        out[l, c * 128 : (c + 1) * 128, 128:192] = g[:, 0:64]
        out[l, half + c * 128 : half + (c + 1) * 128, 128:192] = g[:, 64:128]


def square_rows(ref, start, stop, acc):
    step = 64
    for at in range(start, stop, step):
        g = ref[at : min(at + step, stop), :].astype(F32)
        g = g * g
        for lane in range(0, g.shape[1], 128):
            part = g[:, lane : lane + 128]
            rows = part.shape[0]
            part = jnp.sum(part.reshape(rows // 8, 8, part.shape[1]), 0)
            if part.shape[1] < 128:
                part = jnp.concatenate([part, jnp.zeros((8, 128 - part.shape[1]), F32)], 1)
            acc = acc + part
    return acc


def total_of(x):
    return jnp.sum(jnp.sum(x, 0, keepdims=True), 1, keepdims=True)


def muon_kernel(column_width, row_width, n_pieces, place, *refs):
    pieces = refs[:n_pieces]
    (
        g2,
        headflat,
        exact,
        basis,
        mom,
        wide_w,
        wide_mom,
        down_w,
        down_mom,
    ) = refs[n_pieces : n_pieces + 9]
    (
        wide_new,
        wide_mom_new,
        wide_copy,
        down_new,
        down_mom_new,
        down_copy,
        share_grad,
        scal,
        flat,
        mid_rows,
        first_rows,
        coef,
        gfull,
        mats,
        powers,
    ) = refs[n_pieces + 9 :]
    wide_at, down_at, mine = place[2], place[3], place[4]
    start = pl.multiple_of(place[0], 192)
    count = place[1]
    inner = pieces[0].shape[0]
    total_pieces = n_pieces * inner
    mr, fr = MIDDLE_ROWS // total_pieces, FIRST_ROWS // total_pieces

    for k in range(n_pieces):
        for z in range(inner):
            at = mine ^ (k * inner + z)
            mid_rows[pl.ds(pl.multiple_of(at * mr, 16), mr), :] = pieces[k][z, 0:mr, :]
            first_rows[pl.ds(pl.multiple_of(at * fr, 16), fr), :] = pieces[k][z, mr : mr + fr, :]
            coef[pl.ds(pl.multiple_of(at * 16, 16), 16), :] = pieces[k][
                z, mr + fr : mr + fr + 16, :
            ].astype(F32)
    unpack_layer(first_rows, gfull, 0, 0)
    unpack_layer(mid_rows, gfull, 1, 1)
    gfull[2, 0:D, :] = g2[0:D, :]
    gfull[2, 3 * D : ROWS_OUT, :] = g2[3 * D :, :]
    gfull[2, D : 3 * D, 0:128] = mid_rows[PACKED : PACKED + 2 * D, :].astype(F32)
    tail = mid_rows[PACKED + 2 * D : PACKED + 3 * D, :].astype(F32)
    gfull[2, D : 2 * D, 128:192] = tail[:, 0:64]
    gfull[2, 2 * D : 3 * D, 128:192] = tail[:, 64:128]

    base = PACKED + PATCH_ROWS
    flat[0:PATCH_ROWS, :] = first_rows[PACKED:base, :].astype(F32)
    flat[PATCH_ROWS : PATCH_ROWS + HEAD_ROWS, :] = headflat[0:HEAD_ROWS, :]
    flat[TAIL_ROW : TAIL_ROW + TAIL_ROWS, :] = first_rows[base : base + TAIL_ROWS, :].astype(F32)
    flat[TAIL_ROW + TAIL_ROWS :, :] = jnp.zeros(
        (flat.shape[0] - TAIL_ROW - TAIL_ROWS, 128), F32
    )
    block = block_row(exact)

    sums = jnp.zeros((16, 128), F32)
    for at in range(total_pieces):
        sums = sums + coef[16 * at : 16 * (at + 1), :]
    c = sums[0:1, :] + sums[1:2, :] + sums[2:3, :]
    acc = jnp.zeros((8, 128), F32)
    acc = square_rows(first_rows, 0, PACKED, acc)
    acc = square_rows(mid_rows, 0, PACKED + 3 * D, acc)
    acc = square_rows(g2, 0, D, acc)
    acc = square_rows(g2, 3 * D, ROWS_OUT, acc)
    acc = square_rows(flat, 0, flat.shape[0], acc)
    squares = total_of(acc) + total_of(jnp.where(lanes((1, BLOCK_PAD)) < 2 * D + CLASSES, block * block, 0.0))
    coef_square = jnp.sum(c * c, 1, keepdims=True)
    norm = jnp.sqrt(squares - coef_square)
    factor = CLIP_AT / jnp.maximum(norm, CLIP_AT)
    scal[...] = jnp.zeros_like(scal)
    for k, value in enumerate((norm, factor, jnp.sqrt(coef_square), exact[0:1, 0:1], c)):
        scal[k : k + 1, :] = jnp.broadcast_to(value, (1, 128))

    block = block - split_dot(
        jnp.broadcast_to(c[:, 0:BASIS], (8, BASIS)), basis[...], NN
    )[0:1, :]
    put_entries(flat, 0, FINAL_AT, block, 2 * D + CLASSES)
    rows = share_grad.shape[0]
    at, shift = place[5], place[6]
    base_row = pl.multiple_of((at // 8) * 8, 8)
    off = at - base_row
    window = flat[pl.ds(base_row, rows + 16), :]
    here = pltpu.roll(window, lax.rem(rows + 16 - off, rows + 16), 0)
    there = pltpu.roll(window, lax.rem(rows + 15 - off, rows + 16), 0)[0:rows]
    here = here[0:rows]
    back = lax.rem(128 - shift, 128)
    g = jnp.where(
        lanes((rows, 128)) < 128 - shift, pltpu.roll(here, back, 1), pltpu.roll(there, back, 1)
    )
    share_grad[...] = g * factor

    row = lax.broadcasted_iota(jnp.int32, (FF, 1), 0)
    sizes = []
    eye = (
        lax.broadcasted_iota(jnp.int32, (D, D), 0) == lax.broadcasted_iota(jnp.int32, (D, D), 1)
    ).astype(F32)
    for k in range(2 * LAYERS):
        l, which = divmod(k, 2)
        if which == 0:
            m = mom[pl.ds(start // column_width, FF // column_width), l, 0:column_width, :]
            m = BETA_ONE * m.reshape(FF, D) + factor * gfull[l, pl.ds(start, FF), :]
            m = jnp.where(row < count, m, 0.0)
        else:
            m = BETA_ONE * mom[:, l, column_width:, :].reshape(FF, D) + factor * gfull[l, WIDE:ROWS_OUT, :]
        size = 1.0 / (jnp.sqrt(total_of(m * m)) + SHAPE_EPS)
        sizes.append(size)
        x = m * size
        mats[k] = split_dot(x, x, TN)
        powers[k] = eye

    def polynomial(k):
        a = parts(mats[k])
        b = parts_dot(a, a, NN)
        return a, 3.4445 * eye - 4.775 * mats[k] + 2.0315 * b

    def step(it, carry):
        polys = [polynomial(k) for k in range(2 * LAYERS)]
        ps = [parts(p) for _, p in polys]
        ts = [parts(parts_dot(p, a, NN)) for (a, _), p in zip(polys, ps)]
        for k in range(2 * LAYERS):
            mats[k] = parts_dot(ts[k], ps[k], NN)
            powers[k] = parts_dot(ps[k], parts(powers[k]), NN)
        return carry

    lax.fori_loop(0, 4, step, 0)
    side = jnp.where(count == 4 * D, 768.0, jnp.where(count == 3 * D, 576.0, 192.0))
    rate = jnp.sqrt(jnp.full((1, 1), 1.0, F32) * side) * (MUON_RATE * 0.2)
    for k in range(2 * LAYERS):
        l, which = divmod(k, 2)
        _, p = polynomial(k)
        q = parts_dot(parts(p), parts(powers[k]), NN)
        if which == 0:
            g = own_rows(gfull, l, wide_at, column_width)
            own = BETA_ONE * wide_mom[l] + factor * g
            update = split_dot(own * sizes[k], q, NN)
            new = wide_w[l] - rate * update
            wide_mom_new[l] = own
            wide_new[l] = new
            wide_copy[l] = new.astype(BF)
        else:
            g = own_rows(gfull, l, down_at, row_width)
            own = BETA_ONE * down_mom[l] + factor * g
            update = split_dot(own * sizes[k], q, NN)
            new = down_w[l] - (MUON_RATE * 0.2 * FF**0.5) * update
            down_mom_new[l] = own
            down_new[l] = new
            down_copy[l] = new.astype(BF)


def cost(micros):
    return pl.CostEstimate(
        flops=int(micros * 1.15e9), bytes_accessed=int(micros * 1e6), transcendentals=0
    )


def pad_rows(x, rows):
    return jnp.pad(x, (0, rows * 128 - x.shape[0])).reshape(rows, 128)


def pack_shard(wide_t, down):
    rows = jnp.concatenate([wide_t, down], 1)
    rows = rows.reshape(-1, D).astype(BF)
    a_rows, h = half_rows(rows.shape[0])
    head = jnp.pad(rows[:, :128], ((0, a_rows - rows.shape[0]), (0, 0)))
    tail = jnp.pad(rows[:, 128:], ((0, 2 * h - rows.shape[0]), (0, 0)))
    tail = jnp.concatenate([tail[:h], tail[h:]], 1)
    fill = -(a_rows + h) % 16
    return jnp.concatenate([head, tail] + ([jnp.zeros((fill, 128), BF)] if fill else []), 0)


def stage_masks(stages):
    masks = [0]
    for low, width in reversed(stages):
        masks = [a ^ (m << low) for m in range(1 << width) for a in masks]
    return masks


def gather_stages(arrays, stages, devices, apart=2):
    for depth in reversed(range(len(stages))):
        low, width = stages[depth]
        got = [swap(x, m << low, devices) for m in range(1, 1 << width) for x in arrays]
        arrays = arrays + got
        if depth >= apart:
            arrays = [jnp.concatenate(arrays, 0)]
    return arrays


def swap(x, mask, devices):
    return lax.ppermute(x, AXES, [(i, i ^ mask) for i in range(devices)])


def local(
    patches,
    groups,
    labels,
    wide_w,
    down_w,
    plain,
    wide_mom,
    down_mom,
    plain_first,
    plain_second,
    basis_plain,
):
    devices = lax.axis_size(AXES)
    bits = devices.bit_length() - 1
    me = lax.axis_index(AXES).astype(jnp.int32)
    images = patches.shape[0]
    share = plain.shape[0]
    column_width = wide_w.shape[2]
    row_width = down_w.shape[1]
    vmem = pl.BlockSpec(memory_space=pltpu.VMEM)
    smem = pl.BlockSpec(memory_space=pltpu.SMEM)
    params = pltpu.CompilerParams(vmem_limit_bytes=VMEM_LIMIT)
    S = jax.ShapeDtypeStruct

    number_of = [(0, 1), (1, 2), (3, 2)]
    stages = number_of + ([(5, 2), (7, 1)] if bits == 8 else [(b, 1) for b in range(5, bits)])

    wide_t = jnp.transpose(wide_w, (0, 2, 1))
    plain_rows = -(-(share + 127) // 2048) * 16
    rows = plain_rows
    plain_block = pad_rows(plain, plain_rows)
    high = lax.reduce_precision(plain_block, 8, 7)
    low_half = (plain_block - high).astype(BF)
    shard_one = jnp.concatenate([high.astype(BF), pack_shard(wide_t[:1], down_w[:1])], 0)
    shard_two = pack_shard(wide_t[1:], down_w[1:])

    top = 3 * devices // 4
    if bits == 5 and top * share <= CLS_AT:
        low_all = None
        for m in range(1, 4):
            got = lax.ppermute(
                low_half, AXES, [(i, i ^ (m << 3)) for i in range(top, devices)]
            )
            low_all = got if low_all is None else low_all + got
        low_all = jnp.where(me >= top, low_half, low_all)[None]
        top_arrays = gather_stages([low_all], number_of[:2], devices)
        top_where = [top | ((me ^ m) & 7) for m in stage_masks(number_of[:2])]
    else:
        top_arrays = gather_stages([low_half[None]], stages, devices)
        top_where = [me ^ m for m in stage_masks(stages)]
    one = gather_stages([shard_one[None]], stages[1:], devices, 1)
    two = gather_stages([shard_two[None]], stages[2:], devices, 0)
    one, two = lax.optimization_barrier((one, two))
    pieces_one = gather_stages(one, stages[:1], devices)
    two = gather_stages(two, stages[1:2], devices)
    where_one = [me ^ m for m in stage_masks(stages)]

    lead = jnp.clip(FINAL_AT - me * share + BLOCK_PAD, 0, share + BLOCK_PAD)
    basis_block = lax.dynamic_slice(
        jnp.pad(basis_plain, ((0, 0), (BLOCK_PAD, BLOCK_PAD))), (0, lead), (BASIS, BLOCK_PAD)
    )

    info = jnp.concatenate([groups, labels, (me & 1)[None]]).astype(jnp.int32)
    flat_rows = -(-((devices - 1) * share // 128 + rows + 8) // 8) * 8
    n = images * TQ
    saved = [
        S((n, D), F32),
        S((n, D), BF),
        S((images, TK, D), BF),
        S((images, TK, D), BF),
        S((n, D), BF),
        S((n, FF), BF),
        S((n, FF), F32),
    ]
    factor_rows = EXACT_ROWS + -(-FACTOR_BLOCKS * images // 8) * 8
    where = jnp.stack(where_one + top_where).astype(jnp.int32)
    weight_rows = shard_one.shape[0] - rows
    x0, *saved0, x1, gains0, wt0, dn0, flat = pl.pallas_call(
        functools.partial(
            start_kernel, devices, share, images, column_width, row_width, len(pieces_one), None
        ),
        out_shape=[S((n, D), F32)]
        + saved
        + [
            S((n, D), F32),
            S((8, D), F32),
            S((1, WIDE, D), BF),
            S((1, FF, D), BF),
            S((flat_rows, 128), F32),
        ],
        in_specs=[smem] * 2 + [vmem] * (2 * len(pieces_one) + 1),
        out_specs=[vmem] * 13,
        scratch_shapes=[
            pltpu.VMEM((devices, rows, 128), F32),
            pltpu.VMEM((devices, weight_rows, 128), BF),
            pltpu.VMEM((ROWS_OUT, D), F32),
            pltpu.VMEM((4, rows + 8, 128), F32),
            pltpu.VMEM((2, PATCH_DIM, 128), F32),
            pltpu.VMEM((2, TQ, 128), F32),
        ],
        compiler_params=params,
        cost_estimate=cost(20),
        name="start",
    )(info, where, *pieces_one, *top_arrays, patches)

    two, x1 = lax.optimization_barrier((two, x1))
    pieces_two = gather_stages(two, stages[:1], devices)
    *saved1, gains1, gstream, kv, factors, small, wt12, dn12 = pl.pallas_call(
        functools.partial(
            forward_kernel,
            float(images * devices),
            images,
            column_width,
            row_width,
            len(pieces_two),
        ),
        out_shape=saved
        + [
            S((8, D), F32),
            S((n, D), F32),
            S((3 * D, 128), F32),
            S((factor_rows, 128), F32),
            S((16, CLASSES_PAD), F32),
            S((2, WIDE, D), BF),
            S((2, FF, D), BF),
        ],
        in_specs=[smem] * 2 + [vmem] * (len(pieces_two) + 2),
        out_specs=[vmem] * 14,
        scratch_shapes=[
            pltpu.VMEM((devices, shard_two.shape[0], 128), BF),
            pltpu.VMEM((ROWS_OUT, D), F32),
            pltpu.VMEM((8, D, 128), F32),
            pltpu.VMEM((n, D), F32),
            pltpu.VMEM((images, TK, D), BF),
            pltpu.VMEM((images, TK, D), BF),
            pltpu.VMEM((n, D), BF),
            pltpu.VMEM((n, D), BF),
        ]
        + [pltpu.VMEM((16, D), F32)] * 6
        + [pltpu.VMEM((n, D), BF)],
        compiler_params=params,
        cost_estimate=cost(30),
        name="forward",
    )(info, where, flat, x1, *pieces_two)

    mom_shard = jnp.concatenate([jnp.transpose(wide_mom, (0, 2, 1)), down_mom], 1)
    mom_shard, _ = lax.optimization_barrier((mom_shard, pieces_one[:4]))
    mom_all = lax.all_gather(mom_shard, AXES, axis=0)
    factors, mom_all = lax.optimization_barrier((factors, mom_all))
    gstream, factors = lax.optimization_barrier((gstream, factors))
    factors_all = lax.all_gather(factors, AXES, axis=0)
    back_scratch = [
        pltpu.VMEM((n, D), BF),
        pltpu.VMEM((n, FF), BF),
        pltpu.VMEM((n, D), BF),
        pltpu.VMEM((n, D), BF),
        pltpu.VMEM((n, D), BF),
        pltpu.VMEM((n, D), BF),
        pltpu.VMEM((n, D), BF),
        pltpu.VMEM((n, D), BF),
    ]
    gstream1, middle_keep, middle_send, vec1, upb1 = pl.pallas_call(
        functools.partial(middle_kernel, images),
        out_shape=[
            S((n, D), F32),
            S((MIDDLE_ROWS // 2, 128), F32),
            S((MIDDLE_ROWS // 2, 128), F32),
            S((8, D), F32),
            S((8, FF), F32),
        ],
        in_specs=[smem] + [vmem] * 13,
        out_specs=[vmem] * 5,
        scratch_shapes=[pltpu.VMEM((MIDDLE_ROWS, 128), F32)] + back_scratch,
        compiler_params=params,
        cost_estimate=cost(23),
        name="middle",
    )(info, x1, *saved1, gains1, gstream, wt12, dn12, kv)

    first_keep, first_send = pl.pallas_call(
        functools.partial(first_kernel, images),
        out_shape=[S((FIRST_ROWS // 2, 128), F32)] * 2,
        in_specs=[smem] + [vmem] * 16,
        out_specs=[vmem] * 2,
        scratch_shapes=[
            pltpu.VMEM((FIRST_ROWS, 128), F32),
            pltpu.VMEM((n, D), F32),
            pltpu.VMEM((8, D), F32),
            pltpu.VMEM((8, FF), F32),
            pltpu.VMEM((2, PATCH_DIM, 128), F32),
            pltpu.VMEM((2, TQ + 16, 128), F32),
        ]
        + back_scratch,
        compiler_params=params,
        cost_estimate=cost(25),
        name="first",
    )(info, x0, *saved0, gains0, gstream1, wt0, dn0, patches, small, vec1, upb1)

    exact, extra = pl.pallas_call(
        functools.partial(coefficient_kernel, devices),
        grid=(1,),
        out_shape=[S((EXACT_ROWS, 128), F32), S((16, 128), F32)],
        in_specs=[pl.BlockSpec((devices, EXACT_ROWS, 128), lambda i: (0, 0, 0)), vmem],
        out_specs=[vmem] * 2,
        compiler_params=params,
        cost_estimate=cost(2),
        name="coefficients",
    )(factors_all, basis_block)

    g2, headflat = pl.pallas_call(
        functools.partial(late_kernel, devices, images),
        out_shape=[S((ROWS_OUT, D), F32), S((HEAD_ROWS + 4, 128), F32)],
        in_specs=[vmem],
        out_specs=[vmem] * 2,
        scratch_shapes=[pltpu.VMEM((8, D, 128), F32)],
        compiler_params=params,
        cost_estimate=cost(4),
        name="late",
    )(factors_all.reshape(devices * factor_rows, 128))

    split_bits = 5
    for bit in range(split_bits, bits):
        extra = extra + swap(extra, 1 << bit, devices)
    if bits > split_bits:
        c = extra[0] + extra[1] + extra[2]
        split = []
        for k in range(3):
            split.append(lax.reduce_precision(c, 8, 7))
            c = c - split[-1]
        extra = jnp.concatenate([jnp.stack(split), extra[3:]], 0)
    kept = None
    for low, width in number_of:
        ways = 1 << width
        mine = (me >> low) & (ways - 1)
        if kept is None:
            kept = [
                middle_keep + swap(middle_send, 1, devices),
                first_keep + swap(first_send, 1, devices),
            ]
            kept = jnp.concatenate([x.reshape(4, x.shape[0] // 4, 128) for x in kept], 1)
            continue
        total = lax.dynamic_index_in_dim(kept, mine, 0, keepdims=False)
        for m in range(1, ways):
            send = lax.dynamic_index_in_dim(kept, mine ^ m, 0, keepdims=False).astype(BF)
            total = total + swap(send, m << low, devices).astype(F32)
        if low == 1:
            mr = MIDDLE_ROWS // 8
            kept = jnp.concatenate(
                [
                    total[:mr].reshape(4, mr // 4, 128),
                    total[mr:].reshape(4, (total.shape[0] - mr) // 4, 128),
                ],
                1,
            )
        else:
            kept = total
    for bit in range(split_bits, bits):
        small_part = kept.astype(BF)
        kept = small_part.astype(F32) + swap(small_part, 1 << bit, devices).astype(F32)
    piece = jnp.concatenate([kept, extra], 0).astype(BF)[None]
    pieces = gather_stages([piece], number_of, devices)

    first_column = me * column_width
    in_q = first_column < 3 * D
    in_o = first_column < 4 * D
    start = jnp.where(in_q, 0, jnp.where(in_o, 3 * D, 4 * D))
    count = jnp.where(in_q, 3 * D, jnp.where(in_o, D, FF))
    number = ((me & 1) << 4) | (((me >> 1) & 3) << 2) | ((me >> 3) & 3)
    at = me * share
    spots = jnp.stack(
        [start, count, first_column, WIDE + me * row_width, number, at // 128, at % 128]
    )
    wide_shape = (LAYERS, column_width, D)
    down_shape = (LAYERS, row_width, D)
    flat_rows = -(-((devices - 1) * share // 128 + rows + 24) // 8) * 8
    (
        wide_new,
        wide_mom_new,
        wide_copy,
        down_new,
        down_mom_new,
        down_copy,
        share_grad,
        scal,
    ) = pl.pallas_call(
        functools.partial(muon_kernel, column_width, row_width, len(pieces)),
        out_shape=[
            S(wide_shape, F32),
            S(wide_shape, F32),
            S(wide_shape, BF),
            S(down_shape, F32),
            S(down_shape, F32),
            S(down_shape, BF),
            S((rows, 128), F32),
            S((8, 128), F32),
        ],
        in_specs=[smem] + [vmem] * (len(pieces) + 9),
        out_specs=[vmem] * 8,
        scratch_shapes=[
            pltpu.VMEM((flat_rows, 128), F32),
            pltpu.VMEM((MIDDLE_ROWS, 128), BF),
            pltpu.VMEM((FIRST_ROWS, 128), BF),
            pltpu.VMEM((16 * 32, 128), F32),
            pltpu.VMEM((LAYERS, ROWS_OUT + 16, D), F32),
            pltpu.VMEM((2 * LAYERS, D, D), F32),
            pltpu.VMEM((2 * LAYERS, D, D), F32),
        ],
        compiler_params=params,
        cost_estimate=cost(20),
        name="muon",
    )(
        spots.astype(jnp.int32),
        *pieces,
        g2,
        headflat,
        exact,
        basis_block,
        mom_all,
        wide_t,
        jnp.transpose(wide_mom, (0, 2, 1)),
        down_w,
        down_mom,
    )
    grad_norm, _, removed_norm, loss_sum = [scal[k, 0] for k in range(4)]
    clipped = share_grad.reshape(-1)[:share]
    first_new = BETA_ONE * plain_first + (1.0 - BETA_ONE) * clipped
    second_new = BETA_TWO * plain_second + (1.0 - BETA_TWO) * clipped * clipped
    first_hat = first_new / (1.0 - BETA_ONE**STEP)
    second_hat = second_new / (1.0 - BETA_TWO**STEP)
    plain_new = plain - ADAM_RATE * (
        first_hat / (jnp.sqrt(second_hat) + ADAM_EPS) + DECAY_RATE * plain
    )
    plain_copy = plain_new.astype(BF)
    return (
        loss_sum,
        removed_norm,
        grad_norm,
        *[jnp.transpose(x, (0, 2, 1)) for x in (wide_new, wide_mom_new, wide_copy)],
        down_new,
        down_mom_new,
        down_copy,
        plain_new,
        first_new,
        second_new,
        plain_copy,
    )


def solution(mesh):
    placed = (
        P(AXES, None, None),
        P(AXES),
        P(AXES),
        P(None, None, AXES),
        P(None, AXES, None),
        P(AXES),
        P(None, None, AXES),
        P(None, AXES, None),
        P(AXES),
        P(AXES),
        P(None, AXES),
    )
    return jax.shard_map(
        local,
        mesh=mesh,
        in_specs=placed,
        out_specs=(
            P(),
            P(),
            P(),
            P(None, None, AXES),
            P(None, None, AXES),
            P(None, None, AXES),
            P(None, AXES, None),
            P(None, AXES, None),
            P(None, AXES, None),
            P(AXES),
            P(AXES),
            P(AXES),
            P(AXES),
        ),
        check_vma=False,
    )
```

```python
import functools
import math

import jax
import jax.numpy as jnp
from jax import lax
from jax.experimental import pallas as pl
from jax.experimental.pallas import tpu as pltpu
from jax.sharding import PartitionSpec as P

D = 192
HEADS = 3
HD = 64
FF = 768
PATCH_DIM = 768
CLASSES = 1000
CLASSES_PAD = 1024
LAYERS = 3
SEQ = 325
PATCHES = SEQ - 1
LEN_MID = 197
LEN_SHORT = 101
BASIS = 64
STEP = 10
WIDE = 1536
ROWS_OUT = WIDE + FF

HEAD_AT = PATCH_DIM * D
CLS_AT = HEAD_AT + D * CLASSES
PATCH_B_AT = CLS_AT + D
POS_AT = PATCH_B_AT + D
VEC_AT = POS_AT + SEQ * D
VEC_LAYER = 6 * D + FF
FINAL_AT = VEC_AT + LAYERS * VEC_LAYER
HEAD_B_AT = FINAL_AT + 2 * D
USED = HEAD_B_AT + CLASSES
HEAD_ROWS = D * CLASSES // 128
BLOCK_PAD = 2 * D + CLASSES_PAD
PATCH_ROWS = HEAD_AT // 128
TAIL_ROW = CLS_AT // 128
TAIL_ROWS = FINAL_AT // 128 + 1 - TAIL_ROW

PACKED = ROWS_OUT * 3 // 2
MIDDLE_ROWS = 4096
FIRST_ROWS = 5632

TQ = 336
TK = 384
CLS_ROW = 0
PATCH_AT = 8
SIZES = ((112, 128), (208, 256), (336, 384))

NORM_EPS = 1e-06
CLIP_AT = 0.02
MUON_RATE = 0.3
ADAM_RATE = 0.05
BETA_ONE = 0.5
BETA_TWO = 0.95
DECAY_RATE = 0.01
ADAM_EPS = 1e-08
SHAPE_EPS = 1e-07
MASKED = -1e30
GELU_C = math.sqrt(2.0 / math.pi)
GELU_K = 0.044715

F32 = jnp.float32
BF = jnp.bfloat16
AXES = ("dp", "fsdp")
NN = (((1,), (0,)), ((), ()))
NT = (((1,), (1,)), ((), ()))
TN = (((0,), (0,)), ((), ()))
VMEM_LIMIT = 60 * 1024 * 1024


def dot(a, b, how):
    return lax.dot_general(a, b, how, preferred_element_type=F32)


def lanes(shape):
    return lax.broadcasted_iota(jnp.int32, shape, len(shape) - 1)


def head_mask(h):
    lane = lanes((1, D))
    return jnp.where((lane >= h * HD) & (lane < (h + 1) * HD), 1.0, 0.0)


def norm_stats(x):
    mean = jnp.mean(x, -1, keepdims=True)
    centered = x - mean
    var = jnp.mean(centered * centered, -1, keepdims=True)
    rstd = lax.rsqrt(var + NORM_EPS)
    return centered * rstd, rstd


def norm_back(dn, xhat, rstd, gain):
    scaled = dn * gain
    m1 = jnp.mean(scaled, -1, keepdims=True)
    m2 = jnp.mean(scaled * xhat, -1, keepdims=True)
    return rstd * (scaled - m1 - xhat * m2)


def colsum(x):
    return jnp.sum(x, 0, keepdims=True)


def key_mask(length, keys):
    key = lanes((1, keys))
    return ((key >= PATCH_AT) & (key < PATCH_AT + length - 1)) | (key == CLS_ROW)


def by_size(group, body):
    pl.when(group == 0)(lambda: body(*SIZES[0]))
    pl.when(group == 1)(lambda: body(*SIZES[1]))
    pl.when((group != 0) & (group != 1))(lambda: body(*SIZES[2]))


def softmax_rows(scores):
    top = jnp.max(scores, -1, keepdims=True)
    e = jnp.exp(scores - top)
    return e / jnp.sum(e, -1, keepdims=True)


def merge(a, b, shift):
    if shift == 0:
        return a
    lane = lanes(a.shape)
    return jnp.where(
        lane < 128 - shift, pltpu.roll(a, 128 - shift, 1), pltpu.roll(b, 128 - shift, 1)
    )


def flat_vec(flat, at, n):
    blocks = []
    for j in range(-(-n // 128)):
        q, r = divmod(at + 128 * j, 128)
        blocks.append(merge(flat[q : q + 1, :], flat[q + 1 : q + 2, :], r))
    row = blocks[0] if len(blocks) == 1 else jnp.concatenate(blocks, 1)
    return row[:, :n]


def unpack_flat(blocks, flat, tmp, devices, share):
    rows = blocks.shape[1]
    lane = lanes((rows, 128))
    for d in range(devices):
        q, r = divmod(d * share, 128)
        block = blocks[d]
        if r == 0:
            flat[q : q + rows, :] = block
            continue
        slot = d % 4
        tmp[slot, 8 : 8 + rows, :] = pltpu.roll(block, r, 1)
        tmp[slot, 7:8, :] = flat[q : q + 1, :]
        flat[q : q + rows, :] = jnp.where(
            lane >= r, tmp[slot, 8 : 8 + rows, :], tmp[slot, 7 : 7 + rows, :]
        )


def unpack_pairs(flat, row, pairs, out, out_at):
    a = flat[pl.ds(row, pairs, stride=3), :]
    b = flat[pl.ds(row + 1, pairs, stride=3), :]
    c = flat[pl.ds(row + 2, pairs, stride=3), :]
    out[0, pl.ds(out_at, pairs, stride=2), :] = a
    out[1, pl.ds(out_at, pairs, stride=2), :] = b
    out[0, pl.ds(out_at + 1, pairs, stride=2), :] = merge(b, c, 64)
    out[1, pl.ds(out_at + 1, pairs, stride=2), :] = pltpu.roll(c, 64, 1)


def rows192(ref, at, n):
    return jnp.concatenate([ref[0, at : at + n, :], ref[1, at : at + n, 0:64]], 1)


def pack_pairs(src, src_at, flat, row, pairs):
    a = src[0, pl.ds(src_at, pairs, stride=2), :]
    b = src[1, pl.ds(src_at, pairs, stride=2), :]
    c = src[0, pl.ds(src_at + 1, pairs, stride=2), :]
    e = src[1, pl.ds(src_at + 1, pairs, stride=2), :]
    lane = lanes(a.shape)
    c = pltpu.roll(c, 64, 1)
    flat[pl.ds(row, pairs, stride=3), :] = a
    flat[pl.ds(row + 1, pairs, stride=3), :] = jnp.where(lane < 64, b, c)
    flat[pl.ds(row + 2, pairs, stride=3), :] = jnp.where(lane < 64, c, pltpu.roll(e, 64, 1))


def unpack_head(flat, out):
    lane = lanes((12, 128))
    for rho in range(16):
        for k in range(8):
            q, r = divmod(1000 * rho + 128 * k, 128)
            a = flat[pl.ds(HEAD_AT // 128 + q, 12, stride=125), :]
            b = flat[pl.ds(HEAD_AT // 128 + q + 1, 12, stride=125), :]
            block = merge(a, b, r)
            if k == 7:
                block = jnp.where(lane < CLASSES - 896, block, 0.0)
            out[k, pl.ds(rho, 12, stride=16), :] = block


def pack_head(src, out):
    lane = lanes((12, 128))
    for j in range(125):
        rho, c = divmod(128 * j, 1000)
        k, s = divmod(c, 128)
        a = src[k, pl.ds(rho, 12, stride=16), :]
        if s:
            b = a
            if k < 7:
                b = src[k + 1, pl.ds(rho, 12, stride=16), :]
            a = merge(a, b, s)
        left = 1000 - c
        if left < 128:
            nxt = src[0, pl.ds(rho + 1, 12, stride=16), :]
            a = jnp.where(lane < left, a, pltpu.roll(nxt, left, 1))
        out[pl.ds(j, 12, stride=125), :] = a


FACTOR_FLOW = 24
FACTOR_DLOGITS = 26
FACTOR_BLOCKS = 34
EXACT = 13
EXACT_ROWS = 16


def put_factor(ref, block, value, images):
    for k in range(-(-value.shape[1] // 128)):
        part = value[0:images, 128 * k : 128 * (k + 1)].astype(F32)
        at = EXACT_ROWS + (block + k) * images
        ref[at : at + images, 0 : part.shape[1]] = part


def put_entries(ref, shift_rows, at, row, n):
    lane = lanes((1, 128))
    done = 0
    while done < n:
        q, r = divmod(at + done, 128)
        q = q + shift_rows
        take = min(128 - r, n - done)
        block, off = divmod(done, 128)
        piece = row[:, 128 * block : 128 * (block + 1)]
        if off + take > 128:
            piece = merge(piece, row[:, 128 * (block + 1) : 128 * (block + 2)], off)
            off = 0
        shift = (r - off) % 128
        if shift:
            piece = pltpu.roll(piece, shift, 1)
        if take < 128:
            piece = jnp.where((lane >= r) & (lane < r + take), piece, ref[q : q + 1, :])
        ref[q : q + 1, :] = piece
        done += take


def image_rows(i):
    return pl.ds(pl.multiple_of(i * TQ, 16), TQ)


def length_of(group):
    return jnp.where(group == 0, LEN_SHORT, jnp.where(group == 1, LEN_MID, SEQ))


def layer_vectors(flat, l):
    at = VEC_AT + l * VEC_LAYER
    six = [flat_vec(flat, at + k * D, D) for k in range(6)]
    return six, flat_vec(flat, at + 6 * D, FF)


def store_layer_grads(ref, parts):
    tails = []
    for at, g in parts:
        ref[at : at + g.shape[0], :] = g[:, 0:128]
        tails.append((at, g))
    half = ROWS_OUT // 2
    for at, g in tails:
        n = g.shape[0]
        low = max(0, min(n, half - at))
        if low > 0:
            ref[ROWS_OUT + at : ROWS_OUT + at + low, 0:64] = g[:low, 128:192]
        if low < n:
            start = at + low - half
            ref[ROWS_OUT + start : ROWS_OUT + start + n - low, 64:128] = g[low:, 128:192]


def half_rows(rows):
    return -(-rows // 8) * 8, -(-rows // 16) * 8


def unpack_weights(blocks, layers, column_width, row_width, asm, wt, dn):
    devices = blocks.shape[0]
    per_layer = column_width + row_width
    a_rows, h = half_rows(layers * per_layer)
    for l in range(layers):
        for d in range(devices):
            block = blocks[d].astype(F32)
            for at, n, to in (
                (l * per_layer, column_width, d * column_width),
                (l * per_layer + column_width, row_width, WIDE + d * row_width),
            ):
                asm[to : to + n, 0:128] = block[at : at + n]
                low = max(0, min(n, h - at))
                if low:
                    asm[to : to + low, 128:192] = block[a_rows + at : a_rows + at + low, 0:64]
                if low < n:
                    start = a_rows + at + low - h
                    asm[to + low : to + n, 128:192] = block[start : start + n - low, 64:128]
        wt[l] = asm[0:WIDE, :].astype(BF)
        dn[l] = asm[WIDE:ROWS_OUT, :].astype(BF)


def layer_forward(l, group, flat, wt, dn, gains, xin, xout, saved):
    mid, qs, ks, vs, probs, mixs, acts, gps = saved
    masks = [head_mask(h).astype(BF) for h in range(HEADS)]
    (gain1, shift1, out_bias, gain2, shift2, down_bias), up_bias = layer_vectors(flat, l)
    for k, value in enumerate((gain1, shift1, gain2, shift2)):
        gains[k : k + 1, :] = value

    def body(tq, tk):
        x = xin[0:tq, :]
        xhat, _ = norm_stats(x)
        n1 = (xhat * gain1 + shift1).astype(BF)
        q = (dot(n1, wt[0, 0:D, :], NT) * HD ** (-0.5)).astype(BF)
        k = dot(n1, wt[0, D : 2 * D, :], NT).astype(BF)
        v = dot(n1, wt[0, 2 * D : 3 * D, :], NT).astype(BF)
        qs[0:tq, :] = q
        ks[0, 0:tq, :] = k
        vs[0, 0:tq, :] = v
        ks[0, tq:tk, :] = jnp.zeros((tk - tq, D), BF)
        vs[0, tq:tk, :] = jnp.zeros((tk - tq, D), BF)
        valid = key_mask(length_of(group), tk)
        kk = ks[0, 0:tk, :]
        vv = vs[0, 0:tk, :]
        mix = None
        for h in range(HEADS):
            s = dot(q * masks[h], kk, NT)
            s = jnp.where(valid, s, MASKED)
            p = softmax_rows(s)
            probs[0, h, 0:tq, 0:tk] = p
            part = dot(p.astype(BF), vv * masks[h], NN)
            mix = part if mix is None else mix + part
        mix = mix.astype(BF)
        mixs[0:tq, :] = mix
        middle = x + dot(mix, wt[0, 3 * D : 4 * D, :], NT) + out_bias
        mid[0:tq, :] = middle
        xhat2, _ = norm_stats(middle)
        n2 = (xhat2 * gain2 + shift2).astype(BF)
        up = dot(n2, wt[0, 4 * D : WIDE, :], NT) + up_bias
        t = jnp.tanh(GELU_C * (up + GELU_K * (up * up * up)))
        half = 0.5 * (1.0 + t)
        act = (up * half).astype(BF)
        gps[0:tq, :] = half + 0.5 * up * (1.0 - t * t) * (
            GELU_C * (1.0 + 3.0 * GELU_K * (up * up))
        )
        acts[0:tq, :] = act
        xout[0:tq, :] = middle + dot(act, dn[0], NN) + down_bias
        if tq < TQ:
            xout[tq:TQ, :] = jnp.zeros((TQ - tq, D), F32)

    by_size(group, body)


def start_kernel(devices, share, column_width, row_width, places, n_pieces, groups, me, *refs):
    pieces, patches = refs[:n_pieces], refs[n_pieces]
    x0, mid, qs, ks, vs, probs, mixs, acts, gps, x1, gains, wt, dn, flat = refs[
        n_pieces + 1 : n_pieces + 15
    ]
    blocks, weights, asm, tmp, pw, pos, emb = refs[n_pieces + 15 :]
    image = pl.program_id(0)
    pl.when(image == 0)(
        lambda: unpack_start(
            devices, share, column_width, row_width, places, me[0], pieces, wt, dn, flat, blocks, weights,
            asm, tmp, pw, pos, emb,
        )
    )
    cls = flat_vec(flat, CLS_AT, D)
    patch_b = flat_vec(flat, PATCH_B_AT, D)
    e = dot(patches[0], emb[...], NN) + patch_b + rows192(pos, 8, PATCHES)
    x0[0:PATCH_AT, :] = jnp.concatenate(
        [cls + rows192(pos, 7, 1), jnp.zeros((PATCH_AT - 1, D), F32)], 0
    )
    x0[PATCH_AT : PATCH_AT + PATCHES, :] = e
    x0[PATCH_AT + PATCHES :, :] = jnp.zeros((TQ - PATCH_AT - PATCHES, D), F32)
    layer_forward(
        0, groups[image], flat, wt, dn, gains, x0, x1, (mid, qs, ks, vs, probs, mixs, acts, gps)
    )


def unpack_start(
    devices, share, column_width, row_width, places, me, pieces, wt, dn, flat, blocks, weights, asm, tmp,
    pw, pos, emb,
):
    inner_masks, outer_masks, top = places
    rows, weight_rows = blocks.shape[1], weights.shape[1]
    body = rows + weight_rows
    step = body if top is not None else body + rows
    for k, outer in enumerate(outer_masks):
        piece = pieces[k // pieces[0].shape[0]].at[k % pieces[0].shape[0]]
        for j, inner in enumerate(inner_masks):
            d = me ^ (outer | inner)
            at = j * step
            value = piece[at : at + rows, :].astype(F32)
            if top is None:
                value = value + piece[at + body : at + body + rows, :].astype(F32)
            blocks[d] = value
            weights[d] = piece[at + rows : at + body, :]
        if top is not None:
            d = top | ((me ^ outer) & 7)
            at = len(inner_masks) * step
            blocks[d] = blocks[d] + piece[at : at + rows, :].astype(F32)
    unpack_flat(blocks, flat, tmp, devices, share)
    unpack_weights(weights, 1, column_width, row_width, asm, wt, dn)
    unpack_pairs(flat, 0, PATCH_DIM // 2, pw, 0)
    unpack_pairs(flat, POS_AT // 128, SEQ // 2, pos, 7)
    last = flat_vec(flat, POS_AT + (SEQ - 1) * D, D)
    pos[0, 7 + SEQ - 1 : 7 + SEQ, :] = last[:, 0:128]
    pos[1, 7 + SEQ - 1 : 7 + SEQ, 0:64] = last[:, 128:192]
    emb[...] = rows192(pw, 0, PATCH_DIM).astype(BF)


def forward_kernel(
    total_images, images, column_width, row_width, masks, n_pieces, groups, labels, me, flat, x1, *refs
):
    pieces = refs[:n_pieces]
    mid, qs, ks, vs, probs, mixs, acts, gps, gains, *rest = refs[n_pieces:]
    gstream, kv, factors, small, wt_all, dn_all, weights, asm, hw, x2 = rest[:10]
    image = pl.program_id(0)

    @pl.when(image == 0)
    def _():
        inner = pieces[0].shape[0]
        for k in range(n_pieces):
            for j in range(inner):
                weights[me[0] ^ masks[k * inner + j]] = pieces[k][j]
        unpack_weights(weights, 2, column_width, row_width, asm, wt_all, dn_all)
        unpack_head(flat, hw)
        factors[...] = jnp.zeros_like(factors)

    layer_forward(
        1,
        groups[image],
        flat,
        wt_all,
        dn_all,
        gains,
        x1,
        x2.at[image_rows(image)],
        (mid, qs, ks, vs, probs, mixs, acts, gps),
    )
    pl.when(image == images - 1)(
        lambda: last_layer(
            total_images, images, groups, labels, flat, gstream, kv, factors, small, wt_all.at[1],
            dn_all.at[1], hw, x2, *rest[10:],
        )
    )


def last_layer(
    total_images, images, groups, labels, flat, gstream, kv, factors, small, wt, dn, hw, x2, kbuf, vbuf,
    dkbuf, dvbuf, clsbuf, qcls, mixcls, dmixcls, dqcls, midgrad, n1low,
):
    l = 2
    (gain1, shift1, out_bias, gain2, shift2, down_bias), up_bias = layer_vectors(flat, l)
    wk = wt[D : 2 * D, :]
    wv = wt[2 * D : 3 * D, :]
    clsbuf[...] = jnp.zeros_like(clsbuf)
    mixcls[...] = jnp.zeros_like(mixcls)
    kbuf[:, TQ:TK, :] = jnp.zeros((images, TK - TQ, D), BF)
    vbuf[:, TQ:TK, :] = jnp.zeros((images, TK - TQ, D), BF)

    def keys(i, carry):
        rows = image_rows(i)
        xhat, _ = norm_stats(x2[rows, :])
        n1 = (xhat * gain1 + shift1).astype(BF)
        kbuf[i, 0:TQ, :] = dot(n1, wk, NT).astype(BF)
        vbuf[i, 0:TQ, :] = dot(n1, wv, NT).astype(BF)
        clsbuf[pl.ds(i, 1), :] = x2[pl.ds(i * TQ + CLS_ROW, 1), :]
        return carry

    lax.fori_loop(0, images, keys, 0)
    xc = clsbuf[...]
    xhat1c, rstd1c = norm_stats(xc)
    n1c = (xhat1c * gain1 + shift1).astype(BF)
    qc = (dot(n1c, wt[0:D, :], NT) * HD ** (-0.5)).astype(BF)
    qcls[...] = qc.astype(F32)
    mask3 = jnp.concatenate([head_mask(h) for h in range(HEADS)] + [jnp.zeros((13, D), F32)], 0)

    def cls_probs(i):
        q3 = (qcls[pl.ds(i, 1), :] * mask3).astype(BF)
        s = dot(q3, kbuf[i], NT)
        s = jnp.where(key_mask(length_of(groups[i]), TK), s, MASKED)
        return q3, softmax_rows(s)

    def attend(i, carry):
        q3, p = cls_probs(i)
        m = dot(p.astype(BF), vbuf[i], NN)
        mixcls[pl.ds(i, 1), :] = colsum(m * mask3)
        return carry

    lax.fori_loop(0, images, attend, 0)
    mixc = mixcls[...].astype(BF)
    midc = xc + dot(mixc, wt[3 * D : 4 * D, :], NT) + out_bias
    xhat2c, rstd2c = norm_stats(midc)
    n2c = (xhat2c * gain2 + shift2).astype(BF)
    upc = dot(n2c, wt[4 * D : WIDE, :], NT) + up_bias
    tc = jnp.tanh(GELU_C * (upc + GELU_K * (upc * upc * upc)))
    halfc = 0.5 * (1.0 + tc)
    actc = (upc * halfc).astype(BF)
    gpc = halfc + 0.5 * upc * (1.0 - tc * tc) * (GELU_C * (1.0 + 3.0 * GELU_K * (upc * upc)))
    outc = midc + dot(actc, dn[...], NN) + down_bias

    fgain = flat_vec(flat, FINAL_AT, D)
    fshift = flat_vec(flat, FINAL_AT + D, D)
    head_b = jnp.concatenate(
        [flat_vec(flat, HEAD_B_AT, CLASSES), jnp.zeros((1, CLASSES_PAD - CLASSES), F32)], 1
    )
    row16 = lax.broadcasted_iota(jnp.int32, (16, 1), 0)
    real = (row16 < images).astype(F32)
    xhatf, rstdf = norm_stats(outc)
    flow = (xhatf * fgain + fshift).astype(BF)
    head_low = jnp.concatenate([hw[k] for k in range(8)], 1).astype(BF)
    cls_lane = lanes((16, CLASSES_PAD))
    logits = dot(flow, head_low, NN) + head_b
    logits = jnp.where(cls_lane < CLASSES, logits, MASKED)
    top = jnp.max(logits, -1, keepdims=True)
    e = jnp.exp(logits - top)
    total = jnp.sum(e, -1, keepdims=True)
    label = jnp.zeros((16, 1), jnp.int32)
    for i in range(images):
        label = jnp.where(row16 == i, labels[i], label)
    onehot = (cls_lane == label).astype(F32)
    picked = jnp.sum(jnp.where(cls_lane == label, logits, 0.0), -1, keepdims=True)
    loss = jnp.sum((top + jnp.log(total) - picked) * real, 0, keepdims=True)
    dlogits = (e / total - onehot) * (real / total_images)
    dlow = dlogits.astype(BF)
    dflow = dot(dlow, head_low, NT)
    put_factor(factors, FACTOR_FLOW, flow, images)
    put_factor(factors, FACTOR_DLOGITS, dlow, images)
    small[...] = jnp.zeros_like(small)
    exact = [jnp.broadcast_to(loss, (1, 128))]
    head_bias_grad = colsum(dlogits)
    exact += [head_bias_grad[:, 128 * k : 128 * (k + 1)] for k in range(8)]
    for value in (colsum(dflow * xhatf), colsum(dflow)):
        value = jnp.concatenate([value, jnp.zeros((1, 64), F32)], 1)
        exact += [value[:, 0:128], value[:, 128:256]]
    for k, value in enumerate(exact):
        factors[k : k + 1, :] = value
    gout = norm_back(dflow, xhatf, rstdf, fgain) * real

    ol = gout.astype(BF)
    dact = dot(ol, dn[...], NT)
    dup = dact * gpc * real
    ul = dup.astype(BF)
    dn2 = dot(ul, wt[4 * D : WIDE, :], NN)
    dmid = norm_back(dn2, xhat2c, rstd2c, gain2) + gout
    ml = dmid.astype(BF)
    small[4:5, 0:FF] = colsum(dup)
    small[10:11, 0:D] = colsum(dmid)
    small[11:12, 0:D] = colsum(dn2 * xhat2c)
    small[12:13, 0:D] = colsum(dn2)
    small[13:14, 0:D] = colsum(gout)
    dmixcls[...] = dot(ml, wt[3 * D : 4 * D, :], NN).astype(BF).astype(F32)
    dqcls[...] = jnp.zeros_like(dqcls)

    def attend_back(i, carry):
        q3, p = cls_probs(i)
        dm3 = (dmixcls[pl.ds(i, 1), :] * mask3).astype(BF)
        dp = dot(dm3, vbuf[i], NT)
        dv = dot(p.astype(BF), dm3, TN)
        ds = (p * (dp - jnp.sum(p * dp, -1, keepdims=True))).astype(BF)
        dq = dot(ds, kbuf[i], NN)
        dk = dot(ds, q3, TN)
        rows = image_rows(i)
        dkbuf[rows, :] = dk[0:TQ].astype(BF)
        dvbuf[rows, :] = dv[0:TQ].astype(BF)
        dqcls[pl.ds(i, 1), :] = colsum(dq * mask3) * HD ** (-0.5)
        return carry

    lax.fori_loop(0, images, attend_back, 0)
    dql = dqcls[...].astype(BF)
    dn1c = dot(dql, wt[0:D, :], NN)
    midgrad[...] = dmid
    dqcls[...] = dn1c
    for k, value in enumerate((ol, n2c, ml, mixc, dql, n1c)):
        put_factor(factors, 2 * k, value, images)
    for k, value in enumerate((actc, ul)):
        put_factor(factors, 12 + 6 * k, value, images)

    def stream_back(i, carry):
        dgain, dshift = carry
        rows = image_rows(i)
        base = pl.multiple_of(i * TQ, 16)
        xhat, rstd = norm_stats(x2[rows, :])
        n1low[rows, :] = (xhat * gain1 + shift1).astype(BF)
        dkl = dkbuf[rows, :]
        dvl = dvbuf[rows, :]
        dn1 = dot(dkl, wk, NN) + dot(dvl, wv, NN)
        at_cls = lax.broadcasted_iota(jnp.int32, (TQ, 1), 0) == CLS_ROW
        dn1 = dn1 + jnp.where(at_cls, dqcls[pl.ds(i, 1), :], 0.0)
        gin = norm_back(dn1, xhat, rstd, gain1)
        gstream[rows, :] = gin + jnp.where(at_cls, midgrad[pl.ds(i, 1), :], 0.0)
        return (dgain + colsum(dn1 * xhat), dshift + colsum(dn1))

    zero_row = jnp.zeros((1, D), F32)
    dgain, dshift = lax.fori_loop(0, images, stream_back, (zero_row, zero_row))
    dwk = dot(dkbuf[...], n1low[...], TN)
    dwv = dot(dvbuf[...], n1low[...], TN)
    small[8:9, 0:D] = dgain
    small[9:10, 0:D] = dshift
    kv[0:D, :] = dwk[:, 0:128]
    kv[D : 2 * D, :] = dwv[:, 0:128]
    kv[2 * D :, 0:64] = dwk[:, 128:192]
    kv[2 * D :, 64:128] = dwv[:, 128:192]


def layer_back(
    images,
    group,
    x,
    mid,
    qs,
    ks,
    vs,
    probs,
    mixs,
    acts,
    gps,
    gains,
    gout,
    wt,
    dn,
    gin,
    gt,
    vec,
    upb,
    olbuf,
    ulbuf,
    n2buf,
    mlbuf,
    n1buf,
    dqbuf,
    dkbuf,
    dvbuf,
    mixbuf,
    actbuf,
):
    gain1, shift1, gain2, shift2 = [gains[k : k + 1, :] for k in range(4)]
    masks = [head_mask(h).astype(BF) for h in range(HEADS)]
    image = pl.program_id(0)
    start = pl.multiple_of(image * TQ, 16)

    @pl.when(image == 0)
    def _():
        vec[...] = jnp.zeros_like(vec)
        upb[...] = jnp.zeros_like(upb)

    def body(tq, tk):
        rows = pl.ds(start, tq)
        go = gout[0:tq, :]
        ol = go.astype(BF)
        olbuf[rows, :] = ol
        actbuf[rows, :] = acts[0:tq, :]
        mixbuf[rows, :] = mixs[0:tq, :]
        dact = dot(ol, dn[0], NT)
        dup = dact * gps[0:tq, :]
        ul = dup.astype(BF)
        ulbuf[rows, :] = ul
        dn2 = dot(ul, wt[0, 4 * D : WIDE, :], NN)
        xhat2, rstd2 = norm_stats(mid[0:tq, :])
        n2buf[rows, :] = (xhat2 * gain2 + shift2).astype(BF)
        dmid = norm_back(dn2, xhat2, rstd2, gain2) + go
        ml = dmid.astype(BF)
        mlbuf[rows, :] = ml
        upb[0:1, :] += colsum(dup)
        vec[2:3, :] += colsum(dmid)
        vec[3:4, :] += colsum(dn2 * xhat2)
        vec[4:5, :] += colsum(dn2)
        vec[5:6, :] += colsum(go)
        dmix = dot(ml, wt[0, 3 * D : 4 * D, :], NN).astype(BF)
        q = qs[0:tq, :]
        kk = ks[0, 0:tk, :]
        vv = vs[0, 0:tk, :]
        dq = dk = dv = None
        for h in range(HEADS):
            qh = q * masks[h]
            dmh = dmix * masks[h]
            p = probs[0, h, 0:tq, 0:tk]
            dp = dot(dmh, vv, NT)
            t = p * dp
            ds = (t - p * jnp.sum(t, -1, keepdims=True)).astype(BF)
            dv_h = dot(p.astype(BF), dmh, TN)
            dq_h = dot(ds, kk * masks[h], NN)
            dk_h = dot(ds, qh, TN)
            dq, dk, dv = (dq_h, dk_h, dv_h) if dq is None else (dq + dq_h, dk + dk_h, dv + dv_h)
        dql = (dq * HD ** (-0.5)).astype(BF)
        dkl = dk[0:tq].astype(BF)
        dvl = dv[0:tq].astype(BF)
        dqbuf[rows, :] = dql
        dkbuf[rows, :] = dkl
        dvbuf[rows, :] = dvl
        dn1 = (
            dot(dql, wt[0, 0:D, :], NN)
            + dot(dkl, wt[0, D : 2 * D, :], NN)
            + dot(dvl, wt[0, 2 * D : 3 * D, :], NN)
        )
        xhat1, rstd1 = norm_stats(x[0:tq, :])
        n1buf[rows, :] = (xhat1 * gain1 + shift1).astype(BF)
        vec[0:1, :] += colsum(dn1 * xhat1)
        vec[1:2, :] += colsum(dn1)
        gin[0:tq, :] = norm_back(dn1, xhat1, rstd1, gain1) + dmid
        if tq < TQ:
            rest = pl.ds(start + tq, TQ - tq)
            gin[tq:TQ, :] = jnp.zeros((TQ - tq, D), F32)
            for ref in (olbuf, ulbuf, n2buf, mlbuf, n1buf, dqbuf, dkbuf, dvbuf, mixbuf, actbuf):
                ref[rest, :] = jnp.zeros((TQ - tq, ref.shape[1]), BF)

    by_size(group, body)

    @pl.when(image == images - 1)
    def _():
        store_layer_grads(
            gt,
            [
                (0, dot(dqbuf[...], n1buf[...], TN)),
                (D, dot(dkbuf[...], n1buf[...], TN)),
                (2 * D, dot(dvbuf[...], n1buf[...], TN)),
                (3 * D, dot(mlbuf[...], mixbuf[...], TN)),
                (4 * D, dot(ulbuf[...], n2buf[...], TN)),
                (WIDE, dot(actbuf[...], olbuf[...], TN)),
            ],
        )


def share_halves(gt, keep, send, mine):
    half = keep.shape[0]
    keep[...] = gt[pl.ds(pl.multiple_of(mine * half, 8), half), :]
    send[...] = gt[pl.ds(pl.multiple_of((1 - mine) * half, 8), half), :]


def middle_kernel(images, groups, me, *refs):
    inputs, kv = refs[:13], refs[13]
    gin, keep, send, vec, upb, gt, *buffers = refs[14:]
    image = pl.program_id(0)
    layer_back(images, groups[image], *inputs, gin, gt, vec, upb, *buffers)

    @pl.when(image == images - 1)
    def _():
        gt[PACKED : PACKED + 3 * D, :] = kv[...]
        gt[PACKED + 3 * D :, :] = jnp.zeros((MIDDLE_ROWS - PACKED - 3 * D, 128), F32)
        share_halves(gt, keep, send, me[0] & 1)


def first_kernel(images, groups, me, *refs):
    inputs, (patches, small, vec1, upb1) = refs[:13], refs[13:17]
    keep, send, gt, gin, vec, upb, pgrad, posgrad, *buffers = refs[17:]
    image = pl.program_id(0)
    layer_back(images, groups[image], *inputs, gin, gt, vec, upb, *buffers)

    @pl.when(image == 0)
    def _():
        pgrad[...] = jnp.zeros_like(pgrad)
        posgrad[...] = jnp.zeros_like(posgrad)

    g = gin[...]
    used = PATCH_AT + PATCHES
    posgrad[0, 0:used, :] += g[0:used, 0:128]
    posgrad[1, 0:used, 0:64] += g[0:used, 128:192]
    pg = dot(patches[0], g[PATCH_AT:used].astype(BF), TN)
    pgrad[0] += pg[:, 0:128]
    pgrad[1, :, 0:64] += pg[:, 128:192]
    pl.when(image == images - 1)(
        lambda: pack_first(keep, send, gt, vec, upb, pgrad, posgrad, small, vec1, upb1, me[0] & 1)
    )


def pack_first(keep, send, gt, vec, upb, pgrad, posgrad, small, vec1, upb1, core):
    def pos_rows(at):
        return jnp.concatenate([posgrad[0, at : at + 1, :], posgrad[1, at : at + 1, :]], 1)

    cls_row = pos_rows(CLS_ROW)
    patch_b = jnp.concatenate(
        [colsum(posgrad[k, PATCH_AT : PATCH_AT + PATCHES, :]) for k in range(2)], 1
    )
    posgrad[0, 7:8, :] = cls_row[:, 0:128]
    posgrad[1, 7:8, :] = cls_row[:, 128:256]
    base = PACKED + PATCH_ROWS
    gt[base:, :] = jnp.zeros((FIRST_ROWS - base, 128), F32)
    pack_pairs(pgrad, 0, gt, PACKED, PATCH_DIM // 2)
    pack_pairs(posgrad, 7, gt, base + POS_AT // 128 - TAIL_ROW, SEQ // 2)
    put = functools.partial(put_entries, gt, base - TAIL_ROW)
    put(CLS_AT, cls_row, D)
    put(PATCH_B_AT, patch_b, D)
    put(POS_AT + (SEQ - 1) * D, pos_rows(7 + SEQ - 1), D)
    for layer in range(LAYERS):
        at = VEC_AT + layer * VEC_LAYER
        for k in range(6):
            if layer == 2:
                row = small[8 + k : 9 + k, 0:256]
            else:
                row = (vec if layer == 0 else vec1)[k : k + 1, :]
                row = jnp.concatenate([row, jnp.zeros((1, 64), F32)], 1)
            put(at + k * D, row, D)
        row = small[4:5, 0:FF] if layer == 2 else (upb1 if layer == 1 else upb)[0:1, :]
        put(at + 6 * D, row, FF)
    share_halves(gt, keep, send, core)


def parts(a):
    high = a.astype(BF)
    return high, (a - high.astype(F32)).astype(BF)


def parts_dot(a, b, how):
    return dot(a[0], b[0], how) + (dot(a[0], b[1], how) + dot(a[1], b[0], how))


def split_dot(a, b, how):
    return parts_dot(parts(a), parts(b), how)


def own_rows(ref, l, at, width):
    if width % 8 == 0:
        return ref[l, pl.ds(pl.multiple_of(at, 8), width), :]
    rows = -(-(width + 7) // 8) * 8
    base = pl.multiple_of((at // 8) * 8, 8)
    x = ref[l, pl.ds(base, rows), :]
    return pltpu.roll(x, lax.rem(rows - (at - base), rows), 0)[:width]


def coefficient_kernel(devices, gathered, basis, exact, extra):
    total = gathered[0]
    for d in range(1, devices):
        total = total + gathered[d]
    exact[...] = total
    c = split_dot(jnp.broadcast_to(block_row(exact), (8, BLOCK_PAD)), basis[...], NT)[0:1, :]
    extra[...] = jnp.zeros_like(extra)
    for k in range(3):
        high = c.astype(BF).astype(F32)
        extra[k : k + 1, 0:BASIS] = high
        c = c - high


def late_kernel(devices, images, gathered, g2, headflat, hg):
    rows = gathered.shape[0] // devices

    def factor(block, count):
        columns = []
        for b in range(block, block + count):
            parts = [
                gathered[pl.ds(EXACT_ROWS + b * images + i, devices, stride=rows), :]
                for i in range(images)
            ]
            columns.append(jnp.concatenate(parts, 0))
        return jnp.concatenate(columns, 1).astype(BF)

    ol, n2, ml, mix, dq, n1 = [factor(2 * k, 2)[:, 0:D] for k in range(6)]
    act, ul = factor(12, 6), factor(18, 6)
    g2[0:D, :] = dot(dq, n1, TN)
    g2[3 * D : 4 * D, :] = dot(ml, mix, TN)
    g2[4 * D : WIDE, :] = dot(ul, n2, TN)
    g2[WIDE:, :] = dot(act, ol, TN)
    flow = factor(FACTOR_FLOW, 2)[:, 0:D]
    for k in range(8):
        hg[k] = dot(flow, factor(FACTOR_DLOGITS + k, 1), TN)
    pack_head(hg, headflat)


def block_row(exact):
    pieces = [
        jnp.concatenate([exact[at : at + 1, :], exact[at + 1 : at + 2, 0:64]], 1) for at in (9, 11)
    ]
    pieces += [exact[1 + k : 2 + k, :] for k in range(8)]
    return jnp.concatenate(pieces, 1)


def unpack_layer(src, out, l, which):
    half = ROWS_OUT // 2
    for c in range(18):
        out[l, c * 128 : (c + 1) * 128, 0:128] = src[c * 128 : (c + 1) * 128, :].astype(F32)
    for c in range(9):
        g = src[ROWS_OUT + c * 128 : ROWS_OUT + (c + 1) * 128, :].astype(F32)
        out[l, c * 128 : (c + 1) * 128, 128:192] = g[:, 0:64]
        out[l, half + c * 128 : half + (c + 1) * 128, 128:192] = g[:, 64:128]


def square_rows(ref, start, stop, acc):
    step = 64
    for at in range(start, stop, step):
        g = ref[at : min(at + step, stop), :].astype(F32)
        g = g * g
        for lane in range(0, g.shape[1], 128):
            part = g[:, lane : lane + 128]
            rows = part.shape[0]
            part = jnp.sum(part.reshape(rows // 8, 8, part.shape[1]), 0)
            if part.shape[1] < 128:
                part = jnp.concatenate([part, jnp.zeros((8, 128 - part.shape[1]), F32)], 1)
            acc = acc + part
    return acc


def total_of(x):
    return jnp.sum(jnp.sum(x, 0, keepdims=True), 1, keepdims=True)


def muon_kernel(column_width, row_width, n_pieces, place, *refs):
    pieces = refs[:n_pieces]
    (
        g2,
        headflat,
        exact,
        basis,
        mom,
        wide_w,
        wide_mom,
        down_w,
        down_mom,
    ) = refs[n_pieces : n_pieces + 9]
    (
        wide_new,
        wide_mom_new,
        wide_copy,
        down_new,
        down_mom_new,
        down_copy,
        share_grad,
        scal,
        flat,
        mid_rows,
        first_rows,
        coef,
        gfull,
        mats,
        powers,
    ) = refs[n_pieces + 9 :]
    wide_at, down_at, mine = place[2], place[3], place[4]
    start = pl.multiple_of(place[0], 192)
    count = place[1]
    inner = pieces[0].shape[0]
    total_pieces = n_pieces * inner
    mr, fr = MIDDLE_ROWS // total_pieces, FIRST_ROWS // total_pieces

    for k in range(n_pieces):
        for z in range(inner):
            at = mine ^ (k * inner + z)
            mid_rows[pl.ds(pl.multiple_of(at * mr, 16), mr), :] = pieces[k][z, 0:mr, :]
            first_rows[pl.ds(pl.multiple_of(at * fr, 16), fr), :] = pieces[k][z, mr : mr + fr, :]
            coef[pl.ds(pl.multiple_of(at * 16, 16), 16), :] = pieces[k][
                z, mr + fr : mr + fr + 16, :
            ].astype(F32)
    unpack_layer(first_rows, gfull, 0, 0)
    unpack_layer(mid_rows, gfull, 1, 1)
    gfull[2, 0:D, :] = g2[0:D, :]
    gfull[2, 3 * D : ROWS_OUT, :] = g2[3 * D :, :]
    gfull[2, D : 3 * D, 0:128] = mid_rows[PACKED : PACKED + 2 * D, :].astype(F32)
    tail = mid_rows[PACKED + 2 * D : PACKED + 3 * D, :].astype(F32)
    gfull[2, D : 2 * D, 128:192] = tail[:, 0:64]
    gfull[2, 2 * D : 3 * D, 128:192] = tail[:, 64:128]

    base = PACKED + PATCH_ROWS
    flat[0:PATCH_ROWS, :] = first_rows[PACKED:base, :].astype(F32)
    flat[PATCH_ROWS : PATCH_ROWS + HEAD_ROWS, :] = headflat[0:HEAD_ROWS, :]
    flat[TAIL_ROW : TAIL_ROW + TAIL_ROWS, :] = first_rows[base : base + TAIL_ROWS, :].astype(F32)
    flat[TAIL_ROW + TAIL_ROWS :, :] = jnp.zeros(
        (flat.shape[0] - TAIL_ROW - TAIL_ROWS, 128), F32
    )
    block = block_row(exact)

    sums = jnp.zeros((16, 128), F32)
    for at in range(total_pieces):
        sums = sums + coef[16 * at : 16 * (at + 1), :]
    c = sums[0:1, :] + sums[1:2, :] + sums[2:3, :]
    acc = jnp.zeros((8, 128), F32)
    acc = square_rows(first_rows, 0, PACKED, acc)
    acc = square_rows(mid_rows, 0, PACKED + 3 * D, acc)
    acc = square_rows(g2, 0, D, acc)
    acc = square_rows(g2, 3 * D, ROWS_OUT, acc)
    acc = square_rows(flat, 0, flat.shape[0], acc)
    squares = total_of(acc) + total_of(jnp.where(lanes((1, BLOCK_PAD)) < 2 * D + CLASSES, block * block, 0.0))
    coef_square = jnp.sum(c * c, 1, keepdims=True)
    norm = jnp.sqrt(squares - coef_square)
    factor = CLIP_AT / jnp.maximum(norm, CLIP_AT)
    scal[...] = jnp.zeros_like(scal)
    for k, value in enumerate((norm, factor, jnp.sqrt(coef_square), exact[0:1, 0:1], c)):
        scal[k : k + 1, :] = jnp.broadcast_to(value, (1, 128))

    block = block - split_dot(
        jnp.broadcast_to(c[:, 0:BASIS], (8, BASIS)), basis[...], NN
    )[0:1, :]
    put_entries(flat, 0, FINAL_AT, block, 2 * D + CLASSES)
    rows = share_grad.shape[0]
    at, shift = place[5], place[6]
    base_row = pl.multiple_of((at // 8) * 8, 8)
    off = at - base_row
    window = flat[pl.ds(base_row, rows + 16), :]
    here = pltpu.roll(window, lax.rem(rows + 16 - off, rows + 16), 0)
    there = pltpu.roll(window, lax.rem(rows + 15 - off, rows + 16), 0)[0:rows]
    here = here[0:rows]
    back = lax.rem(128 - shift, 128)
    g = jnp.where(
        lanes((rows, 128)) < 128 - shift, pltpu.roll(here, back, 1), pltpu.roll(there, back, 1)
    )
    share_grad[...] = g * factor

    row = lax.broadcasted_iota(jnp.int32, (FF, 1), 0)
    sizes = []
    eye = (
        lax.broadcasted_iota(jnp.int32, (D, D), 0) == lax.broadcasted_iota(jnp.int32, (D, D), 1)
    ).astype(F32)
    for k in range(2 * LAYERS):
        l, which = divmod(k, 2)
        if which == 0:
            m = mom[pl.ds(start // column_width, FF // column_width), l, 0:column_width, :]
            m = BETA_ONE * m.reshape(FF, D) + factor * gfull[l, pl.ds(start, FF), :]
            m = jnp.where(row < count, m, 0.0)
        else:
            m = BETA_ONE * mom[:, l, column_width:, :].reshape(FF, D) + factor * gfull[l, WIDE:ROWS_OUT, :]
        size = 1.0 / (jnp.sqrt(total_of(m * m)) + SHAPE_EPS)
        sizes.append(size)
        x = m * size
        mats[k] = split_dot(x, x, TN)
        powers[k] = eye

    def polynomial(k):
        a = parts(mats[k])
        b = parts_dot(a, a, NN)
        return a, 3.4445 * eye - 4.775 * mats[k] + 2.0315 * b

    def step(it, carry):
        polys = [polynomial(k) for k in range(2 * LAYERS)]
        ps = [parts(p) for _, p in polys]
        ts = [parts(parts_dot(p, a, NN)) for (a, _), p in zip(polys, ps)]
        for k in range(2 * LAYERS):
            mats[k] = parts_dot(ts[k], ps[k], NN)
            powers[k] = parts_dot(ps[k], parts(powers[k]), NN)
        return carry

    lax.fori_loop(0, 4, step, 0)
    side = jnp.where(count == 4 * D, 768.0, jnp.where(count == 3 * D, 576.0, 192.0))
    rate = jnp.sqrt(jnp.full((1, 1), 1.0, F32) * side) * (MUON_RATE * 0.2)
    for k in range(2 * LAYERS):
        l, which = divmod(k, 2)
        _, p = polynomial(k)
        q = parts_dot(parts(p), parts(powers[k]), NN)
        if which == 0:
            g = own_rows(gfull, l, wide_at, column_width)
            own = BETA_ONE * wide_mom[l] + factor * g
            update = split_dot(own * sizes[k], q, NN)
            new = wide_w[l] - rate * update
            wide_mom_new[l] = own
            wide_new[l] = new
            wide_copy[l] = new.astype(BF)
        else:
            g = own_rows(gfull, l, down_at, row_width)
            own = BETA_ONE * down_mom[l] + factor * g
            update = split_dot(own * sizes[k], q, NN)
            new = down_w[l] - (MUON_RATE * 0.2 * FF**0.5) * update
            down_mom_new[l] = own
            down_new[l] = new
            down_copy[l] = new.astype(BF)


def cost(micros):
    return pl.CostEstimate(
        flops=int(micros * 1.15e9), bytes_accessed=int(micros * 1e6), transcendentals=0
    )


def pad_rows(x, rows):
    return jnp.pad(x, (0, rows * 128 - x.shape[0])).reshape(rows, 128)


def pack_shard(wide_t, down):
    rows = jnp.concatenate([wide_t, down], 1)
    rows = rows.reshape(-1, D).astype(BF)
    a_rows, h = half_rows(rows.shape[0])
    head = jnp.pad(rows[:, :128], ((0, a_rows - rows.shape[0]), (0, 0)))
    tail = jnp.pad(rows[:, 128:], ((0, 2 * h - rows.shape[0]), (0, 0)))
    tail = jnp.concatenate([tail[:h], tail[h:]], 1)
    fill = -(a_rows + h) % 16
    return jnp.concatenate([head, tail] + ([jnp.zeros((fill, 128), BF)] if fill else []), 0)


def stage_masks(stages):
    masks = [0]
    for low, width in reversed(stages):
        masks = [a ^ (m << low) for m in range(1 << width) for a in masks]
    return masks


def gather_stages(arrays, stages, devices, apart=2):
    for depth in reversed(range(len(stages))):
        low, width = stages[depth]
        got = [swap(x, m << low, devices) for m in range(1, 1 << width) for x in arrays]
        arrays = arrays + got
        if depth >= apart:
            arrays = [jnp.concatenate(arrays, 0)]
    return arrays


def swap(x, mask, devices):
    return lax.ppermute(x, AXES, [(i, i ^ mask) for i in range(devices)])


def local(
    patches,
    groups,
    labels,
    wide_w,
    down_w,
    plain,
    wide_mom,
    down_mom,
    plain_first,
    plain_second,
    basis_plain,
):
    devices = lax.axis_size(AXES)
    bits = devices.bit_length() - 1
    me = lax.axis_index(AXES).astype(jnp.int32)
    images = patches.shape[0]
    share = plain.shape[0]
    column_width = wide_w.shape[2]
    row_width = down_w.shape[1]
    vmem = pl.BlockSpec(memory_space=pltpu.VMEM)
    smem = pl.BlockSpec(memory_space=pltpu.SMEM)
    params = pltpu.CompilerParams(vmem_limit_bytes=VMEM_LIMIT)
    S = jax.ShapeDtypeStruct

    number_of = [(0, 1), (1, 2), (3, 2)]
    stages = number_of + ([(5, 2), (7, 1)] if bits == 8 else [(b, 1) for b in range(5, bits)])

    wide_t = jnp.transpose(wide_w, (0, 2, 1))
    plain_rows = -(-(share + 127) // 2048) * 16
    rows = plain_rows
    plain_block = pad_rows(plain, plain_rows)
    high = lax.reduce_precision(plain_block, 8, 7)
    low_half = (plain_block - high).astype(BF)
    weights_one = pack_shard(wide_t[:1], down_w[:1])
    shard_one = jnp.concatenate([high.astype(BF), weights_one, low_half], 0)
    shard_two = pack_shard(wide_t[1:], down_w[1:])
    weight_rows = weights_one.shape[0]

    one = gather_stages([shard_one[None]], stages[2:], devices, 0)[0]
    two = gather_stages([shard_two[None]], stages[2:], devices, 0)
    first_masks = stage_masks(stages[2:])
    top = 3 * devices // 4
    compact = bits == 5 and top * share <= CLS_AT
    body = rows + weight_rows
    if compact:
        low_top = lax.dynamic_index_in_dim(one[:, body:], (me >> 3) ^ 3, 0, keepdims=False)
        one = jnp.concatenate([one[:, :body].reshape(-1, 128), low_top], 0)
    else:
        one = one.reshape(-1, 128)
    one = gather_stages([one[None]], stages[1:2], devices)
    one[0] = one[0] + 0.0 * jnp.max(two[0][:, 0, 0])
    pieces_one = gather_stages([jnp.concatenate(one, 0)], stages[:1], devices)
    two = gather_stages(two, stages[1:2], devices)
    places = (first_masks, stage_masks(stages[:2]), top if compact else None)

    lead = jnp.clip(FINAL_AT - me * share + BLOCK_PAD, 0, share + BLOCK_PAD)
    basis_block = lax.dynamic_slice(
        jnp.pad(basis_plain, ((0, 0), (BLOCK_PAD, BLOCK_PAD))), (0, lead), (BASIS, BLOCK_PAD)
    )

    number = me[None]
    groups = groups.astype(jnp.int32)
    labels = labels.astype(jnp.int32)
    flat_rows = -(-((devices - 1) * share // 128 + rows + 8) // 8) * 8
    n = images * TQ
    saved = [
        S((n, D), F32),
        S((n, D), BF),
        S((images, TK, D), BF),
        S((images, TK, D), BF),
        S((images, HEADS, TQ, TK), F32),
        S((n, D), BF),
        S((n, FF), BF),
        S((n, FF), F32),
    ]
    rows_spec = pl.BlockSpec((TQ, D), lambda i: (i, 0))
    wide_spec = pl.BlockSpec((TQ, FF), lambda i: (i, 0))
    key_spec = pl.BlockSpec((1, TK, D), lambda i: (i, 0, 0))
    patch_spec = pl.BlockSpec((1, PATCHES, PATCH_DIM), lambda i: (i, 0, 0))
    saved_specs = [
        rows_spec,
        rows_spec,
        key_spec,
        key_spec,
        pl.BlockSpec((1, HEADS, TQ, TK), lambda i: (i, 0, 0, 0)),
        rows_spec,
        wide_spec,
        wide_spec,
    ]
    factor_rows = EXACT_ROWS + -(-FACTOR_BLOCKS * images // 8) * 8
    x0, *saved0, x1, gains0, wt0, dn0, flat = pl.pallas_call(
        functools.partial(
            start_kernel, devices, share, column_width, row_width, places, len(pieces_one)
        ),
        grid=(images,),
        out_shape=[S((n, D), F32)]
        + saved
        + [
            S((n, D), F32),
            S((8, D), F32),
            S((1, WIDE, D), BF),
            S((1, FF, D), BF),
            S((flat_rows, 128), F32),
        ],
        in_specs=[smem] * 2 + [vmem] * len(pieces_one) + [patch_spec],
        out_specs=[rows_spec] + saved_specs + [rows_spec] + [vmem] * 4,
        scratch_shapes=[
            pltpu.VMEM((devices, rows, 128), F32),
            pltpu.VMEM((devices, weight_rows, 128), BF),
            pltpu.VMEM((ROWS_OUT, D), F32),
            pltpu.VMEM((4, rows + 8, 128), F32),
            pltpu.VMEM((2, PATCH_DIM, 128), F32),
            pltpu.VMEM((2, TQ, 128), F32),
            pltpu.VMEM((PATCH_DIM, D), BF),
        ],
        compiler_params=params,
        cost_estimate=cost(20),
        name="start",
    )(groups, number, *pieces_one, patches)

    two, x1 = lax.optimization_barrier((two, x1))
    pieces_two = gather_stages(two, stages[:1], devices)
    *saved1, gains1, gstream, kv, factors, small, wt12, dn12 = pl.pallas_call(
        functools.partial(
            forward_kernel,
            float(images * devices),
            images,
            column_width,
            row_width,
            stage_masks(stages),
            len(pieces_two),
        ),
        grid=(images,),
        out_shape=saved
        + [
            S((8, D), F32),
            S((n, D), F32),
            S((3 * D, 128), F32),
            S((factor_rows, 128), F32),
            S((16, CLASSES_PAD), F32),
            S((2, WIDE, D), BF),
            S((2, FF, D), BF),
        ],
        in_specs=[smem] * 3 + [vmem, rows_spec] + [vmem] * len(pieces_two),
        out_specs=saved_specs + [vmem] * 7,
        scratch_shapes=[
            pltpu.VMEM((devices, shard_two.shape[0], 128), BF),
            pltpu.VMEM((ROWS_OUT, D), F32),
            pltpu.VMEM((8, D, 128), F32),
            pltpu.VMEM((n, D), F32),
            pltpu.VMEM((images, TK, D), BF),
            pltpu.VMEM((images, TK, D), BF),
            pltpu.VMEM((n, D), BF),
            pltpu.VMEM((n, D), BF),
        ]
        + [pltpu.VMEM((16, D), F32)] * 6
        + [pltpu.VMEM((n, D), BF)],
        compiler_params=params,
        cost_estimate=cost(30),
        name="forward",
    )(groups, labels, number, flat, x1, *pieces_two)

    mom_shard = jnp.concatenate([jnp.transpose(wide_mom, (0, 2, 1)), down_mom], 1)
    mom_all = lax.all_gather(mom_shard, AXES, axis=0)
    factors, mom_all = lax.optimization_barrier((factors, mom_all))
    gstream, factors = lax.optimization_barrier((gstream, factors))
    factors_all = lax.all_gather(factors, AXES, axis=0)
    back_scratch = [
        pltpu.VMEM((n, D), BF),
        pltpu.VMEM((n, FF), BF),
        pltpu.VMEM((n, D), BF),
        pltpu.VMEM((n, D), BF),
        pltpu.VMEM((n, D), BF),
        pltpu.VMEM((n, D), BF),
        pltpu.VMEM((n, D), BF),
        pltpu.VMEM((n, D), BF),
        pltpu.VMEM((n, D), BF),
        pltpu.VMEM((n, FF), BF),
    ]
    gstream1, middle_keep, middle_send, vec1, upb1 = pl.pallas_call(
        functools.partial(middle_kernel, images),
        out_shape=[
            S((n, D), F32),
            S((MIDDLE_ROWS // 2, 128), F32),
            S((MIDDLE_ROWS // 2, 128), F32),
            S((8, D), F32),
            S((8, FF), F32),
        ],
        grid=(images,),
        in_specs=[smem] * 2 + [rows_spec] + saved_specs + [vmem, rows_spec] + [vmem] * 3,
        out_specs=[rows_spec] + [vmem] * 4,
        scratch_shapes=[pltpu.VMEM((MIDDLE_ROWS, 128), F32)] + back_scratch,
        compiler_params=params,
        cost_estimate=cost(23),
        name="middle",
    )(groups, number, x1, *saved1, gains1, gstream, wt12, dn12, kv)

    first_keep, first_send = pl.pallas_call(
        functools.partial(first_kernel, images),
        out_shape=[S((FIRST_ROWS // 2, 128), F32)] * 2,
        grid=(images,),
        in_specs=[smem] * 2
        + [rows_spec]
        + saved_specs
        + [vmem, rows_spec]
        + [vmem] * 2
        + [patch_spec]
        + [vmem] * 3,
        out_specs=[vmem] * 2,
        scratch_shapes=[
            pltpu.VMEM((FIRST_ROWS, 128), F32),
            pltpu.VMEM((TQ, D), F32),
            pltpu.VMEM((8, D), F32),
            pltpu.VMEM((8, FF), F32),
            pltpu.VMEM((2, PATCH_DIM, 128), F32),
            pltpu.VMEM((2, TQ + 16, 128), F32),
        ]
        + back_scratch,
        compiler_params=params,
        cost_estimate=cost(25),
        name="first",
    )(groups, number, x0, *saved0, gains0, gstream1, wt0, dn0, patches, small, vec1, upb1)

    exact, extra = pl.pallas_call(
        functools.partial(coefficient_kernel, devices),
        grid=(1,),
        out_shape=[S((EXACT_ROWS, 128), F32), S((16, 128), F32)],
        in_specs=[pl.BlockSpec((devices, EXACT_ROWS, 128), lambda i: (0, 0, 0)), vmem],
        out_specs=[vmem] * 2,
        compiler_params=params,
        cost_estimate=cost(2),
        name="coefficients",
    )(factors_all, basis_block)

    g2, headflat = pl.pallas_call(
        functools.partial(late_kernel, devices, images),
        out_shape=[S((ROWS_OUT, D), F32), S((HEAD_ROWS + 4, 128), F32)],
        in_specs=[vmem],
        out_specs=[vmem] * 2,
        scratch_shapes=[pltpu.VMEM((8, D, 128), F32)],
        compiler_params=params,
        cost_estimate=cost(4),
        name="late",
    )(factors_all.reshape(devices * factor_rows, 128))

    split_bits = 5
    for bit in range(split_bits, bits):
        extra = extra + swap(extra, 1 << bit, devices)
    if bits > split_bits:
        c = extra[0] + extra[1] + extra[2]
        split = []
        for k in range(3):
            split.append(lax.reduce_precision(c, 8, 7))
            c = c - split[-1]
        extra = jnp.concatenate([jnp.stack(split), extra[3:]], 0)
    kept = None
    for low, width in number_of:
        ways = 1 << width
        mine = (me >> low) & (ways - 1)
        if kept is None:
            kept = [
                middle_keep + swap(middle_send, 1, devices),
                first_keep + swap(first_send, 1, devices),
            ]
            kept = jnp.concatenate([x.reshape(4, x.shape[0] // 4, 128) for x in kept], 1)
            continue
        total = lax.dynamic_index_in_dim(kept, mine, 0, keepdims=False)
        for m in range(1, ways):
            send = lax.dynamic_index_in_dim(kept, mine ^ m, 0, keepdims=False).astype(BF)
            total = total + swap(send, m << low, devices).astype(F32)
        if low == 1:
            total, extra, g2, headflat = lax.optimization_barrier((total, extra, g2, headflat))
            mr = MIDDLE_ROWS // 8
            kept = jnp.concatenate(
                [
                    total[:mr].reshape(4, mr // 4, 128),
                    total[mr:].reshape(4, (total.shape[0] - mr) // 4, 128),
                ],
                1,
            )
        else:
            kept = total
    for bit in range(split_bits, bits):
        small_part = kept.astype(BF)
        kept = small_part.astype(F32) + swap(small_part, 1 << bit, devices).astype(F32)
    piece = jnp.concatenate([kept, extra], 0).astype(BF)[None]
    pieces = gather_stages([piece], number_of, devices)

    first_column = me * column_width
    in_q = first_column < 3 * D
    in_o = first_column < 4 * D
    start = jnp.where(in_q, 0, jnp.where(in_o, 3 * D, 4 * D))
    count = jnp.where(in_q, 3 * D, jnp.where(in_o, D, FF))
    piece_number = ((me & 1) << 4) | (((me >> 1) & 3) << 2) | ((me >> 3) & 3)
    at = me * share
    spots = jnp.stack(
        [start, count, first_column, WIDE + me * row_width, piece_number, at // 128, at % 128]
    )
    wide_shape = (LAYERS, column_width, D)
    down_shape = (LAYERS, row_width, D)
    flat_rows = -(-((devices - 1) * share // 128 + rows + 24) // 8) * 8
    (
        wide_new,
        wide_mom_new,
        wide_copy,
        down_new,
        down_mom_new,
        down_copy,
        share_grad,
        scal,
    ) = pl.pallas_call(
        functools.partial(muon_kernel, column_width, row_width, len(pieces)),
        out_shape=[
            S(wide_shape, F32),
            S(wide_shape, F32),
            S(wide_shape, BF),
            S(down_shape, F32),
            S(down_shape, F32),
            S(down_shape, BF),
            S((rows, 128), F32),
            S((8, 128), F32),
        ],
        in_specs=[smem] + [vmem] * (len(pieces) + 9),
        out_specs=[vmem] * 8,
        scratch_shapes=[
            pltpu.VMEM((flat_rows, 128), F32),
            pltpu.VMEM((MIDDLE_ROWS, 128), BF),
            pltpu.VMEM((FIRST_ROWS, 128), BF),
            pltpu.VMEM((16 * 32, 128), F32),
            pltpu.VMEM((LAYERS, ROWS_OUT + 16, D), F32),
            pltpu.VMEM((2 * LAYERS, D, D), F32),
            pltpu.VMEM((2 * LAYERS, D, D), F32),
        ],
        compiler_params=pltpu.CompilerParams(vmem_limit_bytes=32 * 1024 * 1024),
        cost_estimate=cost(20),
        name="muon",
    )(
        spots.astype(jnp.int32),
        *pieces,
        g2,
        headflat,
        exact,
        basis_block,
        mom_all,
        wide_t,
        jnp.transpose(wide_mom, (0, 2, 1)),
        down_w,
        down_mom,
    )
    grad_norm, _, removed_norm, loss_sum = [scal[k, 0] for k in range(4)]
    clipped = share_grad.reshape(-1)[:share]
    first_new = BETA_ONE * plain_first + (1.0 - BETA_ONE) * clipped
    second_new = BETA_TWO * plain_second + (1.0 - BETA_TWO) * clipped * clipped
    first_hat = first_new / (1.0 - BETA_ONE**STEP)
    second_hat = second_new / (1.0 - BETA_TWO**STEP)
    plain_new = plain - ADAM_RATE * (
        first_hat / (jnp.sqrt(second_hat) + ADAM_EPS) + DECAY_RATE * plain
    )
    plain_copy = plain_new.astype(BF)
    return (
        loss_sum,
        removed_norm,
        grad_norm,
        *[jnp.transpose(x, (0, 2, 1)) for x in (wide_new, wide_mom_new, wide_copy)],
        down_new,
        down_mom_new,
        down_copy,
        plain_new,
        first_new,
        second_new,
        plain_copy,
    )


def solution(mesh):
    placed = (
        P(AXES, None, None),
        P(AXES),
        P(AXES),
        P(None, None, AXES),
        P(None, AXES, None),
        P(AXES),
        P(None, None, AXES),
        P(None, AXES, None),
        P(AXES),
        P(AXES),
        P(None, AXES),
    )
    return jax.shard_map(
        local,
        mesh=mesh,
        in_specs=placed,
        out_specs=(
            P(),
            P(),
            P(),
            P(None, None, AXES),
            P(None, None, AXES),
            P(None, None, AXES),
            P(None, AXES, None),
            P(None, AXES, None),
            P(None, AXES, None),
            P(AXES),
            P(AXES),
            P(AXES),
            P(AXES),
        ),
        check_vma=False,
    )
```

```python
import functools
import math

import jax
import jax.numpy as jnp
from jax import lax
from jax.experimental import pallas as pl
from jax.experimental.pallas import tpu as pltpu
from jax.sharding import PartitionSpec as P

D = 192
HEADS = 3
HD = 64
FF = 768
PATCH_DIM = 768
CLASSES = 1000
CLASSES_PAD = 1024
LAYERS = 3
SEQ = 325
PATCHES = SEQ - 1
LEN_MID = 197
LEN_SHORT = 101
BASIS = 64
STEP = 10
WIDE = 1536
ROWS_OUT = WIDE + FF

HEAD_AT = PATCH_DIM * D
CLS_AT = HEAD_AT + D * CLASSES
PATCH_B_AT = CLS_AT + D
POS_AT = PATCH_B_AT + D
VEC_AT = POS_AT + SEQ * D
VEC_LAYER = 6 * D + FF
FINAL_AT = VEC_AT + LAYERS * VEC_LAYER
HEAD_B_AT = FINAL_AT + 2 * D
USED = HEAD_B_AT + CLASSES
HEAD_ROWS = D * CLASSES // 128
BLOCK_PAD = 2 * D + CLASSES_PAD
PATCH_ROWS = HEAD_AT // 128
TAIL_ROW = CLS_AT // 128
VEC_ROW = (VEC_AT + VEC_LAYER) // 128
TAIL_ROWS = VEC_ROW + 1 - TAIL_ROW
VEC_ROWS = FINAL_AT // 128 + 1 - VEC_ROW

PACKED = ROWS_OUT * 3 // 2
MIDDLE_ROWS = 4096
FIRST_ROWS = 5120
VEC_KEPT = PACKED + 3 * D

TQ = 336
TK = 384
CLS_ROW = 0
PATCH_AT = 8
SIZES = ((112, 128), (208, 256), (336, 384))

NORM_EPS = 1e-06
CLIP_AT = 0.02
MUON_RATE = 0.3
ADAM_RATE = 0.05
BETA_ONE = 0.5
BETA_TWO = 0.95
DECAY_RATE = 0.01
ADAM_EPS = 1e-08
SHAPE_EPS = 1e-07
MASKED = -1e30
GELU_C = math.sqrt(2.0 / math.pi)
GELU_K = 0.044715

F32 = jnp.float32
BF = jnp.bfloat16
AXES = ("dp", "fsdp")
NN = (((1,), (0,)), ((), ()))
NT = (((1,), (1,)), ((), ()))
TN = (((0,), (0,)), ((), ()))
VMEM_LIMIT = 60 * 1024 * 1024


def dot(a, b, how):
    return lax.dot_general(a, b, how, preferred_element_type=F32)


def lanes(shape):
    return lax.broadcasted_iota(jnp.int32, shape, len(shape) - 1)


def head_mask(h):
    lane = lanes((1, D))
    return jnp.where((lane >= h * HD) & (lane < (h + 1) * HD), 1.0, 0.0)


def norm_stats(x):
    mean = jnp.mean(x, -1, keepdims=True)
    centered = x - mean
    var = jnp.mean(centered * centered, -1, keepdims=True)
    rstd = lax.rsqrt(var + NORM_EPS)
    return centered * rstd, rstd


def norm_back(dn, xhat, rstd, gain):
    scaled = dn * gain
    m1 = jnp.mean(scaled, -1, keepdims=True)
    m2 = jnp.mean(scaled * xhat, -1, keepdims=True)
    return rstd * (scaled - m1 - xhat * m2)


def colsum(x):
    return jnp.sum(x, 0, keepdims=True)


def key_mask(length, keys):
    key = lanes((1, keys))
    return ((key >= PATCH_AT) & (key < PATCH_AT + length - 1)) | (key == CLS_ROW)


def by_size(group, body):
    pl.when(group == 0)(lambda: body(*SIZES[0]))
    pl.when(group == 1)(lambda: body(*SIZES[1]))
    pl.when((group != 0) & (group != 1))(lambda: body(*SIZES[2]))


def softmax_rows(scores):
    top = jnp.max(scores, -1, keepdims=True)
    e = jnp.exp(scores - top)
    return e / jnp.sum(e, -1, keepdims=True)


def merge(a, b, shift):
    if shift == 0:
        return a
    lane = lanes(a.shape)
    return jnp.where(
        lane < 128 - shift, pltpu.roll(a, 128 - shift, 1), pltpu.roll(b, 128 - shift, 1)
    )


def flat_vec(flat, at, n):
    blocks = []
    for j in range(-(-n // 128)):
        q, r = divmod(at + 128 * j, 128)
        blocks.append(merge(flat[q : q + 1, :], flat[q + 1 : q + 2, :], r))
    row = blocks[0] if len(blocks) == 1 else jnp.concatenate(blocks, 1)
    return row[:, :n]


def unpack_flat(blocks, flat, tmp, devices, share):
    rows = blocks.shape[1]
    lane = lanes((rows, 128))
    for d in range(devices):
        q, r = divmod(d * share, 128)
        block = blocks[d]
        if r == 0:
            flat[q : q + rows, :] = block
            continue
        slot = d % 4
        tmp[slot, 8 : 8 + rows, :] = pltpu.roll(block, r, 1)
        tmp[slot, 7:8, :] = flat[q : q + 1, :]
        flat[q : q + rows, :] = jnp.where(
            lane >= r, tmp[slot, 8 : 8 + rows, :], tmp[slot, 7 : 7 + rows, :]
        )


def unpack_pairs(flat, row, pairs, out, out_at):
    a = flat[pl.ds(row, pairs, stride=3), :]
    b = flat[pl.ds(row + 1, pairs, stride=3), :]
    c = flat[pl.ds(row + 2, pairs, stride=3), :]
    out[0, pl.ds(out_at, pairs, stride=2), :] = a
    out[1, pl.ds(out_at, pairs, stride=2), :] = b
    out[0, pl.ds(out_at + 1, pairs, stride=2), :] = merge(b, c, 64)
    out[1, pl.ds(out_at + 1, pairs, stride=2), :] = pltpu.roll(c, 64, 1)


def rows192(ref, at, n):
    return jnp.concatenate([ref[0, at : at + n, :], ref[1, at : at + n, 0:64]], 1)


def pack_pairs(src, src_at, flat, row, pairs):
    a = src[0, pl.ds(src_at, pairs, stride=2), :]
    b = src[1, pl.ds(src_at, pairs, stride=2), :]
    c = src[0, pl.ds(src_at + 1, pairs, stride=2), :]
    e = src[1, pl.ds(src_at + 1, pairs, stride=2), :]
    lane = lanes(a.shape)
    c = pltpu.roll(c, 64, 1)
    flat[pl.ds(row, pairs, stride=3), :] = a
    flat[pl.ds(row + 1, pairs, stride=3), :] = jnp.where(lane < 64, b, c)
    flat[pl.ds(row + 2, pairs, stride=3), :] = jnp.where(lane < 64, c, pltpu.roll(e, 64, 1))


def unpack_head(flat, out):
    lane = lanes((12, 128))
    for rho in range(16):
        for k in range(8):
            q, r = divmod(1000 * rho + 128 * k, 128)
            a = flat[pl.ds(HEAD_AT // 128 + q, 12, stride=125), :]
            b = flat[pl.ds(HEAD_AT // 128 + q + 1, 12, stride=125), :]
            block = merge(a, b, r)
            if k == 7:
                block = jnp.where(lane < CLASSES - 896, block, 0.0)
            out[k, pl.ds(rho, 12, stride=16), :] = block


def pack_head(src, out):
    lane = lanes((12, 128))
    for j in range(125):
        rho, c = divmod(128 * j, 1000)
        k, s = divmod(c, 128)
        a = src[k, pl.ds(rho, 12, stride=16), :]
        if s:
            b = a
            if k < 7:
                b = src[k + 1, pl.ds(rho, 12, stride=16), :]
            a = merge(a, b, s)
        left = 1000 - c
        if left < 128:
            nxt = src[0, pl.ds(rho + 1, 12, stride=16), :]
            a = jnp.where(lane < left, a, pltpu.roll(nxt, left, 1))
        out[pl.ds(j, 12, stride=125), :] = a


FACTOR_FLOW = 24
FACTOR_DLOGITS = 26
FACTOR_BLOCKS = 34
EXACT = 13
EXACT_ROWS = 16


def put_factor(ref, block, value, images):
    for k in range(-(-value.shape[1] // 128)):
        part = value[0:images, 128 * k : 128 * (k + 1)].astype(F32)
        at = EXACT_ROWS + (block + k) * images
        ref[at : at + images, 0 : part.shape[1]] = part


def put_entries(ref, shift_rows, at, row, n):
    lane = lanes((1, 128))
    done = 0
    while done < n:
        q, r = divmod(at + done, 128)
        q = q + shift_rows
        take = min(128 - r, n - done)
        block, off = divmod(done, 128)
        piece = row[:, 128 * block : 128 * (block + 1)]
        if off + take > 128:
            piece = merge(piece, row[:, 128 * (block + 1) : 128 * (block + 2)], off)
            off = 0
        shift = (r - off) % 128
        if shift:
            piece = pltpu.roll(piece, shift, 1)
        if take < 128:
            piece = jnp.where((lane >= r) & (lane < r + take), piece, ref[q : q + 1, :])
        ref[q : q + 1, :] = piece
        done += take


def image_rows(i):
    if isinstance(i, int):
        return pl.ds(i * TQ, TQ)
    return pl.ds(pl.multiple_of(i * TQ, 16), TQ)


def length_of(group):
    return jnp.where(group == 0, LEN_SHORT, jnp.where(group == 1, LEN_MID, SEQ))


def layer_vectors(flat, l):
    at = VEC_AT + l * VEC_LAYER
    six = [flat_vec(flat, at + k * D, D) for k in range(6)]
    return six, flat_vec(flat, at + 6 * D, FF)


def store_layer_grads(ref, parts):
    tails = []
    for at, g in parts:
        ref[at : at + g.shape[0], :] = g[:, 0:128]
        tails.append((at, g))
    half = ROWS_OUT // 2
    for at, g in tails:
        n = g.shape[0]
        low = max(0, min(n, half - at))
        if low > 0:
            ref[ROWS_OUT + at : ROWS_OUT + at + low, 0:64] = g[:low, 128:192]
        if low < n:
            start = at + low - half
            ref[ROWS_OUT + start : ROWS_OUT + start + n - low, 64:128] = g[low:, 128:192]


def half_rows(rows):
    return -(-rows // 8) * 8, -(-rows // 16) * 8


def unpack_weights(blocks, layers, column_width, row_width, asm, wt, dn):
    devices = blocks.shape[0]
    per_layer = column_width + row_width
    a_rows, h = half_rows(layers * per_layer)
    for l in range(layers):
        for d in range(devices):
            block = blocks[d].astype(F32)
            for at, n, to in (
                (l * per_layer, column_width, d * column_width),
                (l * per_layer + column_width, row_width, WIDE + d * row_width),
            ):
                asm[to : to + n, 0:128] = block[at : at + n]
                low = max(0, min(n, h - at))
                if low:
                    asm[to : to + low, 128:192] = block[a_rows + at : a_rows + at + low, 0:64]
                if low < n:
                    start = a_rows + at + low - h
                    asm[to + low : to + n, 128:192] = block[start : start + n - low, 64:128]
        wt[l] = asm[0:WIDE, :].astype(BF)
        dn[l] = asm[WIDE:ROWS_OUT, :].astype(BF)


def layer_forward(l, group, flat, wt, dn, gains, xin, xout, saved):
    mid, qs, ks, vs, probs, mixs, acts, gps = saved
    masks = [head_mask(h).astype(BF) for h in range(HEADS)]
    (gain1, shift1, out_bias, gain2, shift2, down_bias), up_bias = layer_vectors(flat, l)
    for k, value in enumerate((gain1, shift1, gain2, shift2)):
        gains[k : k + 1, :] = value

    def body(tq, tk):
        x = xin[0:tq, :]
        xhat, _ = norm_stats(x)
        n1 = (xhat * gain1 + shift1).astype(BF)
        q = (dot(n1, wt[0, 0:D, :], NT) * HD ** (-0.5)).astype(BF)
        k = dot(n1, wt[0, D : 2 * D, :], NT).astype(BF)
        v = dot(n1, wt[0, 2 * D : 3 * D, :], NT).astype(BF)
        qs[0:tq, :] = q
        ks[0, 0:tq, :] = k
        vs[0, 0:tq, :] = v
        ks[0, tq:tk, :] = jnp.zeros((tk - tq, D), BF)
        vs[0, tq:tk, :] = jnp.zeros((tk - tq, D), BF)
        valid = key_mask(length_of(group), tk)
        kk = ks[0, 0:tk, :]
        vv = vs[0, 0:tk, :]
        mix = None
        for h in range(HEADS):
            s = dot(q * masks[h], kk, NT)
            s = jnp.where(valid, s, MASKED)
            p = softmax_rows(s)
            p = p.astype(BF)
            probs[0, h, 0:tq, 0:tk] = p
            part = dot(p, vv * masks[h], NN)
            mix = part if mix is None else mix + part
        mix = mix.astype(BF)
        mixs[0:tq, :] = mix
        middle = x + dot(mix, wt[0, 3 * D : 4 * D, :], NT) + out_bias
        mid[0:tq, :] = middle
        xhat2, _ = norm_stats(middle)
        n2 = (xhat2 * gain2 + shift2).astype(BF)
        up = dot(n2, wt[0, 4 * D : WIDE, :], NT) + up_bias
        t = jnp.tanh(GELU_C * (up + GELU_K * (up * up * up)))
        half = 0.5 * (1.0 + t)
        act = (up * half).astype(BF)
        slope = half + 0.5 * up * (1.0 - t * t) * (GELU_C * (1.0 + 3.0 * GELU_K * (up * up)))
        gps[0:tq, :] = slope.astype(BF)
        acts[0:tq, :] = act
        xout[0:tq, :] = middle + dot(act, dn[0], NN) + down_bias
        if tq < TQ:
            xout[tq:TQ, :] = jnp.zeros((TQ - tq, D), F32)

    by_size(group, body)


def start_kernel(devices, share, column_width, row_width, places, n_pieces, groups, me, *refs):
    pieces, patches = refs[:n_pieces], refs[n_pieces]
    x0, mid, qs, ks, vs, probs, mixs, acts, gps, x1, gains, wt, dn, flat = refs[
        n_pieces + 1 : n_pieces + 15
    ]
    blocks, weights, asm, tmp, pw, pos, emb = refs[n_pieces + 15 :]
    image = pl.program_id(0)
    pl.when(image == 0)(
        lambda: unpack_start(
            devices, share, column_width, row_width, places, me[0], pieces, wt, dn, flat, blocks, weights,
            asm, tmp, pw, pos, emb,
        )
    )
    cls = flat_vec(flat, CLS_AT, D)
    patch_b = flat_vec(flat, PATCH_B_AT, D)
    e = dot(patches[0], emb[...], NN) + patch_b + rows192(pos, 8, PATCHES)
    x0[0:PATCH_AT, :] = jnp.concatenate(
        [cls + rows192(pos, 7, 1), jnp.zeros((PATCH_AT - 1, D), F32)], 0
    )
    x0[PATCH_AT : PATCH_AT + PATCHES, :] = e
    x0[PATCH_AT + PATCHES :, :] = jnp.zeros((TQ - PATCH_AT - PATCHES, D), F32)
    layer_forward(
        0, groups[image], flat, wt, dn, gains, x0, x1, (mid, qs, ks, vs, probs, mixs, acts, gps)
    )


def unpack_start(
    devices, share, column_width, row_width, places, me, pieces, wt, dn, flat, blocks, weights, asm, tmp,
    pw, pos, emb,
):
    inner_masks, outer_masks, top = places
    rows, weight_rows = blocks.shape[1], weights.shape[1]
    body = rows + weight_rows
    step = body if top is not None else body + rows
    for k, outer in enumerate(outer_masks):
        piece = pieces[k // pieces[0].shape[0]].at[k % pieces[0].shape[0]]
        for j, inner in enumerate(inner_masks):
            d = me ^ (outer | inner)
            at = j * step
            value = piece[at : at + rows, :].astype(F32)
            if top is None:
                value = value + piece[at + body : at + body + rows, :].astype(F32)
            blocks[d] = value
            weights[d] = piece[at + rows : at + body, :]
        if top is not None:
            d = top | ((me ^ outer) & 7)
            at = len(inner_masks) * step
            blocks[d] = blocks[d] + piece[at : at + rows, :].astype(F32)
    unpack_flat(blocks, flat, tmp, devices, share)
    unpack_weights(weights, 1, column_width, row_width, asm, wt, dn)
    unpack_pairs(flat, 0, PATCH_DIM // 2, pw, 0)
    unpack_pairs(flat, POS_AT // 128, SEQ // 2, pos, 7)
    last = flat_vec(flat, POS_AT + (SEQ - 1) * D, D)
    pos[0, 7 + SEQ - 1 : 7 + SEQ, :] = last[:, 0:128]
    pos[1, 7 + SEQ - 1 : 7 + SEQ, 0:64] = last[:, 128:192]
    emb[...] = rows192(pw, 0, PATCH_DIM).astype(BF)


def forward_kernel(
    total_images, images, column_width, row_width, masks, n_pieces, groups, labels, me, flat, x1, *refs
):
    pieces = refs[:n_pieces]
    mid, qs, ks, vs, probs, mixs, acts, gps, gains, *rest = refs[n_pieces:]
    gstream, kv, factors, small, wt_all, dn_all, weights, asm, hw, x2 = rest[:10]
    image = pl.program_id(0)

    @pl.when(image == 0)
    def _():
        inner = pieces[0].shape[0]
        for k in range(n_pieces):
            for j in range(inner):
                weights[me[0] ^ masks[k * inner + j]] = pieces[k][j]
        unpack_weights(weights, 2, column_width, row_width, asm, wt_all, dn_all)
        unpack_head(flat, hw)
        factors[...] = jnp.zeros_like(factors)

    layer_forward(
        1,
        groups[image],
        flat,
        wt_all,
        dn_all,
        gains,
        x1,
        x2.at[image_rows(image)],
        (mid, qs, ks, vs, probs, mixs, acts, gps),
    )
    pl.when(image == images - 1)(
        lambda: last_layer(
            total_images, images, groups, labels, flat, gstream, kv, factors, small, wt_all.at[1],
            dn_all.at[1], hw, x2, *rest[10:],
        )
    )


def last_layer(
    total_images, images, groups, labels, flat, gstream, kv, factors, small, wt, dn, hw, x2, kbuf, vbuf,
    dkbuf, dvbuf, clsbuf, qcls, mixcls, dmixcls, dqcls, midgrad, n1low,
):
    l = 2
    (gain1, shift1, out_bias, gain2, shift2, down_bias), up_bias = layer_vectors(flat, l)
    wk = wt[D : 2 * D, :]
    wv = wt[2 * D : 3 * D, :]
    clsbuf[...] = jnp.zeros_like(clsbuf)
    mixcls[...] = jnp.zeros_like(mixcls)
    kbuf[:, TQ:TK, :] = jnp.zeros((images, TK - TQ, D), BF)
    vbuf[:, TQ:TK, :] = jnp.zeros((images, TK - TQ, D), BF)

    def keys(i, carry):
        rows = image_rows(i)
        xhat, _ = norm_stats(x2[rows, :])
        n1 = (xhat * gain1 + shift1).astype(BF)
        kbuf[i, 0:TQ, :] = dot(n1, wk, NT).astype(BF)
        vbuf[i, 0:TQ, :] = dot(n1, wv, NT).astype(BF)
        clsbuf[pl.ds(i, 1), :] = x2[pl.ds(i * TQ + CLS_ROW, 1), :]
        return carry

    for i in range(images):
        keys(i, 0)
    xc = clsbuf[...]
    xhat1c, rstd1c = norm_stats(xc)
    n1c = (xhat1c * gain1 + shift1).astype(BF)
    qc = (dot(n1c, wt[0:D, :], NT) * HD ** (-0.5)).astype(BF)
    qcls[...] = qc.astype(F32)
    mask3 = jnp.concatenate([head_mask(h) for h in range(HEADS)] + [jnp.zeros((13, D), F32)], 0)

    def cls_probs(i):
        q3 = (qcls[pl.ds(i, 1), :] * mask3).astype(BF)
        s = dot(q3, kbuf[i], NT)
        s = jnp.where(key_mask(length_of(groups[i]), TK), s, MASKED)
        return q3, softmax_rows(s)

    def attend(i, carry):
        q3, p = cls_probs(i)
        m = dot(p.astype(BF), vbuf[i], NN)
        mixcls[pl.ds(i, 1), :] = colsum(m * mask3)
        return carry

    for i in range(images):
        attend(i, 0)
    mixc = mixcls[...].astype(BF)
    midc = xc + dot(mixc, wt[3 * D : 4 * D, :], NT) + out_bias
    xhat2c, rstd2c = norm_stats(midc)
    n2c = (xhat2c * gain2 + shift2).astype(BF)
    upc = dot(n2c, wt[4 * D : WIDE, :], NT) + up_bias
    tc = jnp.tanh(GELU_C * (upc + GELU_K * (upc * upc * upc)))
    halfc = 0.5 * (1.0 + tc)
    actc = (upc * halfc).astype(BF)
    gpc = halfc + 0.5 * upc * (1.0 - tc * tc) * (GELU_C * (1.0 + 3.0 * GELU_K * (upc * upc)))
    outc = midc + dot(actc, dn[...], NN) + down_bias

    fgain = flat_vec(flat, FINAL_AT, D)
    fshift = flat_vec(flat, FINAL_AT + D, D)
    head_b = jnp.concatenate(
        [flat_vec(flat, HEAD_B_AT, CLASSES), jnp.zeros((1, CLASSES_PAD - CLASSES), F32)], 1
    )
    row16 = lax.broadcasted_iota(jnp.int32, (16, 1), 0)
    real = (row16 < images).astype(F32)
    xhatf, rstdf = norm_stats(outc)
    flow = (xhatf * fgain + fshift).astype(BF)
    head_low = jnp.concatenate([hw[k] for k in range(8)], 1).astype(BF)
    cls_lane = lanes((16, CLASSES_PAD))
    logits = dot(flow, head_low, NN) + head_b
    logits = jnp.where(cls_lane < CLASSES, logits, MASKED)
    top = jnp.max(logits, -1, keepdims=True)
    e = jnp.exp(logits - top)
    total = jnp.sum(e, -1, keepdims=True)
    label = jnp.zeros((16, 1), jnp.int32)
    for i in range(images):
        label = jnp.where(row16 == i, labels[i], label)
    onehot = (cls_lane == label).astype(F32)
    picked = jnp.sum(jnp.where(cls_lane == label, logits, 0.0), -1, keepdims=True)
    loss = jnp.sum((top + jnp.log(total) - picked) * real, 0, keepdims=True)
    dlogits = (e / total - onehot) * (real / total_images)
    dlow = dlogits.astype(BF)
    dflow = dot(dlow, head_low, NT)
    put_factor(factors, FACTOR_FLOW, flow, images)
    put_factor(factors, FACTOR_DLOGITS, dlow, images)
    small[...] = jnp.zeros_like(small)
    exact = [jnp.broadcast_to(loss, (1, 128))]
    head_bias_grad = colsum(dlogits)
    exact += [head_bias_grad[:, 128 * k : 128 * (k + 1)] for k in range(8)]
    for value in (colsum(dflow * xhatf), colsum(dflow)):
        value = jnp.concatenate([value, jnp.zeros((1, 64), F32)], 1)
        exact += [value[:, 0:128], value[:, 128:256]]
    for k, value in enumerate(exact):
        factors[k : k + 1, :] = value
    gout = norm_back(dflow, xhatf, rstdf, fgain) * real

    ol = gout.astype(BF)
    dact = dot(ol, dn[...], NT)
    dup = dact * gpc * real
    ul = dup.astype(BF)
    dn2 = dot(ul, wt[4 * D : WIDE, :], NN)
    dmid = norm_back(dn2, xhat2c, rstd2c, gain2) + gout
    ml = dmid.astype(BF)
    small[4:5, 0:FF] = colsum(dup)
    small[10:11, 0:D] = colsum(dmid)
    small[11:12, 0:D] = colsum(dn2 * xhat2c)
    small[12:13, 0:D] = colsum(dn2)
    small[13:14, 0:D] = colsum(gout)
    dmixcls[...] = dot(ml, wt[3 * D : 4 * D, :], NN).astype(BF).astype(F32)
    dqcls[...] = jnp.zeros_like(dqcls)

    def attend_back(i, carry):
        q3, p = cls_probs(i)
        dm3 = (dmixcls[pl.ds(i, 1), :] * mask3).astype(BF)
        dp = dot(dm3, vbuf[i], NT)
        dv = dot(p.astype(BF), dm3, TN)
        ds = (p * (dp - jnp.sum(p * dp, -1, keepdims=True))).astype(BF)
        dq = dot(ds, kbuf[i], NN)
        dk = dot(ds, q3, TN)
        rows = image_rows(i)
        dkbuf[rows, :] = dk[0:TQ].astype(BF)
        dvbuf[rows, :] = dv[0:TQ].astype(BF)
        dqcls[pl.ds(i, 1), :] = colsum(dq * mask3) * HD ** (-0.5)
        return carry

    for i in range(images):
        attend_back(i, 0)
    dql = dqcls[...].astype(BF)
    dn1c = dot(dql, wt[0:D, :], NN)
    midgrad[...] = dmid
    dqcls[...] = dn1c
    for k, value in enumerate((ol, n2c, ml, mixc, dql, n1c)):
        put_factor(factors, 2 * k, value, images)
    for k, value in enumerate((actc, ul)):
        put_factor(factors, 12 + 6 * k, value, images)

    def stream_back(i, carry):
        dgain, dshift = carry
        rows = image_rows(i)
        xhat, rstd = norm_stats(x2[rows, :])
        n1low[rows, :] = (xhat * gain1 + shift1).astype(BF)
        dkl = dkbuf[rows, :]
        dvl = dvbuf[rows, :]
        dn1 = dot(dkl, wk, NN) + dot(dvl, wv, NN)
        at_cls = lax.broadcasted_iota(jnp.int32, (TQ, 1), 0) == CLS_ROW
        dn1 = dn1 + jnp.where(at_cls, dqcls[pl.ds(i, 1), :], 0.0)
        gin = norm_back(dn1, xhat, rstd, gain1)
        gstream[rows, :] = gin + jnp.where(at_cls, midgrad[pl.ds(i, 1), :], 0.0)
        return (dgain + colsum(dn1 * xhat), dshift + colsum(dn1))

    zero_row = jnp.zeros((1, D), F32)
    dgain, dshift = zero_row, zero_row
    for i in range(images):
        dgain, dshift = stream_back(i, (dgain, dshift))
    dwk = dot(dkbuf[...], n1low[...], TN)
    dwv = dot(dvbuf[...], n1low[...], TN)
    small[8:9, 0:D] = dgain
    small[9:10, 0:D] = dshift
    kv[0:D, :] = dwk[:, 0:128]
    kv[D : 2 * D, :] = dwv[:, 0:128]
    kv[2 * D :, 0:64] = dwk[:, 128:192]
    kv[2 * D :, 64:128] = dwv[:, 128:192]


def layer_back(
    images,
    group,
    x,
    mid,
    qs,
    ks,
    vs,
    probs,
    mixs,
    acts,
    gps,
    gains,
    gout,
    wt,
    dn,
    gin,
    gt,
    vec,
    upb,
    olbuf,
    ulbuf,
    n2buf,
    mlbuf,
    n1buf,
    dqbuf,
    dkbuf,
    dvbuf,
    mixbuf,
    actbuf,
):
    gain1, shift1, gain2, shift2 = [gains[k : k + 1, :] for k in range(4)]
    masks = [head_mask(h).astype(BF) for h in range(HEADS)]
    image = pl.program_id(0)
    start = pl.multiple_of(image * TQ, 16)

    @pl.when(image == 0)
    def _():
        vec[...] = jnp.zeros_like(vec)
        upb[...] = jnp.zeros_like(upb)

    def body(tq, tk):
        rows = pl.ds(start, tq)
        go = gout[0:tq, :]
        ol = go.astype(BF)
        olbuf[rows, :] = ol
        actbuf[rows, :] = acts[0:tq, :]
        mixbuf[rows, :] = mixs[0:tq, :]
        dact = dot(ol, dn[0], NT)
        dup = dact * gps[0:tq, :].astype(F32)
        ul = dup.astype(BF)
        ulbuf[rows, :] = ul
        dn2 = dot(ul, wt[0, 4 * D : WIDE, :], NN)
        xhat2, rstd2 = norm_stats(mid[0:tq, :])
        n2buf[rows, :] = (xhat2 * gain2 + shift2).astype(BF)
        dmid = norm_back(dn2, xhat2, rstd2, gain2) + go
        ml = dmid.astype(BF)
        mlbuf[rows, :] = ml
        upb[0:1, :] += colsum(dup)
        vec[2:3, :] += colsum(dmid)
        vec[3:4, :] += colsum(dn2 * xhat2)
        vec[4:5, :] += colsum(dn2)
        vec[5:6, :] += colsum(go)
        dmix = dot(ml, wt[0, 3 * D : 4 * D, :], NN).astype(BF)
        q = qs[0:tq, :]
        kk = ks[0, 0:tk, :]
        vv = vs[0, 0:tk, :]
        dq = dk = dv = None
        for h in range(HEADS):
            qh = q * masks[h]
            dmh = dmix * masks[h]
            low = probs[0, h, 0:tq, 0:tk]
            p = low.astype(F32)
            dp = dot(dmh, vv, NT)
            t = p * dp
            ds = (t - p * jnp.sum(t, -1, keepdims=True)).astype(BF)
            dv_h = dot(low, dmh, TN)
            dq_h = dot(ds, kk * masks[h], NN)
            dk_h = dot(ds, qh, TN)
            dq, dk, dv = (dq_h, dk_h, dv_h) if dq is None else (dq + dq_h, dk + dk_h, dv + dv_h)
        dql = (dq * HD ** (-0.5)).astype(BF)
        dkl = dk[0:tq].astype(BF)
        dvl = dv[0:tq].astype(BF)
        dqbuf[rows, :] = dql
        dkbuf[rows, :] = dkl
        dvbuf[rows, :] = dvl
        dn1 = (
            dot(dql, wt[0, 0:D, :], NN)
            + dot(dkl, wt[0, D : 2 * D, :], NN)
            + dot(dvl, wt[0, 2 * D : 3 * D, :], NN)
        )
        xhat1, rstd1 = norm_stats(x[0:tq, :])
        n1buf[rows, :] = (xhat1 * gain1 + shift1).astype(BF)
        vec[0:1, :] += colsum(dn1 * xhat1)
        vec[1:2, :] += colsum(dn1)
        gin[0:tq, :] = norm_back(dn1, xhat1, rstd1, gain1) + dmid
        if tq < TQ:
            rest = pl.ds(start + tq, TQ - tq)
            gin[tq:TQ, :] = jnp.zeros((TQ - tq, D), F32)
            for ref in (olbuf, ulbuf, n2buf, mlbuf, n1buf, dqbuf, dkbuf, dvbuf, mixbuf, actbuf):
                ref[rest, :] = jnp.zeros((TQ - tq, ref.shape[1]), BF)

    by_size(group, body)

    @pl.when(image == images - 1)
    def _():
        store_layer_grads(
            gt,
            [
                (0, dot(dqbuf[...], n1buf[...], TN)),
                (D, dot(dkbuf[...], n1buf[...], TN)),
                (2 * D, dot(dvbuf[...], n1buf[...], TN)),
                (3 * D, dot(mlbuf[...], mixbuf[...], TN)),
                (4 * D, dot(ulbuf[...], n2buf[...], TN)),
                (WIDE, dot(actbuf[...], olbuf[...], TN)),
            ],
        )


def share_halves(gt, keep, send, mine):
    half = keep.shape[0]
    keep[...] = gt[pl.ds(pl.multiple_of(mine * half, 8), half), :]
    send[...] = gt[pl.ds(pl.multiple_of((1 - mine) * half, 8), half), :]


def middle_kernel(images, groups, me, *refs):
    inputs, (kv, small) = refs[:13], refs[13:15]
    gin, keep, send, vec, upb, gt, *buffers = refs[15:]
    image = pl.program_id(0)
    layer_back(images, groups[image], *inputs, gin, gt, vec, upb, *buffers)

    @pl.when(image == images - 1)
    def _():
        gt[PACKED:VEC_KEPT, :] = kv[...]
        gt[VEC_KEPT:, :] = jnp.zeros((MIDDLE_ROWS - VEC_KEPT, 128), F32)
        put = functools.partial(put_entries, gt, VEC_KEPT - VEC_ROW)
        put_vectors(put, 1, vec, upb[0:1, :])
        put_vectors(put, 2, small[8:14, :], small[4:5, 0:FF])
        share_halves(gt, keep, send, me[0] & 1)


def first_kernel(images, groups, me, *refs):
    inputs, patches = refs[:13], refs[13]
    keep, send, gt, gin, vec, upb, pgrad, posgrad, *buffers = refs[14:]
    image = pl.program_id(0)
    layer_back(images, groups[image], *inputs, gin, gt, vec, upb, *buffers)

    @pl.when(image == 0)
    def _():
        pgrad[...] = jnp.zeros_like(pgrad)
        posgrad[...] = jnp.zeros_like(posgrad)

    g = gin[...]
    used = PATCH_AT + PATCHES
    posgrad[0, 0:used, :] += g[0:used, 0:128]
    posgrad[1, 0:used, 0:64] += g[0:used, 128:192]
    pg = dot(patches[0], g[PATCH_AT:used].astype(BF), TN)
    pgrad[0] += pg[:, 0:128]
    pgrad[1, :, 0:64] += pg[:, 128:192]
    pl.when(image == images - 1)(
        lambda: pack_first(keep, send, gt, vec, upb, pgrad, posgrad, me[0] & 1)
    )


def put_vectors(put, l, six, up):
    at = VEC_AT + l * VEC_LAYER
    for k in range(6):
        row = jnp.concatenate([six[k : k + 1, 0:D], jnp.zeros((1, 64), F32)], 1)
        put(at + k * D, row, D)
    put(at + 6 * D, up, FF)


def pack_first(keep, send, gt, vec, upb, pgrad, posgrad, core):
    def pos_rows(at):
        return jnp.concatenate([posgrad[0, at : at + 1, :], posgrad[1, at : at + 1, :]], 1)

    cls_row = pos_rows(CLS_ROW)
    patch_b = jnp.concatenate(
        [colsum(posgrad[k, PATCH_AT : PATCH_AT + PATCHES, :]) for k in range(2)], 1
    )
    posgrad[0, 7:8, :] = cls_row[:, 0:128]
    posgrad[1, 7:8, :] = cls_row[:, 128:256]
    base = PACKED + PATCH_ROWS
    gt[base:, :] = jnp.zeros((FIRST_ROWS - base, 128), F32)
    pack_pairs(pgrad, 0, gt, PACKED, PATCH_DIM // 2)
    pack_pairs(posgrad, 7, gt, base + POS_AT // 128 - TAIL_ROW, SEQ // 2)
    put = functools.partial(put_entries, gt, base - TAIL_ROW)
    put(CLS_AT, cls_row, D)
    put(PATCH_B_AT, patch_b, D)
    put(POS_AT + (SEQ - 1) * D, pos_rows(7 + SEQ - 1), D)
    put_vectors(put, 0, vec, upb[0:1, :])
    share_halves(gt, keep, send, core)


def parts(a):
    high = a.astype(BF)
    return high, (a - high.astype(F32)).astype(BF)


def parts_dot(a, b, how):
    return dot(a[0], b[0], how) + (dot(a[0], b[1], how) + dot(a[1], b[0], how))


def split_dot(a, b, how):
    return parts_dot(parts(a), parts(b), how)


def own_rows(ref, l, at, width):
    if width % 8 == 0:
        return ref[l, pl.ds(pl.multiple_of(at, 8), width), :]
    rows = -(-(width + 7) // 8) * 8
    base = pl.multiple_of((at // 8) * 8, 8)
    x = ref[l, pl.ds(base, rows), :]
    return pltpu.roll(x, lax.rem(rows - (at - base), rows), 0)[:width]


def coefficient_kernel(devices, gathered, basis, exact, extra):
    total = gathered[0]
    for d in range(1, devices):
        total = total + gathered[d]
    exact[...] = total
    c = split_dot(jnp.broadcast_to(block_row(exact), (8, BLOCK_PAD)), basis[...], NT)[0:1, :]
    extra[...] = jnp.zeros_like(extra)
    for k in range(3):
        high = c.astype(BF).astype(F32)
        extra[k : k + 1, 0:BASIS] = high
        c = c - high


def late_kernel(devices, images, gathered, g2, headflat, hg):
    rows = gathered.shape[0] // devices

    def factor(block, count):
        columns = []
        for b in range(block, block + count):
            parts = [
                gathered[pl.ds(EXACT_ROWS + b * images + i, devices, stride=rows), :]
                for i in range(images)
            ]
            columns.append(jnp.concatenate(parts, 0))
        return jnp.concatenate(columns, 1).astype(BF)

    ol, n2, ml, mix, dq, n1 = [factor(2 * k, 2)[:, 0:D] for k in range(6)]
    act, ul = factor(12, 6), factor(18, 6)
    g2[0:D, :] = dot(dq, n1, TN)
    g2[3 * D : 4 * D, :] = dot(ml, mix, TN)
    g2[4 * D : WIDE, :] = dot(ul, n2, TN)
    g2[WIDE:, :] = dot(act, ol, TN)
    flow = factor(FACTOR_FLOW, 2)[:, 0:D]
    for k in range(8):
        hg[k] = dot(flow, factor(FACTOR_DLOGITS + k, 1), TN)
    pack_head(hg, headflat)


def block_row(exact):
    pieces = [
        jnp.concatenate([exact[at : at + 1, :], exact[at + 1 : at + 2, 0:64]], 1) for at in (9, 11)
    ]
    pieces += [exact[1 + k : 2 + k, :] for k in range(8)]
    return jnp.concatenate(pieces, 1)


def unpack_layer(src, out, l, which):
    half = ROWS_OUT // 2
    for c in range(18):
        out[l, c * 128 : (c + 1) * 128, 0:128] = src[c * 128 : (c + 1) * 128, :].astype(F32)
    for c in range(9):
        g = src[ROWS_OUT + c * 128 : ROWS_OUT + (c + 1) * 128, :].astype(F32)
        out[l, c * 128 : (c + 1) * 128, 128:192] = g[:, 0:64]
        out[l, half + c * 128 : half + (c + 1) * 128, 128:192] = g[:, 64:128]


def square_rows(ref, start, stop, acc):
    step = 64
    for at in range(start, stop, step):
        g = ref[at : min(at + step, stop), :].astype(F32)
        g = g * g
        for lane in range(0, g.shape[1], 128):
            part = g[:, lane : lane + 128]
            rows = part.shape[0]
            part = jnp.sum(part.reshape(rows // 8, 8, part.shape[1]), 0)
            if part.shape[1] < 128:
                part = jnp.concatenate([part, jnp.zeros((8, 128 - part.shape[1]), F32)], 1)
            acc = acc + part
    return acc


def total_of(x):
    return jnp.sum(jnp.sum(x, 0, keepdims=True), 1, keepdims=True)


def muon_kernel(column_width, row_width, n_pieces, place, *refs):
    pieces = refs[:n_pieces]
    (
        g2,
        headflat,
        exact,
        basis,
        mom_far,
        wide_w,
        wide_mom,
        down_w,
        down_mom,
    ) = refs[n_pieces : n_pieces + 9]
    (
        wide_new,
        wide_mom_new,
        wide_copy,
        down_new,
        down_mom_new,
        down_copy,
        share_grad,
        scal,
        flat,
        mid_rows,
        first_rows,
        coef,
        gfull,
        mats,
        powers,
        mom,
        mom_sem,
    ) = refs[n_pieces + 9 :]
    wide_at, down_at, mine = place[2], place[3], place[4]
    start = pl.multiple_of(place[0], 192)
    count = place[1]
    inner = pieces[0].shape[0]
    total_pieces = n_pieces * inner
    mr, fr = MIDDLE_ROWS // total_pieces, FIRST_ROWS // total_pieces

    mom_copies = [
        pltpu.make_async_copy(mom_far.at[:, l], mom.at[l], mom_sem.at[l]) for l in range(LAYERS)
    ]
    for copy in mom_copies:
        copy.start()

    for k in range(n_pieces):
        for z in range(inner):
            at = mine ^ (k * inner + z)
            mid_rows[pl.ds(pl.multiple_of(at * mr, 16), mr), :] = pieces[k][z, 0:mr, :]
            first_rows[pl.ds(pl.multiple_of(at * fr, 16), fr), :] = pieces[k][z, mr : mr + fr, :]
            coef[pl.ds(pl.multiple_of(at * 16, 16), 16), :] = pieces[k][
                z, mr + fr : mr + fr + 16, :
            ].astype(F32)
    unpack_layer(first_rows, gfull, 0, 0)
    unpack_layer(mid_rows, gfull, 1, 1)
    gfull[2, 0:D, :] = g2[0:D, :]
    gfull[2, 3 * D : ROWS_OUT, :] = g2[3 * D :, :]
    gfull[2, D : 3 * D, 0:128] = mid_rows[PACKED : PACKED + 2 * D, :].astype(F32)
    tail = mid_rows[PACKED + 2 * D : PACKED + 3 * D, :].astype(F32)
    gfull[2, D : 2 * D, 128:192] = tail[:, 0:64]
    gfull[2, 2 * D : 3 * D, 128:192] = tail[:, 64:128]

    base = PACKED + PATCH_ROWS
    flat[0:PATCH_ROWS, :] = first_rows[PACKED:base, :].astype(F32)
    flat[PATCH_ROWS : PATCH_ROWS + HEAD_ROWS, :] = headflat[0:HEAD_ROWS, :]
    tail = first_rows[base:FIRST_ROWS, :].astype(F32)
    vectors = mid_rows[VEC_KEPT : VEC_KEPT + 32, :].astype(F32)
    flat[TAIL_ROW:VEC_ROW, :] = tail[0 : TAIL_ROWS - 1]
    flat[VEC_ROW : VEC_ROW + 1, :] = tail[TAIL_ROWS - 1 : TAIL_ROWS] + vectors[0:1]
    flat[VEC_ROW + 1 : VEC_ROW + VEC_ROWS, :] = vectors[1:VEC_ROWS]
    used = VEC_ROW + VEC_ROWS
    flat[used:, :] = jnp.zeros((flat.shape[0] - used, 128), F32)
    block = block_row(exact)

    sums = jnp.zeros((16, 128), F32)
    for at in range(total_pieces):
        sums = sums + coef[16 * at : 16 * (at + 1), :]
    c = sums[0:1, :] + sums[1:2, :] + sums[2:3, :]
    acc = jnp.zeros((8, 128), F32)
    acc = square_rows(first_rows, 0, PACKED, acc)
    acc = square_rows(mid_rows, 0, VEC_KEPT, acc)
    acc = square_rows(g2, 0, D, acc)
    acc = square_rows(g2, 3 * D, ROWS_OUT, acc)
    acc = square_rows(flat, 0, flat.shape[0], acc)
    squares = total_of(acc) + total_of(jnp.where(lanes((1, BLOCK_PAD)) < 2 * D + CLASSES, block * block, 0.0))
    coef_square = jnp.sum(c * c, 1, keepdims=True)
    norm = jnp.sqrt(squares - coef_square)
    factor = CLIP_AT / jnp.maximum(norm, CLIP_AT)
    scal[...] = jnp.zeros_like(scal)
    for k, value in enumerate((norm, factor, jnp.sqrt(coef_square), exact[0:1, 0:1], c)):
        scal[k : k + 1, :] = jnp.broadcast_to(value, (1, 128))

    block = block - split_dot(
        jnp.broadcast_to(c[:, 0:BASIS], (8, BASIS)), basis[...], NN
    )[0:1, :]
    put_entries(flat, 0, FINAL_AT, block, 2 * D + CLASSES)
    rows = share_grad.shape[0]
    at, shift = place[5], place[6]
    base_row = pl.multiple_of((at // 8) * 8, 8)
    off = at - base_row
    window = flat[pl.ds(base_row, rows + 16), :]
    here = pltpu.roll(window, lax.rem(rows + 16 - off, rows + 16), 0)
    there = pltpu.roll(window, lax.rem(rows + 15 - off, rows + 16), 0)[0:rows]
    here = here[0:rows]
    back = lax.rem(128 - shift, 128)
    g = jnp.where(
        lanes((rows, 128)) < 128 - shift, pltpu.roll(here, back, 1), pltpu.roll(there, back, 1)
    )
    share_grad[...] = g * factor

    row = lax.broadcasted_iota(jnp.int32, (FF, 1), 0)
    sizes = []
    eye = (
        lax.broadcasted_iota(jnp.int32, (D, D), 0) == lax.broadcasted_iota(jnp.int32, (D, D), 1)
    ).astype(F32)
    own = []
    for k in range(2 * LAYERS):
        l, which = divmod(k, 2)
        if which == 0:
            mom_copies[l].wait()
            m = mom[l, pl.ds(start // column_width, FF // column_width), 0:column_width, :]
            m = BETA_ONE * m.reshape(FF, D) + factor * gfull[l, pl.ds(start, FF), :]
            m = jnp.where(row < count, m, 0.0)
            kept = BETA_ONE * wide_mom[l] + factor * own_rows(gfull, l, wide_at, column_width)
            wide_mom_new[l] = kept
        else:
            m = BETA_ONE * mom[l, :, column_width:, :].reshape(FF, D)
            m = m + factor * gfull[l, WIDE:ROWS_OUT, :]
            kept = BETA_ONE * down_mom[l] + factor * own_rows(gfull, l, down_at, row_width)
            down_mom_new[l] = kept
        size = 1.0 / (jnp.sqrt(total_of(m * m)) + SHAPE_EPS)
        high, low = parts(m * size)
        cross = dot(high, low, TN)
        mats[k] = dot(high, high, TN) + (cross + cross.T)
        n = kept.shape[0]
        if n < powers.shape[1]:
            powers[k] = jnp.zeros(powers.shape[1:], F32)
        powers[k, 0:n, :] = kept * size

    def polynomial(k):
        a = parts(mats[k])
        cross = dot(a[0], a[1], NN)
        b = dot(a[0], a[0], NN) + (cross + cross.T)
        return a, 3.4445 * eye - 4.775 * mats[k] + 2.0315 * b

    def step(it, carry):
        polys = [polynomial(k) for k in range(2 * LAYERS)]
        ps = [parts(p) for _, p in polys]
        ts = [parts_dot(p, a, NN) for (a, _), p in zip(polys, ps)]
        for k in range(2 * LAYERS):
            both = parts_dot(parts(jnp.concatenate([ts[k], powers[k]], 0)), ps[k], NN)
            mats[k] = both[0:D]
            powers[k] = both[D:]
        return carry

    lax.fori_loop(0, 4, step, 0)
    side = jnp.where(count == 4 * D, 768.0, jnp.where(count == 3 * D, 576.0, 192.0))
    rate = jnp.sqrt(jnp.full((1, 1), 1.0, F32) * side) * (MUON_RATE * 0.2)
    for k in range(2 * LAYERS):
        l, which = divmod(k, 2)
        _, p = polynomial(k)
        update = parts_dot(parts(powers[k]), parts(p), NN)
        if which == 0:
            new = wide_w[l] - rate * update[0:column_width]
            wide_new[l] = new
            wide_copy[l] = new.astype(BF)
        else:
            new = down_w[l] - (MUON_RATE * 0.2 * FF**0.5) * update[0:row_width]
            down_new[l] = new
            down_copy[l] = new.astype(BF)


def cost(micros):
    return pl.CostEstimate(
        flops=int(micros * 1.15e9), bytes_accessed=int(micros * 1e6), transcendentals=0
    )


def pad_rows(x, rows):
    return jnp.pad(x, (0, rows * 128 - x.shape[0])).reshape(rows, 128)


def pack_shard(wide_t, down):
    rows = jnp.concatenate([wide_t, down], 1)
    rows = rows.reshape(-1, D).astype(BF)
    a_rows, h = half_rows(rows.shape[0])
    head = jnp.pad(rows[:, :128], ((0, a_rows - rows.shape[0]), (0, 0)))
    tail = jnp.pad(rows[:, 128:], ((0, 2 * h - rows.shape[0]), (0, 0)))
    tail = jnp.concatenate([tail[:h], tail[h:]], 1)
    fill = -(a_rows + h) % 16
    return jnp.concatenate([head, tail] + ([jnp.zeros((fill, 128), BF)] if fill else []), 0)


def stage_masks(stages):
    masks = [0]
    for low, width in reversed(stages):
        masks = [a ^ (m << low) for m in range(1 << width) for a in masks]
    return masks


def gather_stages(arrays, stages, devices, apart=2):
    for depth in reversed(range(len(stages))):
        low, width = stages[depth]
        got = [swap(x, m << low, devices) for m in range(1, 1 << width) for x in arrays]
        arrays = arrays + got
        if depth >= apart:
            arrays = [jnp.concatenate(arrays, 0)]
    return arrays


def combine_kernel(spot, middle_keep, middle_got, first_keep, first_got, own, one, two, three):
    mine = spot[0]
    at = 0
    for keep, got in ((middle_keep, middle_got), (first_keep, first_got)):
        n = keep.shape[0] // 4
        for m, out in enumerate((own, one, two, three)):
            rows = pl.ds(pl.multiple_of((mine ^ m) * n, 16), n)
            out[at : at + n, :] = (keep[rows, :] + got[rows, :]).astype(out.dtype)
        at += n


def swap(x, mask, devices):
    return lax.ppermute(x, AXES, [(i, i ^ mask) for i in range(devices)])


def local(
    patches,
    groups,
    labels,
    wide_w,
    down_w,
    plain,
    wide_mom,
    down_mom,
    plain_first,
    plain_second,
    basis_plain,
):
    devices = lax.axis_size(AXES)
    bits = devices.bit_length() - 1
    me = lax.axis_index(AXES).astype(jnp.int32)
    images = patches.shape[0]
    share = plain.shape[0]
    column_width = wide_w.shape[2]
    row_width = down_w.shape[1]
    vmem = pl.BlockSpec(memory_space=pltpu.VMEM)
    smem = pl.BlockSpec(memory_space=pltpu.SMEM)
    params = pltpu.CompilerParams(vmem_limit_bytes=VMEM_LIMIT)
    S = jax.ShapeDtypeStruct

    number_of = [(0, 1), (1, 2), (3, 2)]
    stages = number_of + ([(5, 2), (7, 1)] if bits == 8 else [(b, 1) for b in range(5, bits)])

    wide_t = jnp.transpose(wide_w, (0, 2, 1))
    plain_rows = -(-(share + 127) // 2048) * 16
    rows = plain_rows
    plain_block = pad_rows(plain, plain_rows)
    high = lax.reduce_precision(plain_block, 8, 7)
    low_half = (plain_block - high).astype(BF)
    weights_one = pack_shard(wide_t[:1], down_w[:1])
    shard_one = jnp.concatenate([high.astype(BF), weights_one, low_half], 0)
    shard_two = pack_shard(wide_t[1:], down_w[1:])
    weight_rows = weights_one.shape[0]

    one = gather_stages([shard_one[None]], stages[2:], devices, 0)[0]
    two = gather_stages([shard_two[None]], stages[2:], devices, 0)
    first_masks = stage_masks(stages[2:])
    top = 3 * devices // 4
    compact = bits == 5 and top * share <= CLS_AT
    body = rows + weight_rows
    if compact:
        low_top = lax.dynamic_index_in_dim(one[:, body:], (me >> 3) ^ 3, 0, keepdims=False)
        one = jnp.concatenate([one[:, :body].reshape(-1, 128), low_top], 0)
    else:
        one = one.reshape(-1, 128)
    one = gather_stages([one[None]], stages[1:2], devices)
    one[0] = one[0] + 0.0 * jnp.max(two[0][:, 0, 0])
    pieces_one = gather_stages([jnp.concatenate(one, 0)], stages[:1], devices)
    two = gather_stages(two, stages[1:2], devices)
    places = (first_masks, stage_masks(stages[:2]), top if compact else None)

    lead = jnp.clip(FINAL_AT - me * share + BLOCK_PAD, 0, share + BLOCK_PAD)
    basis_block = lax.dynamic_slice(
        jnp.pad(basis_plain, ((0, 0), (BLOCK_PAD, BLOCK_PAD))), (0, lead), (BASIS, BLOCK_PAD)
    )

    number = me[None]
    groups = groups.astype(jnp.int32)
    labels = labels.astype(jnp.int32)
    flat_rows = -(-((devices - 1) * share // 128 + rows + 8) // 8) * 8
    n = images * TQ
    saved = [
        S((n, D), F32),
        S((n, D), BF),
        S((images, TK, D), BF),
        S((images, TK, D), BF),
        S((images, HEADS, TQ, TK), BF),
        S((n, D), BF),
        S((n, FF), BF),
        S((n, FF), BF),
    ]
    rows_spec = pl.BlockSpec((TQ, D), lambda i: (i, 0))
    wide_spec = pl.BlockSpec((TQ, FF), lambda i: (i, 0))
    key_spec = pl.BlockSpec((1, TK, D), lambda i: (i, 0, 0))
    patch_spec = pl.BlockSpec((1, PATCHES, PATCH_DIM), lambda i: (i, 0, 0))
    saved_specs = [
        rows_spec,
        rows_spec,
        key_spec,
        key_spec,
        pl.BlockSpec((1, HEADS, TQ, TK), lambda i: (i, 0, 0, 0)),
        rows_spec,
        wide_spec,
        wide_spec,
    ]
    factor_rows = EXACT_ROWS + -(-FACTOR_BLOCKS * images // 8) * 8
    x0, *saved0, x1, gains0, wt0, dn0, flat = pl.pallas_call(
        functools.partial(
            start_kernel, devices, share, column_width, row_width, places, len(pieces_one)
        ),
        grid=(images,),
        out_shape=[S((n, D), F32)]
        + saved
        + [
            S((n, D), F32),
            S((8, D), F32),
            S((1, WIDE, D), BF),
            S((1, FF, D), BF),
            S((flat_rows, 128), F32),
        ],
        in_specs=[smem] * 2 + [vmem] * len(pieces_one) + [patch_spec],
        out_specs=[rows_spec] + saved_specs + [rows_spec] + [vmem] * 4,
        scratch_shapes=[
            pltpu.VMEM((devices, rows, 128), F32),
            pltpu.VMEM((devices, weight_rows, 128), BF),
            pltpu.VMEM((ROWS_OUT, D), F32),
            pltpu.VMEM((4, rows + 8, 128), F32),
            pltpu.VMEM((2, PATCH_DIM, 128), F32),
            pltpu.VMEM((2, TQ, 128), F32),
            pltpu.VMEM((PATCH_DIM, D), BF),
        ],
        compiler_params=params,
        cost_estimate=cost(20),
        name="start",
    )(groups, number, *pieces_one, patches)

    two, x1 = lax.optimization_barrier((two, x1))
    pieces_two = gather_stages(two, stages[:1], devices)
    *saved1, gains1, gstream, kv, factors, small, wt12, dn12 = pl.pallas_call(
        functools.partial(
            forward_kernel,
            float(images * devices),
            images,
            column_width,
            row_width,
            stage_masks(stages),
            len(pieces_two),
        ),
        grid=(images,),
        out_shape=saved
        + [
            S((8, D), F32),
            S((n, D), F32),
            S((3 * D, 128), F32),
            S((factor_rows, 128), F32),
            S((16, CLASSES_PAD), F32),
            S((2, WIDE, D), BF),
            S((2, FF, D), BF),
        ],
        in_specs=[smem] * 3 + [vmem, rows_spec] + [vmem] * len(pieces_two),
        out_specs=saved_specs + [vmem] * 7,
        scratch_shapes=[
            pltpu.VMEM((devices, shard_two.shape[0], 128), BF),
            pltpu.VMEM((ROWS_OUT, D), F32),
            pltpu.VMEM((8, D, 128), F32),
            pltpu.VMEM((n, D), F32),
            pltpu.VMEM((images, TK, D), BF),
            pltpu.VMEM((images, TK, D), BF),
            pltpu.VMEM((n, D), BF),
            pltpu.VMEM((n, D), BF),
        ]
        + [pltpu.VMEM((16, D), F32)] * 6
        + [pltpu.VMEM((n, D), BF)],
        compiler_params=params,
        cost_estimate=cost(30),
        name="forward",
    )(groups, labels, number, flat, x1, *pieces_two)

    mom_shard = jnp.concatenate([jnp.transpose(wide_mom, (0, 2, 1)), down_mom], 1)
    mom_all = lax.all_gather(mom_shard, AXES, axis=0)
    factors, mom_all = lax.optimization_barrier((factors, mom_all))
    gstream, factors = lax.optimization_barrier((gstream, factors))
    factors_all = lax.all_gather(factors, AXES, axis=0)
    back_scratch = [
        pltpu.VMEM((n, D), BF),
        pltpu.VMEM((n, FF), BF),
        pltpu.VMEM((n, D), BF),
        pltpu.VMEM((n, D), BF),
        pltpu.VMEM((n, D), BF),
        pltpu.VMEM((n, D), BF),
        pltpu.VMEM((n, D), BF),
        pltpu.VMEM((n, D), BF),
        pltpu.VMEM((n, D), BF),
        pltpu.VMEM((n, FF), BF),
    ]
    gstream1, middle_keep, middle_send = pl.pallas_call(
        functools.partial(middle_kernel, images),
        out_shape=[
            S((n, D), F32),
            S((MIDDLE_ROWS // 2, 128), F32),
            S((MIDDLE_ROWS // 2, 128), F32),
        ],
        grid=(images,),
        in_specs=[smem] * 2 + [rows_spec] + saved_specs + [vmem, rows_spec] + [vmem] * 4,
        out_specs=[rows_spec] + [vmem] * 2,
        scratch_shapes=[
            pltpu.VMEM((8, D), F32),
            pltpu.VMEM((8, FF), F32),
            pltpu.VMEM((MIDDLE_ROWS, 128), F32),
        ]
        + back_scratch,
        compiler_params=params,
        cost_estimate=cost(23),
        name="middle",
    )(groups, number, x1, *saved1, gains1, gstream, wt12, dn12, kv, small)

    first_keep, first_send = pl.pallas_call(
        functools.partial(first_kernel, images),
        out_shape=[S((FIRST_ROWS // 2, 128), F32)] * 2,
        grid=(images,),
        in_specs=[smem] * 2
        + [rows_spec]
        + saved_specs
        + [vmem, rows_spec]
        + [vmem] * 2
        + [patch_spec],
        out_specs=[vmem] * 2,
        scratch_shapes=[
            pltpu.VMEM((FIRST_ROWS, 128), F32),
            pltpu.VMEM((TQ, D), F32),
            pltpu.VMEM((8, D), F32),
            pltpu.VMEM((8, FF), F32),
            pltpu.VMEM((2, PATCH_DIM, 128), F32),
            pltpu.VMEM((2, TQ + 16, 128), F32),
        ]
        + back_scratch,
        compiler_params=params,
        cost_estimate=cost(25),
        name="first",
    )(groups, number, x0, *saved0, gains0, gstream1, wt0, dn0, patches)

    late_params = pltpu.CompilerParams(
        vmem_limit_bytes=12 * 1024 * 1024 + 1024 * devices * factor_rows
    )
    exact, extra = pl.pallas_call(
        functools.partial(coefficient_kernel, devices),
        grid=(1,),
        out_shape=[S((EXACT_ROWS, 128), F32), S((16, 128), F32)],
        in_specs=[pl.BlockSpec((devices, EXACT_ROWS, 128), lambda i: (0, 0, 0)), vmem],
        out_specs=[vmem] * 2,
        compiler_params=late_params,
        cost_estimate=cost(2),
        name="coefficients",
    )(factors_all, basis_block)

    g2, headflat = pl.pallas_call(
        functools.partial(late_kernel, devices, images),
        out_shape=[S((ROWS_OUT, D), F32), S((HEAD_ROWS + 4, 128), F32)],
        in_specs=[vmem],
        out_specs=[vmem] * 2,
        scratch_shapes=[pltpu.VMEM((8, D, 128), F32)],
        compiler_params=late_params,
        cost_estimate=cost(4),
        name="late",
    )(factors_all.reshape(devices * factor_rows, 128))

    split_bits = 5
    for bit in range(split_bits, bits):
        extra = extra + swap(extra, 1 << bit, devices)
    if bits > split_bits:
        c = extra[0] + extra[1] + extra[2]
        split = []
        for k in range(3):
            split.append(lax.reduce_precision(c, 8, 7))
            c = c - split[-1]
        extra = jnp.concatenate([jnp.stack(split), extra[3:]], 0)
    quarter = (MIDDLE_ROWS + FIRST_ROWS) // 8
    small_params = pltpu.CompilerParams(vmem_limit_bytes=16 * 1024 * 1024)
    total, *sends = pl.pallas_call(
        combine_kernel,
        out_shape=[S((quarter, 128), F32)] + [S((quarter, 128), BF)] * 3,
        in_specs=[smem] + [vmem] * 4,
        out_specs=[vmem] * 4,
        compiler_params=small_params,
        cost_estimate=cost(2),
        name="combine",
    )(
        ((me >> 1) & 3)[None],
        middle_keep,
        swap(middle_send, 1, devices),
        first_keep,
        swap(first_send, 1, devices),
    )
    for m in range(1, 4):
        total = total + swap(sends[m - 1], m << 1, devices).astype(F32)
    mr, fr = MIDDLE_ROWS // 8, FIRST_ROWS // 8
    kept = jnp.concatenate(
        [total[:mr].reshape(4, mr // 4, 128), total[mr:].reshape(4, fr // 4, 128)], 1
    )
    mine = (me >> 3) & 3
    total = lax.dynamic_index_in_dim(kept, mine, 0, keepdims=False)
    for m in range(1, 4):
        send = lax.dynamic_index_in_dim(kept, mine ^ m, 0, keepdims=False)
        if m == 3:
            send = send + 0.0 * extra[0, 0]
        total = total + swap(send.astype(BF), m << 3, devices).astype(F32)
    kept = total
    for bit in range(split_bits, bits):
        small_part = kept.astype(BF)
        kept = small_part.astype(F32) + swap(small_part, 1 << bit, devices).astype(F32)
    piece = jnp.concatenate([kept, extra], 0).astype(BF)[None]
    piece = gather_stages([piece], number_of[2:], devices, 0)[0]
    pieces = [piece] + [swap(piece, m << 1, devices) for m in range(1, 3)]
    pieces = pieces + [swap(piece + (0.0 * g2[0, 0]).astype(BF), 3 << 1, devices)]
    pieces = pieces + [swap(p, 1, devices) for p in pieces]

    first_column = me * column_width
    in_q = first_column < 3 * D
    in_o = first_column < 4 * D
    start = jnp.where(in_q, 0, jnp.where(in_o, 3 * D, 4 * D))
    count = jnp.where(in_q, 3 * D, jnp.where(in_o, D, FF))
    piece_number = ((me & 1) << 4) | (((me >> 1) & 3) << 2) | ((me >> 3) & 3)
    at = me * share
    spots = jnp.stack(
        [start, count, first_column, WIDE + me * row_width, piece_number, at // 128, at % 128]
    )
    wide_shape = (LAYERS, column_width, D)
    down_shape = (LAYERS, row_width, D)
    flat_rows = -(-((devices - 1) * share // 128 + rows + 24) // 8) * 8
    (
        wide_new,
        wide_mom_new,
        wide_copy,
        down_new,
        down_mom_new,
        down_copy,
        share_grad,
        scal,
    ) = pl.pallas_call(
        functools.partial(muon_kernel, column_width, row_width, len(pieces)),
        out_shape=[
            S(wide_shape, F32),
            S(wide_shape, F32),
            S(wide_shape, BF),
            S(down_shape, F32),
            S(down_shape, F32),
            S(down_shape, BF),
            S((rows, 128), F32),
            S((8, 128), F32),
        ],
        in_specs=[smem]
        + [vmem] * (len(pieces) + 4)
        + [pl.BlockSpec(memory_space=pltpu.HBM)]
        + [vmem] * 4,
        out_specs=[vmem] * 8,
        scratch_shapes=[
            pltpu.VMEM((flat_rows, 128), F32),
            pltpu.VMEM((MIDDLE_ROWS, 128), BF),
            pltpu.VMEM((FIRST_ROWS, 128), BF),
            pltpu.VMEM((16 * 32, 128), F32),
            pltpu.VMEM((LAYERS, ROWS_OUT + 16, D), F32),
            pltpu.VMEM((2 * LAYERS, D, D), F32),
            pltpu.VMEM((2 * LAYERS, -(-max(column_width, row_width) // 8) * 8, D), F32),
            pltpu.VMEM((LAYERS, devices, column_width + row_width, D), F32),
            pltpu.SemaphoreType.DMA((LAYERS,)),
        ],
        compiler_params=pltpu.CompilerParams(vmem_limit_bytes=48 * 1024 * 1024),
        cost_estimate=cost(20),
        name="muon",
    )(
        spots.astype(jnp.int32),
        *pieces,
        g2,
        headflat,
        exact,
        basis_block,
        mom_all,
        wide_t,
        jnp.transpose(wide_mom, (0, 2, 1)),
        down_w,
        down_mom,
    )
    grad_norm, _, removed_norm, loss_sum = [scal[k, 0] for k in range(4)]
    clipped = share_grad.reshape(-1)[:share]
    first_new = BETA_ONE * plain_first + (1.0 - BETA_ONE) * clipped
    second_new = BETA_TWO * plain_second + (1.0 - BETA_TWO) * clipped * clipped
    first_hat = first_new / (1.0 - BETA_ONE**STEP)
    second_hat = second_new / (1.0 - BETA_TWO**STEP)
    plain_new = plain - ADAM_RATE * (
        first_hat / (jnp.sqrt(second_hat) + ADAM_EPS) + DECAY_RATE * plain
    )
    plain_copy = plain_new.astype(BF)
    return (
        loss_sum,
        removed_norm,
        grad_norm,
        *[jnp.transpose(x, (0, 2, 1)) for x in (wide_new, wide_mom_new, wide_copy)],
        down_new,
        down_mom_new,
        down_copy,
        plain_new,
        first_new,
        second_new,
        plain_copy,
    )


def solution(mesh):
    placed = (
        P(AXES, None, None),
        P(AXES),
        P(AXES),
        P(None, None, AXES),
        P(None, AXES, None),
        P(AXES),
        P(None, None, AXES),
        P(None, AXES, None),
        P(AXES),
        P(AXES),
        P(None, AXES),
    )
    return jax.shard_map(
        local,
        mesh=mesh,
        in_specs=placed,
        out_specs=(
            P(),
            P(),
            P(),
            P(None, None, AXES),
            P(None, None, AXES),
            P(None, None, AXES),
            P(None, AXES, None),
            P(None, AXES, None),
            P(None, AXES, None),
            P(AXES),
            P(AXES),
            P(AXES),
            P(AXES),
        ),
        check_vma=False,
    )
```

```python
import functools
import math

import jax
import jax.numpy as jnp
from jax import lax
from jax.experimental import pallas as pl
from jax.experimental.pallas import tpu as pltpu
from jax.sharding import PartitionSpec as P

D = 192
HEADS = 3
HD = 64
FF = 768
PATCH_DIM = 768
CLASSES = 1000
CLASSES_PAD = 1024
LAYERS = 3
SEQ = 325
PATCHES = SEQ - 1
LEN_MID = 197
LEN_SHORT = 101
BASIS = 64
STEP = 10
WIDE = 1536
ROWS_OUT = WIDE + FF

HEAD_AT = PATCH_DIM * D
CLS_AT = HEAD_AT + D * CLASSES
PATCH_B_AT = CLS_AT + D
POS_AT = PATCH_B_AT + D
VEC_AT = POS_AT + SEQ * D
VEC_LAYER = 6 * D + FF
FINAL_AT = VEC_AT + LAYERS * VEC_LAYER
HEAD_B_AT = FINAL_AT + 2 * D
USED = HEAD_B_AT + CLASSES
HEAD_ROWS = D * CLASSES // 128
HEAD_ROOM = 256
HEAD_FLAT_ROOM = 2000
BLOCK_PAD = 2 * D + CLASSES_PAD
PATCH_ROWS = HEAD_AT // 128
TAIL_ROW = CLS_AT // 128
VEC_ROW = (VEC_AT + VEC_LAYER) // 128
TAIL_ROWS = VEC_ROW + 1 - TAIL_ROW
VEC_ROWS = FINAL_AT // 128 + 1 - VEC_ROW

PACKED = ROWS_OUT * 3 // 2
MIDDLE_ROWS = 4096
FIRST_ROWS = 5120
VEC_KEPT = PACKED + 3 * D

TQ = 336
TK = 384
CLS_ROW = 0
PATCH_AT = 8
SIZES = ((112, 128), (208, 256), (336, 384))

NORM_EPS = 1e-06
CLIP_AT = 0.02
MUON_RATE = 0.3
ADAM_RATE = 0.05
BETA_ONE = 0.5
BETA_TWO = 0.95
DECAY_RATE = 0.01
ADAM_EPS = 1e-08
SHAPE_EPS = 1e-07
MASKED = -1e30
GELU_C = math.sqrt(2.0 / math.pi)
GELU_K = 0.044715

F32 = jnp.float32
BF = jnp.bfloat16
AXES = ("dp", "fsdp")
NN = (((1,), (0,)), ((), ()))
NT = (((1,), (1,)), ((), ()))
TN = (((0,), (0,)), ((), ()))
VMEM_LIMIT = 60 * 1024 * 1024


def dot(a, b, how):
    return lax.dot_general(a, b, how, preferred_element_type=F32)


def lanes(shape):
    return lax.broadcasted_iota(jnp.int32, shape, len(shape) - 1)


def head_mask(h):
    lane = lanes((1, D))
    return jnp.where((lane >= h * HD) & (lane < (h + 1) * HD), 1.0, 0.0)


def norm_stats(x):
    mean = jnp.mean(x, -1, keepdims=True)
    centered = x - mean
    var = jnp.mean(centered * centered, -1, keepdims=True)
    rstd = lax.rsqrt(var + NORM_EPS)
    return centered * rstd, rstd


def norm_back(dn, xhat, rstd, gain):
    scaled = dn * gain
    m1 = jnp.mean(scaled, -1, keepdims=True)
    m2 = jnp.mean(scaled * xhat, -1, keepdims=True)
    return rstd * (scaled - m1 - xhat * m2)


def colsum(x):
    return jnp.sum(x, 0, keepdims=True)


def key_mask(length, keys):
    key = lanes((1, keys))
    return ((key >= PATCH_AT) & (key < PATCH_AT + length - 1)) | (key == CLS_ROW)


def by_size(group, body):
    pl.when(group == 0)(lambda: body(*SIZES[0]))
    pl.when(group == 1)(lambda: body(*SIZES[1]))
    pl.when((group != 0) & (group != 1))(lambda: body(*SIZES[2]))


def softmax_rows(scores):
    top = jnp.max(scores, -1, keepdims=True)
    e = jnp.exp(scores - top)
    return e / jnp.sum(e, -1, keepdims=True)


def merge(a, b, shift):
    if shift == 0:
        return a
    lane = lanes(a.shape)
    return jnp.where(
        lane < 128 - shift, pltpu.roll(a, 128 - shift, 1), pltpu.roll(b, 128 - shift, 1)
    )


def flat_vec(flat, at, n):
    blocks = []
    for j in range(-(-n // 128)):
        q, r = divmod(at + 128 * j, 128)
        blocks.append(merge(flat[q : q + 1, :], flat[q + 1 : q + 2, :], r))
    row = blocks[0] if len(blocks) == 1 else jnp.concatenate(blocks, 1)
    return row[:, :n]


def unpack_flat(blocks, flat, tmp, devices, share):
    rows = blocks.shape[1]
    lane = lanes((rows, 128))
    for d in range(devices):
        q, r = divmod(d * share, 128)
        block = blocks[d]
        if r == 0:
            flat[q : q + rows, :] = block
            continue
        slot = d % 4
        tmp[slot, 8 : 8 + rows, :] = pltpu.roll(block, r, 1)
        tmp[slot, 7:8, :] = flat[q : q + 1, :]
        flat[q : q + rows, :] = jnp.where(
            lane >= r, tmp[slot, 8 : 8 + rows, :], tmp[slot, 7 : 7 + rows, :]
        )


def unpack_pairs(flat, row, pairs, out, out_at):
    a = flat[pl.ds(row, pairs, stride=3), :]
    b = flat[pl.ds(row + 1, pairs, stride=3), :]
    c = flat[pl.ds(row + 2, pairs, stride=3), :]
    out[0, pl.ds(out_at, pairs, stride=2), :] = a
    out[1, pl.ds(out_at, pairs, stride=2), :] = b
    out[0, pl.ds(out_at + 1, pairs, stride=2), :] = merge(b, c, 64)
    out[1, pl.ds(out_at + 1, pairs, stride=2), :] = pltpu.roll(c, 64, 1)


def rows192(ref, at, n):
    return jnp.concatenate([ref[0, at : at + n, :], ref[1, at : at + n, 0:64]], 1)


def pack_pairs(src, src_at, flat, row, pairs):
    a = src[0, pl.ds(src_at, pairs, stride=2), :]
    b = src[1, pl.ds(src_at, pairs, stride=2), :]
    c = src[0, pl.ds(src_at + 1, pairs, stride=2), :]
    e = src[1, pl.ds(src_at + 1, pairs, stride=2), :]
    lane = lanes(a.shape)
    c = pltpu.roll(c, 64, 1)
    flat[pl.ds(row, pairs, stride=3), :] = a
    flat[pl.ds(row + 1, pairs, stride=3), :] = jnp.where(lane < 64, b, c)
    flat[pl.ds(row + 2, pairs, stride=3), :] = jnp.where(lane < 64, c, pltpu.roll(e, 64, 1))


def unpack_head(flat, out):
    lane = lanes((12, 128))
    for rho in range(16):
        for k in range(8):
            q, r = divmod(1000 * rho + 128 * k, 128)
            a = flat[pl.ds(HEAD_AT // 128 + q, 12, stride=125), :]
            b = flat[pl.ds(HEAD_AT // 128 + q + 1, 12, stride=125), :]
            block = merge(a, b, r)
            if k == 7:
                block = jnp.where(lane < CLASSES - 896, block, 0.0)
            out[k, pl.ds(rho, 12, stride=16), :] = block


def pack_head(src, out):
    lane = lanes((12, 128))
    for j in range(125):
        rho, c = divmod(128 * j, 1000)
        k, s = divmod(c, 128)
        a = src[k, pl.ds(rho, 12, stride=16), :]
        if s:
            b = a
            if k < 7:
                b = src[k + 1, pl.ds(rho, 12, stride=16), :]
            a = merge(a, b, s)
        left = 1000 - c
        if left < 128:
            nxt = src[0, pl.ds(rho + 1, 12, stride=16), :]
            a = jnp.where(lane < left, a, pltpu.roll(nxt, left, 1))
        out[pl.ds(j, 12, stride=125), :] = a


FACTOR_FLOW = 24
FACTOR_DLOGITS = 26
FACTOR_BLOCKS = 34
EXACT = 13
EXACT_ROWS = 16


def put_factor(ref, block, value, images):
    for k in range(-(-value.shape[1] // 128)):
        part = value[0:images, 128 * k : 128 * (k + 1)].astype(F32)
        at = EXACT_ROWS + (block + k) * images
        ref[at : at + images, 0 : part.shape[1]] = part


def put_entries(ref, shift_rows, at, row, n):
    lane = lanes((1, 128))
    done = 0
    while done < n:
        q, r = divmod(at + done, 128)
        q = q + shift_rows
        take = min(128 - r, n - done)
        block, off = divmod(done, 128)
        piece = row[:, 128 * block : 128 * (block + 1)]
        if off + take > 128:
            piece = merge(piece, row[:, 128 * (block + 1) : 128 * (block + 2)], off)
            off = 0
        shift = (r - off) % 128
        if shift:
            piece = pltpu.roll(piece, shift, 1)
        if take < 128:
            piece = jnp.where((lane >= r) & (lane < r + take), piece, ref[q : q + 1, :])
        ref[q : q + 1, :] = piece
        done += take


def image_rows(i):
    if isinstance(i, int):
        return pl.ds(i * TQ, TQ)
    return pl.ds(pl.multiple_of(i * TQ, 16), TQ)


def length_of(group):
    return jnp.where(group == 0, LEN_SHORT, jnp.where(group == 1, LEN_MID, SEQ))


def layer_vectors(flat, l):
    at = VEC_AT + l * VEC_LAYER
    six = [flat_vec(flat, at + k * D, D) for k in range(6)]
    return six, flat_vec(flat, at + 6 * D, FF)


def store_layer_grads(ref, parts):
    tails = []
    for at, g in parts:
        ref[at : at + g.shape[0], :] = g[:, 0:128]
        tails.append((at, g))
    half = ROWS_OUT // 2
    for at, g in tails:
        n = g.shape[0]
        low = max(0, min(n, half - at))
        if low > 0:
            ref[ROWS_OUT + at : ROWS_OUT + at + low, 0:64] = g[:low, 128:192]
        if low < n:
            start = at + low - half
            ref[ROWS_OUT + start : ROWS_OUT + start + n - low, 64:128] = g[low:, 128:192]


def half_rows(rows):
    return -(-rows // 8) * 8, -(-rows // 16) * 8


def unpack_weights(blocks, layers, column_width, row_width, asm, wt, dn):
    devices = blocks.shape[0]
    per_layer = column_width + row_width
    a_rows, h = half_rows(layers * per_layer)
    for l in range(layers):
        for d in range(devices):
            block = blocks[d].astype(F32)
            for at, n, to in (
                (l * per_layer, column_width, d * column_width),
                (l * per_layer + column_width, row_width, WIDE + d * row_width),
            ):
                asm[to : to + n, 0:128] = block[at : at + n]
                low = max(0, min(n, h - at))
                if low:
                    asm[to : to + low, 128:192] = block[a_rows + at : a_rows + at + low, 0:64]
                if low < n:
                    start = a_rows + at + low - h
                    asm[to + low : to + n, 128:192] = block[start : start + n - low, 64:128]
        wt[l] = asm[0:WIDE, :].astype(BF)
        dn[l] = asm[WIDE:ROWS_OUT, :].astype(BF)


def layer_forward(l, group, flat, wt, dn, gains, xin, xout, saved):
    mid, qs, ks, vs, probs, mixs, acts, gps = saved
    masks = [head_mask(h).astype(BF) for h in range(HEADS)]
    (gain1, shift1, out_bias, gain2, shift2, down_bias), up_bias = layer_vectors(flat, l)
    for k, value in enumerate((gain1, shift1, gain2, shift2)):
        gains[k : k + 1, :] = value

    def body(tq, tk):
        x = xin[0:tq, :]
        xhat, _ = norm_stats(x)
        n1 = (xhat * gain1 + shift1).astype(BF)
        q = (dot(n1, wt[0, 0:D, :], NT) * HD ** (-0.5)).astype(BF)
        k = dot(n1, wt[0, D : 2 * D, :], NT).astype(BF)
        v = dot(n1, wt[0, 2 * D : 3 * D, :], NT).astype(BF)
        qs[0:tq, :] = q
        ks[0, 0:tq, :] = k
        vs[0, 0:tq, :] = v
        ks[0, tq:tk, :] = jnp.zeros((tk - tq, D), BF)
        vs[0, tq:tk, :] = jnp.zeros((tk - tq, D), BF)
        valid = key_mask(length_of(group), tk)
        kk = ks[0, 0:tk, :]
        vv = vs[0, 0:tk, :]
        mix = None
        for h in range(HEADS):
            s = dot(q * masks[h], kk, NT)
            s = jnp.where(valid, s, MASKED)
            p = softmax_rows(s)
            p = p.astype(BF)
            probs[0, h, 0:tq, 0:tk] = p
            part = dot(p, vv * masks[h], NN)
            mix = part if mix is None else mix + part
        mix = mix.astype(BF)
        mixs[0:tq, :] = mix
        middle = x + dot(mix, wt[0, 3 * D : 4 * D, :], NT) + out_bias
        mid[0:tq, :] = middle
        xhat2, _ = norm_stats(middle)
        n2 = (xhat2 * gain2 + shift2).astype(BF)
        up = dot(n2, wt[0, 4 * D : WIDE, :], NT) + up_bias
        t = jnp.tanh(GELU_C * (up + GELU_K * (up * up * up)))
        half = 0.5 * (1.0 + t)
        act = (up * half).astype(BF)
        slope = half + 0.5 * up * (1.0 - t * t) * (GELU_C * (1.0 + 3.0 * GELU_K * (up * up)))
        gps[0:tq, :] = slope.astype(BF)
        acts[0:tq, :] = act
        xout[0:tq, :] = middle + dot(act, dn[0], NN) + down_bias
        if tq < TQ:
            xout[tq:TQ, :] = jnp.zeros((TQ - tq, D), F32)

    by_size(group, body)


def start_kernel(devices, share, column_width, row_width, places, n_pieces, groups, me, *refs):
    pieces, patches = refs[:n_pieces], refs[n_pieces]
    x0, mid, qs, ks, vs, probs, mixs, acts, gps, x1, gains, wt, dn, flat = refs[
        n_pieces + 1 : n_pieces + 15
    ]
    blocks, weights, asm, tmp, pw, pos, emb = refs[n_pieces + 15 :]
    image = pl.program_id(0)
    pl.when(image == 0)(
        lambda: unpack_start(
            devices, share, column_width, row_width, places, me[0], pieces, wt, dn, flat, blocks, weights,
            asm, tmp, pw, pos, emb,
        )
    )
    cls = flat_vec(flat, CLS_AT, D)
    patch_b = flat_vec(flat, PATCH_B_AT, D)
    e = dot(patches[0], emb[...], NN) + patch_b + rows192(pos, 8, PATCHES)
    x0[0:PATCH_AT, :] = jnp.concatenate(
        [cls + rows192(pos, 7, 1), jnp.zeros((PATCH_AT - 1, D), F32)], 0
    )
    x0[PATCH_AT : PATCH_AT + PATCHES, :] = e
    x0[PATCH_AT + PATCHES :, :] = jnp.zeros((TQ - PATCH_AT - PATCHES, D), F32)
    layer_forward(
        0, groups[image], flat, wt, dn, gains, x0, x1, (mid, qs, ks, vs, probs, mixs, acts, gps)
    )


def unpack_start(
    devices, share, column_width, row_width, places, me, pieces, wt, dn, flat, blocks, weights, asm, tmp,
    pw, pos, emb,
):
    inner_masks, outer_masks, top = places
    rows, weight_rows = blocks.shape[1], weights.shape[1]
    body = rows + weight_rows
    step = body if top is not None else body + rows
    for k, outer in enumerate(outer_masks):
        piece = pieces[k // pieces[0].shape[0]].at[k % pieces[0].shape[0]]
        for j, inner in enumerate(inner_masks):
            d = me ^ (outer | inner)
            at = j * step
            value = piece[at : at + rows, :].astype(F32)
            if top is None:
                value = value + piece[at + body : at + body + rows, :].astype(F32)
            blocks[d] = value
            weights[d] = piece[at + rows : at + body, :]
        if top is not None:
            d = top | ((me ^ outer) & 7)
            at = len(inner_masks) * step
            blocks[d] = blocks[d] + piece[at : at + rows, :].astype(F32)
    unpack_flat(blocks, flat, tmp, devices, share)
    unpack_weights(weights, 1, column_width, row_width, asm, wt, dn)
    unpack_pairs(flat, 0, PATCH_DIM // 2, pw, 0)
    unpack_pairs(flat, POS_AT // 128, SEQ // 2, pos, 7)
    last = flat_vec(flat, POS_AT + (SEQ - 1) * D, D)
    pos[0, 7 + SEQ - 1 : 7 + SEQ, :] = last[:, 0:128]
    pos[1, 7 + SEQ - 1 : 7 + SEQ, 0:64] = last[:, 128:192]
    emb[...] = rows192(pw, 0, PATCH_DIM).astype(BF)


def forward_kernel(
    total_images, images, column_width, row_width, masks, n_pieces, groups, labels, me, flat, x1, *refs
):
    pieces = refs[:n_pieces]
    mid, qs, ks, vs, probs, mixs, acts, gps, gains, *rest = refs[n_pieces:]
    gstream, kv, factors, small, wt_all, dn_all, weights, asm, hw, x2 = rest[:10]
    image = pl.program_id(0)

    @pl.when(image == 0)
    def _():
        inner = pieces[0].shape[0]
        for k in range(n_pieces):
            for j in range(inner):
                weights[me[0] ^ masks[k * inner + j]] = pieces[k][j]
        unpack_weights(weights, 2, column_width, row_width, asm, wt_all, dn_all)
        unpack_head(flat, hw)
        factors[...] = jnp.zeros_like(factors)

    layer_forward(
        1,
        groups[image],
        flat,
        wt_all,
        dn_all,
        gains,
        x1,
        x2.at[image_rows(image)],
        (mid, qs, ks, vs, probs, mixs, acts, gps),
    )
    pl.when(image == images - 1)(
        lambda: last_layer(
            total_images, images, groups, labels, flat, gstream, kv, factors, small, wt_all.at[1],
            dn_all.at[1], hw, x2, *rest[10:],
        )
    )


def last_layer(
    total_images, images, groups, labels, flat, gstream, kv, factors, small, wt, dn, hw, x2, kbuf, vbuf,
    dkbuf, dvbuf, clsbuf, qcls, mixcls, dmixcls, dqcls, midgrad, n1low,
):
    l = 2
    (gain1, shift1, out_bias, gain2, shift2, down_bias), up_bias = layer_vectors(flat, l)
    wk = wt[D : 2 * D, :]
    wv = wt[2 * D : 3 * D, :]
    clsbuf[...] = jnp.zeros_like(clsbuf)
    mixcls[...] = jnp.zeros_like(mixcls)
    kbuf[:, TQ:TK, :] = jnp.zeros((images, TK - TQ, D), BF)
    vbuf[:, TQ:TK, :] = jnp.zeros((images, TK - TQ, D), BF)

    def keys(i, carry):
        rows = image_rows(i)
        xhat, _ = norm_stats(x2[rows, :])
        n1 = (xhat * gain1 + shift1).astype(BF)
        kbuf[i, 0:TQ, :] = dot(n1, wk, NT).astype(BF)
        vbuf[i, 0:TQ, :] = dot(n1, wv, NT).astype(BF)
        clsbuf[pl.ds(i, 1), :] = x2[pl.ds(i * TQ + CLS_ROW, 1), :]
        return carry

    for i in range(images):
        keys(i, 0)
    xc = clsbuf[...]
    xhat1c, rstd1c = norm_stats(xc)
    n1c = (xhat1c * gain1 + shift1).astype(BF)
    qc = (dot(n1c, wt[0:D, :], NT) * HD ** (-0.5)).astype(BF)
    qcls[...] = qc.astype(F32)
    mask3 = jnp.concatenate([head_mask(h) for h in range(HEADS)] + [jnp.zeros((13, D), F32)], 0)

    def cls_probs(i):
        q3 = (qcls[pl.ds(i, 1), :] * mask3).astype(BF)
        s = dot(q3, kbuf[i], NT)
        s = jnp.where(key_mask(length_of(groups[i]), TK), s, MASKED)
        return q3, softmax_rows(s)

    def attend(i, carry):
        q3, p = cls_probs(i)
        m = dot(p.astype(BF), vbuf[i], NN)
        mixcls[pl.ds(i, 1), :] = colsum(m * mask3)
        return carry

    for i in range(images):
        attend(i, 0)
    mixc = mixcls[...].astype(BF)
    midc = xc + dot(mixc, wt[3 * D : 4 * D, :], NT) + out_bias
    xhat2c, rstd2c = norm_stats(midc)
    n2c = (xhat2c * gain2 + shift2).astype(BF)
    upc = dot(n2c, wt[4 * D : WIDE, :], NT) + up_bias
    tc = jnp.tanh(GELU_C * (upc + GELU_K * (upc * upc * upc)))
    halfc = 0.5 * (1.0 + tc)
    actc = (upc * halfc).astype(BF)
    gpc = halfc + 0.5 * upc * (1.0 - tc * tc) * (GELU_C * (1.0 + 3.0 * GELU_K * (upc * upc)))
    outc = midc + dot(actc, dn[...], NN) + down_bias

    fgain = flat_vec(flat, FINAL_AT, D)
    fshift = flat_vec(flat, FINAL_AT + D, D)
    head_b = jnp.concatenate(
        [flat_vec(flat, HEAD_B_AT, CLASSES), jnp.zeros((1, CLASSES_PAD - CLASSES), F32)], 1
    )
    row16 = lax.broadcasted_iota(jnp.int32, (16, 1), 0)
    real = (row16 < images).astype(F32)
    xhatf, rstdf = norm_stats(outc)
    flow = (xhatf * fgain + fshift).astype(BF)
    head_low = jnp.concatenate([hw[k, 0:D, :] for k in range(8)], 1).astype(BF)
    cls_lane = lanes((16, CLASSES_PAD))
    logits = dot(flow, head_low, NN) + head_b
    logits = jnp.where(cls_lane < CLASSES, logits, MASKED)
    top = jnp.max(logits, -1, keepdims=True)
    e = jnp.exp(logits - top)
    total = jnp.sum(e, -1, keepdims=True)
    label = jnp.zeros((16, 1), jnp.int32)
    for i in range(images):
        label = jnp.where(row16 == i, labels[i], label)
    onehot = (cls_lane == label).astype(F32)
    picked = jnp.sum(jnp.where(cls_lane == label, logits, 0.0), -1, keepdims=True)
    loss = jnp.sum((top + jnp.log(total) - picked) * real, 0, keepdims=True)
    dlogits = (e / total - onehot) * (real / total_images)
    dlow = dlogits.astype(BF)
    dflow = dot(dlow, head_low, NT)
    put_factor(factors, FACTOR_FLOW, flow, images)
    put_factor(factors, FACTOR_DLOGITS, dlow, images)
    small[...] = jnp.zeros_like(small)
    exact = [jnp.broadcast_to(loss, (1, 128))]
    head_bias_grad = colsum(dlogits)
    exact += [head_bias_grad[:, 128 * k : 128 * (k + 1)] for k in range(8)]
    for value in (colsum(dflow * xhatf), colsum(dflow)):
        value = jnp.concatenate([value, jnp.zeros((1, 64), F32)], 1)
        exact += [value[:, 0:128], value[:, 128:256]]
    for k, value in enumerate(exact):
        factors[k : k + 1, :] = value
    gout = norm_back(dflow, xhatf, rstdf, fgain) * real

    ol = gout.astype(BF)
    dact = dot(ol, dn[...], NT)
    dup = dact * gpc * real
    ul = dup.astype(BF)
    dn2 = dot(ul, wt[4 * D : WIDE, :], NN)
    dmid = norm_back(dn2, xhat2c, rstd2c, gain2) + gout
    ml = dmid.astype(BF)
    small[4:5, 0:FF] = colsum(dup)
    small[10:11, 0:D] = colsum(dmid)
    small[11:12, 0:D] = colsum(dn2 * xhat2c)
    small[12:13, 0:D] = colsum(dn2)
    small[13:14, 0:D] = colsum(gout)
    dmixcls[...] = dot(ml, wt[3 * D : 4 * D, :], NN).astype(BF).astype(F32)
    dqcls[...] = jnp.zeros_like(dqcls)

    def attend_back(i, carry):
        q3, p = cls_probs(i)
        dm3 = (dmixcls[pl.ds(i, 1), :] * mask3).astype(BF)
        dp = dot(dm3, vbuf[i], NT)
        dv = dot(p.astype(BF), dm3, TN)
        ds = (p * (dp - jnp.sum(p * dp, -1, keepdims=True))).astype(BF)
        dq = dot(ds, kbuf[i], NN)
        dk = dot(ds, q3, TN)
        rows = image_rows(i)
        dkbuf[rows, :] = dk[0:TQ].astype(BF)
        dvbuf[rows, :] = dv[0:TQ].astype(BF)
        dqcls[pl.ds(i, 1), :] = colsum(dq * mask3) * HD ** (-0.5)
        return carry

    for i in range(images):
        attend_back(i, 0)
    dql = dqcls[...].astype(BF)
    dn1c = dot(dql, wt[0:D, :], NN)
    midgrad[...] = dmid
    dqcls[...] = dn1c
    for k, value in enumerate((ol, n2c, ml, mixc, dql, n1c)):
        put_factor(factors, 2 * k, value, images)
    for k, value in enumerate((actc, ul)):
        put_factor(factors, 12 + 6 * k, value, images)

    def stream_back(i, carry):
        dgain, dshift = carry
        rows = image_rows(i)
        xhat, rstd = norm_stats(x2[rows, :])
        n1low[rows, :] = (xhat * gain1 + shift1).astype(BF)
        dkl = dkbuf[rows, :]
        dvl = dvbuf[rows, :]
        dn1 = dot(dkl, wk, NN) + dot(dvl, wv, NN)
        at_cls = lax.broadcasted_iota(jnp.int32, (TQ, 1), 0) == CLS_ROW
        dn1 = dn1 + jnp.where(at_cls, dqcls[pl.ds(i, 1), :], 0.0)
        gin = norm_back(dn1, xhat, rstd, gain1)
        gstream[rows, :] = gin + jnp.where(at_cls, midgrad[pl.ds(i, 1), :], 0.0)
        return (dgain + colsum(dn1 * xhat), dshift + colsum(dn1))

    zero_row = jnp.zeros((1, D), F32)
    dgain, dshift = zero_row, zero_row
    for i in range(images):
        dgain, dshift = stream_back(i, (dgain, dshift))
    dwk = dot(dkbuf[...], n1low[...], TN)
    dwv = dot(dvbuf[...], n1low[...], TN)
    small[8:9, 0:D] = dgain
    small[9:10, 0:D] = dshift
    kv[0:D, :] = dwk[:, 0:128]
    kv[D : 2 * D, :] = dwv[:, 0:128]
    kv[2 * D :, 0:64] = dwk[:, 128:192]
    kv[2 * D :, 64:128] = dwv[:, 128:192]


def layer_back(
    images,
    group,
    x,
    mid,
    qs,
    ks,
    vs,
    probs,
    mixs,
    acts,
    gps,
    gains,
    gout,
    wt,
    dn,
    gin,
    gt,
    vec,
    upb,
    olbuf,
    ulbuf,
    n2buf,
    mlbuf,
    n1buf,
    dqbuf,
    dkbuf,
    dvbuf,
    mixbuf,
    actbuf,
):
    gain1, shift1, gain2, shift2 = [gains[k : k + 1, :] for k in range(4)]
    masks = [head_mask(h).astype(BF) for h in range(HEADS)]
    image = pl.program_id(0)
    start = pl.multiple_of(image * TQ, 16)

    @pl.when(image == 0)
    def _():
        vec[...] = jnp.zeros_like(vec)
        upb[...] = jnp.zeros_like(upb)

    def body(tq, tk):
        rows = pl.ds(start, tq)
        go = gout[0:tq, :]
        ol = go.astype(BF)
        olbuf[rows, :] = ol
        actbuf[rows, :] = acts[0:tq, :]
        mixbuf[rows, :] = mixs[0:tq, :]
        dact = dot(ol, dn[0], NT)
        dup = dact * gps[0:tq, :].astype(F32)
        ul = dup.astype(BF)
        ulbuf[rows, :] = ul
        dn2 = dot(ul, wt[0, 4 * D : WIDE, :], NN)
        xhat2, rstd2 = norm_stats(mid[0:tq, :])
        n2buf[rows, :] = (xhat2 * gain2 + shift2).astype(BF)
        dmid = norm_back(dn2, xhat2, rstd2, gain2) + go
        ml = dmid.astype(BF)
        mlbuf[rows, :] = ml
        upb[0:1, :] += colsum(dup)
        vec[2:3, :] += colsum(dmid)
        vec[3:4, :] += colsum(dn2 * xhat2)
        vec[4:5, :] += colsum(dn2)
        vec[5:6, :] += colsum(go)
        dmix = dot(ml, wt[0, 3 * D : 4 * D, :], NN).astype(BF)
        q = qs[0:tq, :]
        kk = ks[0, 0:tk, :]
        vv = vs[0, 0:tk, :]
        dq = dk = dv = None
        for h in range(HEADS):
            qh = q * masks[h]
            dmh = dmix * masks[h]
            low = probs[0, h, 0:tq, 0:tk]
            p = low.astype(F32)
            dp = dot(dmh, vv, NT)
            t = p * dp
            ds = (t - p * jnp.sum(t, -1, keepdims=True)).astype(BF)
            dv_h = dot(low, dmh, TN)
            dq_h = dot(ds, kk * masks[h], NN)
            dk_h = dot(ds, qh, TN)
            dq, dk, dv = (dq_h, dk_h, dv_h) if dq is None else (dq + dq_h, dk + dk_h, dv + dv_h)
        dql = (dq * HD ** (-0.5)).astype(BF)
        dkl = dk[0:tq].astype(BF)
        dvl = dv[0:tq].astype(BF)
        dqbuf[rows, :] = dql
        dkbuf[rows, :] = dkl
        dvbuf[rows, :] = dvl
        dn1 = (
            dot(dql, wt[0, 0:D, :], NN)
            + dot(dkl, wt[0, D : 2 * D, :], NN)
            + dot(dvl, wt[0, 2 * D : 3 * D, :], NN)
        )
        xhat1, rstd1 = norm_stats(x[0:tq, :])
        n1buf[rows, :] = (xhat1 * gain1 + shift1).astype(BF)
        vec[0:1, :] += colsum(dn1 * xhat1)
        vec[1:2, :] += colsum(dn1)
        gin[0:tq, :] = norm_back(dn1, xhat1, rstd1, gain1) + dmid
        if tq < TQ:
            rest = pl.ds(start + tq, TQ - tq)
            gin[tq:TQ, :] = jnp.zeros((TQ - tq, D), F32)
            for ref in (olbuf, ulbuf, n2buf, mlbuf, n1buf, dqbuf, dkbuf, dvbuf, mixbuf, actbuf):
                ref[rest, :] = jnp.zeros((TQ - tq, ref.shape[1]), BF)

    by_size(group, body)

    @pl.when(image == images - 1)
    def _():
        store_layer_grads(
            gt,
            [
                (0, dot(dqbuf[...], n1buf[...], TN)),
                (D, dot(dkbuf[...], n1buf[...], TN)),
                (2 * D, dot(dvbuf[...], n1buf[...], TN)),
                (3 * D, dot(mlbuf[...], mixbuf[...], TN)),
                (4 * D, dot(ulbuf[...], n2buf[...], TN)),
                (WIDE, dot(actbuf[...], olbuf[...], TN)),
            ],
        )


def share_halves(gt, keep, send, mine):
    half = keep.shape[0]
    keep[...] = gt[pl.ds(pl.multiple_of(mine * half, 8), half), :]
    send[...] = gt[pl.ds(pl.multiple_of((1 - mine) * half, 8), half), :]


def middle_kernel(images, groups, me, *refs):
    inputs, (kv, small) = refs[:13], refs[13:15]
    gin, keep, send, vec, upb, gt, *buffers = refs[15:]
    image = pl.program_id(0)
    layer_back(images, groups[image], *inputs, gin, gt, vec, upb, *buffers)

    @pl.when(image == images - 1)
    def _():
        gt[PACKED:VEC_KEPT, :] = kv[...]
        gt[VEC_KEPT:, :] = jnp.zeros((MIDDLE_ROWS - VEC_KEPT, 128), F32)
        put = functools.partial(put_entries, gt, VEC_KEPT - VEC_ROW)
        put_vectors(put, 1, vec, upb[0:1, :])
        put_vectors(put, 2, small[8:14, :], small[4:5, 0:FF])
        share_halves(gt, keep, send, me[0] & 1)


def first_kernel(images, groups, me, *refs):
    inputs, patches = refs[:13], refs[13]
    keep, send, gt, gin, vec, upb, pgrad, posgrad, *buffers = refs[14:]
    image = pl.program_id(0)
    layer_back(images, groups[image], *inputs, gin, gt, vec, upb, *buffers)

    @pl.when(image == 0)
    def _():
        pgrad[...] = jnp.zeros_like(pgrad)
        posgrad[...] = jnp.zeros_like(posgrad)

    g = gin[...]
    used = PATCH_AT + PATCHES
    posgrad[0, 0:used, :] += g[0:used, 0:128]
    posgrad[1, 0:used, 0:64] += g[0:used, 128:192]
    pg = dot(patches[0], g[PATCH_AT:used].astype(BF), TN)
    pgrad[0] += pg[:, 0:128]
    pgrad[1, :, 0:64] += pg[:, 128:192]
    pl.when(image == images - 1)(
        lambda: pack_first(keep, send, gt, vec, upb, pgrad, posgrad, me[0] & 1)
    )


def put_vectors(put, l, six, up):
    at = VEC_AT + l * VEC_LAYER
    for k in range(6):
        row = jnp.concatenate([six[k : k + 1, 0:D], jnp.zeros((1, 64), F32)], 1)
        put(at + k * D, row, D)
    put(at + 6 * D, up, FF)


def pack_first(keep, send, gt, vec, upb, pgrad, posgrad, core):
    def pos_rows(at):
        return jnp.concatenate([posgrad[0, at : at + 1, :], posgrad[1, at : at + 1, :]], 1)

    cls_row = pos_rows(CLS_ROW)
    patch_b = jnp.concatenate(
        [colsum(posgrad[k, PATCH_AT : PATCH_AT + PATCHES, :]) for k in range(2)], 1
    )
    posgrad[0, 7:8, :] = cls_row[:, 0:128]
    posgrad[1, 7:8, :] = cls_row[:, 128:256]
    base = PACKED + PATCH_ROWS
    gt[base:, :] = jnp.zeros((FIRST_ROWS - base, 128), F32)
    pack_pairs(pgrad, 0, gt, PACKED, PATCH_DIM // 2)
    pack_pairs(posgrad, 7, gt, base + POS_AT // 128 - TAIL_ROW, SEQ // 2)
    put = functools.partial(put_entries, gt, base - TAIL_ROW)
    put(CLS_AT, cls_row, D)
    put(PATCH_B_AT, patch_b, D)
    put(POS_AT + (SEQ - 1) * D, pos_rows(7 + SEQ - 1), D)
    put_vectors(put, 0, vec, upb[0:1, :])
    share_halves(gt, keep, send, core)


def parts(a):
    high = a.astype(BF)
    return high, (a - high.astype(F32)).astype(BF)


def parts_dot(a, b, how):
    return dot(a[0], b[0], how) + (dot(a[0], b[1], how) + dot(a[1], b[0], how))


def split_dot(a, b, how):
    return parts_dot(parts(a), parts(b), how)


def own_rows(ref, l, at, width):
    if width % 8 == 0:
        return ref[l, pl.ds(pl.multiple_of(at, 8), width), :]
    rows = -(-(width + 7) // 8) * 8
    base = pl.multiple_of((at // 8) * 8, 8)
    x = ref[l, pl.ds(base, rows), :]
    return pltpu.roll(x, lax.rem(rows - (at - base), rows), 0)[:width]


def coefficient_kernel(devices, gathered, basis, exact, extra):
    total = gathered[0]
    for d in range(1, devices):
        total = total + gathered[d]
    exact[...] = total
    c = split_dot(jnp.broadcast_to(block_row(exact), (8, BLOCK_PAD)), basis[...], NT)[0:1, :]
    extra[...] = jnp.zeros_like(extra)
    for k in range(3):
        high = c.astype(BF).astype(F32)
        extra[k : k + 1, 0:BASIS] = high
        c = c - high


def late_kernel(devices, images, gathered, g2, headflat, hg):
    rows = gathered.shape[0] // devices

    def factor(block, count):
        columns = []
        for b in range(block, block + count):
            parts = [
                gathered[pl.ds(EXACT_ROWS + b * images + i, devices, stride=rows), :]
                for i in range(images)
            ]
            columns.append(jnp.concatenate(parts, 0))
        return jnp.concatenate(columns, 1).astype(BF)

    ol, n2, ml, mix, dq, n1 = [factor(2 * k, 2)[:, 0:D] for k in range(6)]
    act, ul = factor(12, 6), factor(18, 6)
    g2[0:D, :] = dot(dq, n1, TN)
    g2[3 * D : 4 * D, :] = dot(ml, mix, TN)
    g2[4 * D : WIDE, :] = dot(ul, n2, TN)
    g2[WIDE:, :] = dot(act, ol, TN)
    flow = factor(FACTOR_FLOW, 2)[:, 0:D]
    for k in range(8):
        hg[k, 0:D, :] = dot(flow, factor(FACTOR_DLOGITS + k, 1), TN)
    hg[:, D:, :] = jnp.zeros((8, HEAD_ROOM - D, 128), F32)
    pack_head(hg, headflat)


def block_row(exact):
    pieces = [
        jnp.concatenate([exact[at : at + 1, :], exact[at + 1 : at + 2, 0:64]], 1) for at in (9, 11)
    ]
    pieces += [exact[1 + k : 2 + k, :] for k in range(8)]
    return jnp.concatenate(pieces, 1)


def unpack_layer(src, out, l, which):
    half = ROWS_OUT // 2
    for c in range(18):
        out[l, c * 128 : (c + 1) * 128, 0:128] = src[c * 128 : (c + 1) * 128, :].astype(F32)
    for c in range(9):
        g = src[ROWS_OUT + c * 128 : ROWS_OUT + (c + 1) * 128, :].astype(F32)
        out[l, c * 128 : (c + 1) * 128, 128:192] = g[:, 0:64]
        out[l, half + c * 128 : half + (c + 1) * 128, 128:192] = g[:, 64:128]


def square_rows(ref, start, stop, acc):
    step = 64
    for at in range(start, stop, step):
        g = ref[at : min(at + step, stop), :].astype(F32)
        g = g * g
        for lane in range(0, g.shape[1], 128):
            part = g[:, lane : lane + 128]
            rows = part.shape[0]
            part = jnp.sum(part.reshape(rows // 8, 8, part.shape[1]), 0)
            if part.shape[1] < 128:
                part = jnp.concatenate([part, jnp.zeros((8, 128 - part.shape[1]), F32)], 1)
            acc = acc + part
    return acc


def total_of(x):
    return jnp.sum(jnp.sum(x, 0, keepdims=True), 1, keepdims=True)


def muon_kernel(column_width, row_width, n_pieces, place, *refs):
    pieces = refs[:n_pieces]
    (
        g2,
        headflat,
        exact,
        basis,
        mom_far,
        wide_w,
        wide_mom,
        down_w,
        down_mom,
    ) = refs[n_pieces : n_pieces + 9]
    (
        wide_new,
        wide_mom_new,
        wide_copy,
        down_new,
        down_mom_new,
        down_copy,
        share_grad,
        scal,
        flat,
        mid_rows,
        first_rows,
        coef,
        gfull,
        mats,
        powers,
        mom,
        mom_sem,
    ) = refs[n_pieces + 9 :]
    wide_at, down_at, mine = place[2], place[3], place[4]
    start = pl.multiple_of(place[0], 192)
    count = place[1]
    inner = pieces[0].shape[0]
    total_pieces = n_pieces * inner
    mr, fr = MIDDLE_ROWS // total_pieces, FIRST_ROWS // total_pieces

    mom_copies = [
        pltpu.make_async_copy(mom_far.at[:, l], mom.at[l], mom_sem.at[l]) for l in range(LAYERS)
    ]
    for copy in mom_copies:
        copy.start()

    for k in range(n_pieces):
        for z in range(inner):
            at = mine ^ (k * inner + z)
            mid_rows[pl.ds(pl.multiple_of(at * mr, 16), mr), :] = pieces[k][z, 0:mr, :]
            first_rows[pl.ds(pl.multiple_of(at * fr, 16), fr), :] = pieces[k][z, mr : mr + fr, :]
            coef[pl.ds(pl.multiple_of(at * 16, 16), 16), :] = pieces[k][
                z, mr + fr : mr + fr + 16, :
            ].astype(F32)
    unpack_layer(first_rows, gfull, 0, 0)
    unpack_layer(mid_rows, gfull, 1, 1)
    gfull[2, 0:D, :] = g2[0:D, :]
    gfull[2, 3 * D : ROWS_OUT, :] = g2[3 * D :, :]
    gfull[2, D : 3 * D, 0:128] = mid_rows[PACKED : PACKED + 2 * D, :].astype(F32)
    tail = mid_rows[PACKED + 2 * D : PACKED + 3 * D, :].astype(F32)
    gfull[2, D : 2 * D, 128:192] = tail[:, 0:64]
    gfull[2, 2 * D : 3 * D, 128:192] = tail[:, 64:128]

    base = PACKED + PATCH_ROWS
    flat[0:PATCH_ROWS, :] = first_rows[PACKED:base, :].astype(F32)
    flat[PATCH_ROWS : PATCH_ROWS + HEAD_ROWS, :] = headflat[0:HEAD_ROWS, :]
    tail = first_rows[base:FIRST_ROWS, :].astype(F32)
    vectors = mid_rows[VEC_KEPT : VEC_KEPT + 32, :].astype(F32)
    flat[TAIL_ROW:VEC_ROW, :] = tail[0 : TAIL_ROWS - 1]
    flat[VEC_ROW : VEC_ROW + 1, :] = tail[TAIL_ROWS - 1 : TAIL_ROWS] + vectors[0:1]
    flat[VEC_ROW + 1 : VEC_ROW + VEC_ROWS, :] = vectors[1:VEC_ROWS]
    used = VEC_ROW + VEC_ROWS
    flat[used:, :] = jnp.zeros((flat.shape[0] - used, 128), F32)
    block = block_row(exact)

    sums = jnp.zeros((16, 128), F32)
    for at in range(total_pieces):
        sums = sums + coef[16 * at : 16 * (at + 1), :]
    c = sums[0:1, :] + sums[1:2, :] + sums[2:3, :]
    acc = jnp.zeros((8, 128), F32)
    acc = square_rows(first_rows, 0, PACKED, acc)
    acc = square_rows(mid_rows, 0, VEC_KEPT, acc)
    acc = square_rows(g2, 0, D, acc)
    acc = square_rows(g2, 3 * D, ROWS_OUT, acc)
    acc = square_rows(flat, 0, flat.shape[0], acc)
    squares = total_of(acc) + total_of(jnp.where(lanes((1, BLOCK_PAD)) < 2 * D + CLASSES, block * block, 0.0))
    coef_square = jnp.sum(c * c, 1, keepdims=True)
    norm = jnp.sqrt(squares - coef_square)
    factor = CLIP_AT / jnp.maximum(norm, CLIP_AT)
    scal[...] = jnp.zeros_like(scal)
    for k, value in enumerate((norm, factor, jnp.sqrt(coef_square), exact[0:1, 0:1], c)):
        scal[k : k + 1, :] = jnp.broadcast_to(value, (1, 128))

    block = block - split_dot(
        jnp.broadcast_to(c[:, 0:BASIS], (8, BASIS)), basis[...], NN
    )[0:1, :]
    put_entries(flat, 0, FINAL_AT, block, 2 * D + CLASSES)
    rows = share_grad.shape[0]
    at, shift = place[5], place[6]
    base_row = pl.multiple_of((at // 8) * 8, 8)
    off = at - base_row
    window = flat[pl.ds(base_row, rows + 16), :]
    here = pltpu.roll(window, lax.rem(rows + 16 - off, rows + 16), 0)
    there = pltpu.roll(window, lax.rem(rows + 15 - off, rows + 16), 0)[0:rows]
    here = here[0:rows]
    back = lax.rem(128 - shift, 128)
    g = jnp.where(
        lanes((rows, 128)) < 128 - shift, pltpu.roll(here, back, 1), pltpu.roll(there, back, 1)
    )
    share_grad[...] = g * factor

    row = lax.broadcasted_iota(jnp.int32, (FF, 1), 0)
    sizes = []
    eye = (
        lax.broadcasted_iota(jnp.int32, (D, D), 0) == lax.broadcasted_iota(jnp.int32, (D, D), 1)
    ).astype(F32)
    own = []
    for k in range(2 * LAYERS):
        l, which = divmod(k, 2)
        if which == 0:
            mom_copies[l].wait()
            m = mom[l, pl.ds(start // column_width, FF // column_width), 0:column_width, :]
            m = BETA_ONE * m.reshape(FF, D) + factor * gfull[l, pl.ds(start, FF), :]
            m = jnp.where(row < count, m, 0.0)
            kept = BETA_ONE * wide_mom[l] + factor * own_rows(gfull, l, wide_at, column_width)
            wide_mom_new[l] = kept
        else:
            m = BETA_ONE * mom[l, :, column_width:, :].reshape(FF, D)
            m = m + factor * gfull[l, WIDE:ROWS_OUT, :]
            kept = BETA_ONE * down_mom[l] + factor * own_rows(gfull, l, down_at, row_width)
            down_mom_new[l] = kept
        size = 1.0 / (jnp.sqrt(total_of(m * m)) + SHAPE_EPS)
        high, low = parts(m * size)
        cross = dot(high, low, TN)
        mats[k] = dot(high, high, TN) + (cross + cross.T)
        n = kept.shape[0]
        if n < powers.shape[1]:
            powers[k] = jnp.zeros(powers.shape[1:], F32)
        powers[k, 0:n, :] = kept * size

    def polynomial(k):
        a = parts(mats[k])
        cross = dot(a[0], a[1], NN)
        b = dot(a[0], a[0], NN) + (cross + cross.T)
        return a, 3.4445 * eye - 4.775 * mats[k] + 2.0315 * b

    def step(it, carry):
        polys = [polynomial(k) for k in range(2 * LAYERS)]
        ps = [parts(p) for _, p in polys]
        ts = [parts_dot(p, a, NN) for (a, _), p in zip(polys, ps)]
        for k in range(2 * LAYERS):
            both = parts_dot(parts(jnp.concatenate([ts[k], powers[k]], 0)), ps[k], NN)
            mats[k] = both[0:D]
            powers[k] = both[D:]
        return carry

    lax.fori_loop(0, 4, step, 0)
    side = jnp.where(count == 4 * D, 768.0, jnp.where(count == 3 * D, 576.0, 192.0))
    rate = jnp.sqrt(jnp.full((1, 1), 1.0, F32) * side) * (MUON_RATE * 0.2)
    for k in range(2 * LAYERS):
        l, which = divmod(k, 2)
        _, p = polynomial(k)
        update = parts_dot(parts(powers[k]), parts(p), NN)
        if which == 0:
            new = wide_w[l] - rate * update[0:column_width]
            wide_new[l] = new
            wide_copy[l] = new.astype(BF)
        else:
            new = down_w[l] - (MUON_RATE * 0.2 * FF**0.5) * update[0:row_width]
            down_new[l] = new
            down_copy[l] = new.astype(BF)


def cost(micros):
    return pl.CostEstimate(
        flops=int(micros * 1.15e9), bytes_accessed=int(micros * 1e6), transcendentals=0
    )


def pad_rows(x, rows):
    return jnp.pad(x, (0, rows * 128 - x.shape[0])).reshape(rows, 128)


def pack_shard(wide_t, down):
    rows = jnp.concatenate([wide_t, down], 1)
    rows = rows.reshape(-1, D).astype(BF)
    a_rows, h = half_rows(rows.shape[0])
    head = jnp.pad(rows[:, :128], ((0, a_rows - rows.shape[0]), (0, 0)))
    tail = jnp.pad(rows[:, 128:], ((0, 2 * h - rows.shape[0]), (0, 0)))
    tail = jnp.concatenate([tail[:h], tail[h:]], 1)
    fill = -(a_rows + h) % 16
    return jnp.concatenate([head, tail] + ([jnp.zeros((fill, 128), BF)] if fill else []), 0)


def stage_masks(stages):
    masks = [0]
    for low, width in reversed(stages):
        masks = [a ^ (m << low) for m in range(1 << width) for a in masks]
    return masks


def gather_stages(arrays, stages, devices, apart=2):
    for depth in reversed(range(len(stages))):
        low, width = stages[depth]
        got = [swap(x, m << low, devices) for m in range(1, 1 << width) for x in arrays]
        arrays = arrays + got
        if depth >= apart:
            arrays = [jnp.concatenate(arrays, 0)]
    return arrays


def combine_kernel(spot, middle_keep, middle_got, first_keep, first_got, own, one, two, three):
    mine = spot[0]
    at = 0
    for keep, got in ((middle_keep, middle_got), (first_keep, first_got)):
        n = keep.shape[0] // 4
        for m, out in enumerate((own, one, two, three)):
            rows = pl.ds(pl.multiple_of((mine ^ m) * n, 16), n)
            out[at : at + n, :] = (keep[rows, :] + got[rows, :]).astype(out.dtype)
        at += n


def swap(x, mask, devices):
    return lax.ppermute(x, AXES, [(i, i ^ mask) for i in range(devices)])


def local(
    patches,
    groups,
    labels,
    wide_w,
    down_w,
    plain,
    wide_mom,
    down_mom,
    plain_first,
    plain_second,
    basis_plain,
):
    devices = lax.axis_size(AXES)
    bits = devices.bit_length() - 1
    me = lax.axis_index(AXES).astype(jnp.int32)
    images = patches.shape[0]
    share = plain.shape[0]
    column_width = wide_w.shape[2]
    row_width = down_w.shape[1]
    vmem = pl.BlockSpec(memory_space=pltpu.VMEM)
    smem = pl.BlockSpec(memory_space=pltpu.SMEM)
    params = pltpu.CompilerParams(vmem_limit_bytes=VMEM_LIMIT)
    S = jax.ShapeDtypeStruct

    number_of = [(0, 1), (1, 2), (3, 2)]
    stages = number_of + ([(5, 2), (7, 1)] if bits == 8 else [(b, 1) for b in range(5, bits)])

    wide_t = jnp.transpose(wide_w, (0, 2, 1))
    plain_rows = -(-(share + 127) // 2048) * 16
    rows = plain_rows
    plain_block = pad_rows(plain, plain_rows)
    high = lax.reduce_precision(plain_block, 8, 7)
    low_half = (plain_block - high).astype(BF)
    weights_one = pack_shard(wide_t[:1], down_w[:1])
    shard_one = jnp.concatenate([high.astype(BF), weights_one, low_half], 0)
    shard_two = pack_shard(wide_t[1:], down_w[1:])
    weight_rows = weights_one.shape[0]

    one = gather_stages([shard_one[None]], stages[2:], devices, 0)[0]
    two = gather_stages([shard_two[None]], stages[2:], devices, 0)
    first_masks = stage_masks(stages[2:])
    top = 3 * devices // 4
    compact = bits == 5 and top * share <= CLS_AT
    body = rows + weight_rows
    if compact:
        low_top = lax.dynamic_index_in_dim(one[:, body:], (me >> 3) ^ 3, 0, keepdims=False)
        one = jnp.concatenate([one[:, :body].reshape(-1, 128), low_top], 0)
    else:
        one = one.reshape(-1, 128)
    one = gather_stages([one[None]], stages[1:2], devices)
    one[0] = one[0] + 0.0 * jnp.max(two[0][:, 0, 0])
    pieces_one = gather_stages([jnp.concatenate(one, 0)], stages[:1], devices)
    two = gather_stages(two, stages[1:2], devices)
    places = (first_masks, stage_masks(stages[:2]), top if compact else None)

    lead = jnp.clip(FINAL_AT - me * share + BLOCK_PAD, 0, share + BLOCK_PAD)
    basis_block = lax.dynamic_slice(
        jnp.pad(basis_plain, ((0, 0), (BLOCK_PAD, BLOCK_PAD))), (0, lead), (BASIS, BLOCK_PAD)
    )

    number = me[None]
    groups = groups.astype(jnp.int32)
    labels = labels.astype(jnp.int32)
    flat_rows = -(-((devices - 1) * share // 128 + rows + 8) // 8) * 8
    n = images * TQ
    saved = [
        S((n, D), F32),
        S((n, D), BF),
        S((images, TK, D), BF),
        S((images, TK, D), BF),
        S((images, HEADS, TQ, TK), BF),
        S((n, D), BF),
        S((n, FF), BF),
        S((n, FF), BF),
    ]
    rows_spec = pl.BlockSpec((TQ, D), lambda i: (i, 0))
    wide_spec = pl.BlockSpec((TQ, FF), lambda i: (i, 0))
    key_spec = pl.BlockSpec((1, TK, D), lambda i: (i, 0, 0))
    patch_spec = pl.BlockSpec((1, PATCHES, PATCH_DIM), lambda i: (i, 0, 0))
    saved_specs = [
        rows_spec,
        rows_spec,
        key_spec,
        key_spec,
        pl.BlockSpec((1, HEADS, TQ, TK), lambda i: (i, 0, 0, 0)),
        rows_spec,
        wide_spec,
        wide_spec,
    ]
    factor_rows = EXACT_ROWS + -(-FACTOR_BLOCKS * images // 8) * 8 + 8
    x0, *saved0, x1, gains0, wt0, dn0, flat = pl.pallas_call(
        functools.partial(
            start_kernel, devices, share, column_width, row_width, places, len(pieces_one)
        ),
        grid=(images,),
        out_shape=[S((n, D), F32)]
        + saved
        + [
            S((n, D), F32),
            S((8, D), F32),
            S((1, WIDE, D), BF),
            S((1, FF, D), BF),
            S((flat_rows, 128), F32),
        ],
        in_specs=[smem] * 2 + [vmem] * len(pieces_one) + [patch_spec],
        out_specs=[rows_spec] + saved_specs + [rows_spec] + [vmem] * 4,
        scratch_shapes=[
            pltpu.VMEM((devices, rows, 128), F32),
            pltpu.VMEM((devices, weight_rows, 128), BF),
            pltpu.VMEM((ROWS_OUT, D), F32),
            pltpu.VMEM((4, rows + 8, 128), F32),
            pltpu.VMEM((2, PATCH_DIM, 128), F32),
            pltpu.VMEM((2, TQ + 8, 128), F32),
            pltpu.VMEM((PATCH_DIM, D), BF),
        ],
        compiler_params=params,
        cost_estimate=cost(20),
        name="start",
    )(groups, number, *pieces_one, patches)

    two, x1 = lax.optimization_barrier((two, x1))
    pieces_two = gather_stages(two, stages[:1], devices)
    *saved1, gains1, gstream, kv, factors, small, wt12, dn12 = pl.pallas_call(
        functools.partial(
            forward_kernel,
            float(images * devices),
            images,
            column_width,
            row_width,
            stage_masks(stages),
            len(pieces_two),
        ),
        grid=(images,),
        out_shape=saved
        + [
            S((8, D), F32),
            S((n, D), F32),
            S((3 * D, 128), F32),
            S((factor_rows, 128), F32),
            S((16, CLASSES_PAD), F32),
            S((2, WIDE, D), BF),
            S((2, FF, D), BF),
        ],
        in_specs=[smem] * 3 + [vmem, rows_spec] + [vmem] * len(pieces_two),
        out_specs=saved_specs + [vmem] * 7,
        scratch_shapes=[
            pltpu.VMEM((devices, shard_two.shape[0], 128), BF),
            pltpu.VMEM((ROWS_OUT, D), F32),
            pltpu.VMEM((8, HEAD_ROOM, 128), F32),
            pltpu.VMEM((n, D), F32),
            pltpu.VMEM((images, TK, D), BF),
            pltpu.VMEM((images, TK, D), BF),
            pltpu.VMEM((n, D), BF),
            pltpu.VMEM((n, D), BF),
        ]
        + [pltpu.VMEM((16, D), F32)] * 6
        + [pltpu.VMEM((n, D), BF)],
        compiler_params=params,
        cost_estimate=cost(30),
        name="forward",
    )(groups, labels, number, flat, x1, *pieces_two)

    mom_shard = jnp.concatenate([jnp.transpose(wide_mom, (0, 2, 1)), down_mom], 1)
    mom_all = lax.all_gather(mom_shard, AXES, axis=0)
    factors, mom_all = lax.optimization_barrier((factors, mom_all))
    gstream, factors = lax.optimization_barrier((gstream, factors))
    factors_all = lax.all_gather(factors, AXES, axis=0)
    back_scratch = [
        pltpu.VMEM((n, D), BF),
        pltpu.VMEM((n, FF), BF),
        pltpu.VMEM((n, D), BF),
        pltpu.VMEM((n, D), BF),
        pltpu.VMEM((n, D), BF),
        pltpu.VMEM((n, D), BF),
        pltpu.VMEM((n, D), BF),
        pltpu.VMEM((n, D), BF),
        pltpu.VMEM((n, D), BF),
        pltpu.VMEM((n, FF), BF),
    ]
    gstream1, middle_keep, middle_send = pl.pallas_call(
        functools.partial(middle_kernel, images),
        out_shape=[
            S((n, D), F32),
            S((MIDDLE_ROWS // 2, 128), F32),
            S((MIDDLE_ROWS // 2, 128), F32),
        ],
        grid=(images,),
        in_specs=[smem] * 2 + [rows_spec] + saved_specs + [vmem, rows_spec] + [vmem] * 4,
        out_specs=[rows_spec] + [vmem] * 2,
        scratch_shapes=[
            pltpu.VMEM((8, D), F32),
            pltpu.VMEM((8, FF), F32),
            pltpu.VMEM((MIDDLE_ROWS, 128), F32),
        ]
        + back_scratch,
        compiler_params=params,
        cost_estimate=cost(23),
        name="middle",
    )(groups, number, x1, *saved1, gains1, gstream, wt12, dn12, kv, small)

    first_keep, first_send = pl.pallas_call(
        functools.partial(first_kernel, images),
        out_shape=[S((FIRST_ROWS // 2, 128), F32)] * 2,
        grid=(images,),
        in_specs=[smem] * 2
        + [rows_spec]
        + saved_specs
        + [vmem, rows_spec]
        + [vmem] * 2
        + [patch_spec],
        out_specs=[vmem] * 2,
        scratch_shapes=[
            pltpu.VMEM((FIRST_ROWS, 128), F32),
            pltpu.VMEM((TQ, D), F32),
            pltpu.VMEM((8, D), F32),
            pltpu.VMEM((8, FF), F32),
            pltpu.VMEM((2, PATCH_DIM, 128), F32),
            pltpu.VMEM((2, TQ + 16, 128), F32),
        ]
        + back_scratch,
        compiler_params=params,
        cost_estimate=cost(25),
        name="first",
    )(groups, number, x0, *saved0, gains0, gstream1, wt0, dn0, patches)

    late_params = pltpu.CompilerParams(
        vmem_limit_bytes=12 * 1024 * 1024 + 1024 * devices * factor_rows
    )
    exact, extra = pl.pallas_call(
        functools.partial(coefficient_kernel, devices),
        grid=(1,),
        out_shape=[S((EXACT_ROWS, 128), F32), S((16, 128), F32)],
        in_specs=[pl.BlockSpec((devices, EXACT_ROWS, 128), lambda i: (0, 0, 0)), vmem],
        out_specs=[vmem] * 2,
        compiler_params=late_params,
        cost_estimate=cost(2),
        name="coefficients",
    )(factors_all, basis_block)

    g2, headflat = pl.pallas_call(
        functools.partial(late_kernel, devices, images),
        out_shape=[S((ROWS_OUT, D), F32), S((HEAD_FLAT_ROOM, 128), F32)],
        in_specs=[vmem],
        out_specs=[vmem] * 2,
        scratch_shapes=[pltpu.VMEM((8, HEAD_ROOM, 128), F32)],
        compiler_params=late_params,
        cost_estimate=cost(4),
        name="late",
    )(factors_all.reshape(devices * factor_rows, 128))

    split_bits = 5
    for bit in range(split_bits, bits):
        extra = extra + swap(extra, 1 << bit, devices)
    if bits > split_bits:
        c = extra[0] + extra[1] + extra[2]
        split = []
        for k in range(3):
            split.append(lax.reduce_precision(c, 8, 7))
            c = c - split[-1]
        extra = jnp.concatenate([jnp.stack(split), extra[3:]], 0)
    quarter = (MIDDLE_ROWS + FIRST_ROWS) // 8
    small_params = pltpu.CompilerParams(vmem_limit_bytes=16 * 1024 * 1024)
    total, *sends = pl.pallas_call(
        combine_kernel,
        out_shape=[S((quarter, 128), F32)] + [S((quarter, 128), BF)] * 3,
        in_specs=[smem] + [vmem] * 4,
        out_specs=[vmem] * 4,
        compiler_params=small_params,
        cost_estimate=cost(2),
        name="combine",
    )(
        ((me >> 1) & 3)[None],
        middle_keep,
        swap(middle_send, 1, devices),
        first_keep,
        swap(first_send, 1, devices),
    )
    for m in range(1, 4):
        total = total + swap(sends[m - 1], m << 1, devices).astype(F32)
    mr, fr = MIDDLE_ROWS // 8, FIRST_ROWS // 8
    kept = jnp.concatenate(
        [total[:mr].reshape(4, mr // 4, 128), total[mr:].reshape(4, fr // 4, 128)], 1
    )
    mine = (me >> 3) & 3
    total = lax.dynamic_index_in_dim(kept, mine, 0, keepdims=False)
    for m in range(1, 4):
        send = lax.dynamic_index_in_dim(kept, mine ^ m, 0, keepdims=False)
        if m == 3:
            send = send + 0.0 * extra[0, 0]
        total = total + swap(send.astype(BF), m << 3, devices).astype(F32)
    kept = total
    for bit in range(split_bits, bits):
        small_part = kept.astype(BF)
        kept = small_part.astype(F32) + swap(small_part, 1 << bit, devices).astype(F32)
    piece = jnp.concatenate([kept, extra], 0).astype(BF)[None]
    piece = gather_stages([piece], number_of[2:], devices, 0)[0]
    pieces = [piece] + [swap(piece, m << 1, devices) for m in range(1, 3)]
    pieces = pieces + [swap(piece + (0.0 * g2[0, 0]).astype(BF), 3 << 1, devices)]
    pieces = pieces + [swap(p, 1, devices) for p in pieces]

    first_column = me * column_width
    in_q = first_column < 3 * D
    in_o = first_column < 4 * D
    start = jnp.where(in_q, 0, jnp.where(in_o, 3 * D, 4 * D))
    count = jnp.where(in_q, 3 * D, jnp.where(in_o, D, FF))
    piece_number = ((me & 1) << 4) | (((me >> 1) & 3) << 2) | ((me >> 3) & 3)
    at = me * share
    spots = jnp.stack(
        [start, count, first_column, WIDE + me * row_width, piece_number, at // 128, at % 128]
    )
    wide_shape = (LAYERS, column_width, D)
    down_shape = (LAYERS, row_width, D)
    flat_rows = -(-((devices - 1) * share // 128 + rows + 24) // 8) * 8
    (
        wide_new,
        wide_mom_new,
        wide_copy,
        down_new,
        down_mom_new,
        down_copy,
        share_grad,
        scal,
    ) = pl.pallas_call(
        functools.partial(muon_kernel, column_width, row_width, len(pieces)),
        out_shape=[
            S(wide_shape, F32),
            S(wide_shape, F32),
            S(wide_shape, BF),
            S(down_shape, F32),
            S(down_shape, F32),
            S(down_shape, BF),
            S((rows, 128), F32),
            S((8, 128), F32),
        ],
        in_specs=[smem]
        + [vmem] * (len(pieces) + 4)
        + [pl.BlockSpec(memory_space=pltpu.HBM)]
        + [vmem] * 4,
        out_specs=[vmem] * 8,
        scratch_shapes=[
            pltpu.VMEM((flat_rows, 128), F32),
            pltpu.VMEM((MIDDLE_ROWS, 128), BF),
            pltpu.VMEM((FIRST_ROWS, 128), BF),
            pltpu.VMEM((16 * 32, 128), F32),
            pltpu.VMEM((LAYERS, ROWS_OUT + 16, D), F32),
            pltpu.VMEM((2 * LAYERS, D, D), F32),
            pltpu.VMEM((2 * LAYERS, -(-max(column_width, row_width) // 8) * 8, D), F32),
            pltpu.VMEM((LAYERS, devices, column_width + row_width, D), F32),
            pltpu.SemaphoreType.DMA((LAYERS,)),
        ],
        compiler_params=pltpu.CompilerParams(vmem_limit_bytes=48 * 1024 * 1024),
        cost_estimate=cost(20),
        name="muon",
    )(
        spots.astype(jnp.int32),
        *pieces,
        g2,
        headflat,
        exact,
        basis_block,
        mom_all,
        wide_t,
        jnp.transpose(wide_mom, (0, 2, 1)),
        down_w,
        down_mom,
    )
    grad_norm, _, removed_norm, loss_sum = [scal[k, 0] for k in range(4)]
    clipped = share_grad.reshape(-1)[:share]
    first_new = BETA_ONE * plain_first + (1.0 - BETA_ONE) * clipped
    second_new = BETA_TWO * plain_second + (1.0 - BETA_TWO) * clipped * clipped
    first_hat = first_new / (1.0 - BETA_ONE**STEP)
    second_hat = second_new / (1.0 - BETA_TWO**STEP)
    plain_new = plain - ADAM_RATE * (
        first_hat / (jnp.sqrt(second_hat) + ADAM_EPS) + DECAY_RATE * plain
    )
    plain_copy = plain_new.astype(BF)
    return (
        loss_sum,
        removed_norm,
        grad_norm,
        *[jnp.transpose(x, (0, 2, 1)) for x in (wide_new, wide_mom_new, wide_copy)],
        down_new,
        down_mom_new,
        down_copy,
        plain_new,
        first_new,
        second_new,
        plain_copy,
    )


def solution(mesh):
    placed = (
        P(AXES, None, None),
        P(AXES),
        P(AXES),
        P(None, None, AXES),
        P(None, AXES, None),
        P(AXES),
        P(None, None, AXES),
        P(None, AXES, None),
        P(AXES),
        P(AXES),
        P(None, AXES),
    )
    return jax.shard_map(
        local,
        mesh=mesh,
        in_specs=placed,
        out_specs=(
            P(),
            P(),
            P(),
            P(None, None, AXES),
            P(None, None, AXES),
            P(None, None, AXES),
            P(None, AXES, None),
            P(None, AXES, None),
            P(None, AXES, None),
            P(AXES),
            P(AXES),
            P(AXES),
            P(AXES),
        ),
        check_vma=False,
    )
```

```python
import functools
import math

import jax
import jax.numpy as jnp
from jax import lax
from jax.experimental import pallas as pl
from jax.experimental.pallas import tpu as pltpu
from jax.sharding import PartitionSpec as P

D = 192
HEADS = 3
HD = 64
FF = 768
PATCH_DIM = 768
CLASSES = 1000
CLASSES_PAD = 1024
LAYERS = 3
SEQ = 325
PATCHES = SEQ - 1
LEN_MID = 197
LEN_SHORT = 101
BASIS = 64
STEP = 10
WIDE = 1536
ROWS_OUT = WIDE + FF

HEAD_AT = PATCH_DIM * D
CLS_AT = HEAD_AT + D * CLASSES
PATCH_B_AT = CLS_AT + D
POS_AT = PATCH_B_AT + D
VEC_AT = POS_AT + SEQ * D
VEC_LAYER = 6 * D + FF
FINAL_AT = VEC_AT + LAYERS * VEC_LAYER
HEAD_B_AT = FINAL_AT + 2 * D
USED = HEAD_B_AT + CLASSES
HEAD_ROWS = D * CLASSES // 128
HEAD_ROOM = 256
HEAD_FLAT_ROOM = 2000
BLOCK_PAD = 2 * D + CLASSES_PAD
PATCH_ROWS = HEAD_AT // 128
TAIL_ROW = CLS_AT // 128
VEC_ROW = (VEC_AT + VEC_LAYER) // 128
TAIL_ROWS = VEC_ROW + 1 - TAIL_ROW
VEC_ROWS = FINAL_AT // 128 + 1 - VEC_ROW

PACKED = ROWS_OUT * 3 // 2
MIDDLE_ROWS = 4096
FIRST_ROWS = 5120
VEC_KEPT = PACKED + 3 * D

TQ = 336
TK = 384
CLS_ROW = 0
PATCH_AT = 8
SIZES = ((112, 128), (208, 256), (336, 384))

NORM_EPS = 1e-06
CLIP_AT = 0.02
MUON_RATE = 0.3
ADAM_RATE = 0.05
BETA_ONE = 0.5
BETA_TWO = 0.95
DECAY_RATE = 0.01
ADAM_EPS = 1e-08
SHAPE_EPS = 1e-07
MASKED = -1e30
GELU_C = math.sqrt(2.0 / math.pi)
GELU_K = 0.044715

F32 = jnp.float32
BF = jnp.bfloat16
AXES = ("dp", "fsdp")
NN = (((1,), (0,)), ((), ()))
NT = (((1,), (1,)), ((), ()))
TN = (((0,), (0,)), ((), ()))
VMEM_LIMIT = 60 * 1024 * 1024


def dot(a, b, how):
    return lax.dot_general(a, b, how, preferred_element_type=F32)


def lanes(shape):
    return lax.broadcasted_iota(jnp.int32, shape, len(shape) - 1)


def head_mask(h):
    lane = lanes((1, D))
    return jnp.where((lane >= h * HD) & (lane < (h + 1) * HD), 1.0, 0.0)


def norm_stats(x):
    mean = jnp.mean(x, -1, keepdims=True)
    centered = x - mean
    var = jnp.mean(centered * centered, -1, keepdims=True)
    rstd = lax.rsqrt(var + NORM_EPS)
    return centered * rstd, rstd


def norm_back(dn, xhat, rstd, gain):
    scaled = dn * gain
    m1 = jnp.mean(scaled, -1, keepdims=True)
    m2 = jnp.mean(scaled * xhat, -1, keepdims=True)
    return rstd * (scaled - m1 - xhat * m2)


def colsum(x):
    return jnp.sum(x, 0, keepdims=True)


def key_mask(length, keys):
    key = lanes((1, keys))
    return ((key >= PATCH_AT) & (key < PATCH_AT + length - 1)) | (key == CLS_ROW)


def by_size(group, body):
    pl.when(group == 0)(lambda: body(*SIZES[0]))
    pl.when(group == 1)(lambda: body(*SIZES[1]))
    pl.when((group != 0) & (group != 1))(lambda: body(*SIZES[2]))


def softmax_rows(scores):
    top = jnp.max(scores, -1, keepdims=True)
    e = jnp.exp(scores - top)
    return e / jnp.sum(e, -1, keepdims=True)


def merge(a, b, shift):
    if shift == 0:
        return a
    lane = lanes(a.shape)
    return jnp.where(
        lane < 128 - shift, pltpu.roll(a, 128 - shift, 1), pltpu.roll(b, 128 - shift, 1)
    )


def flat_vec(flat, at, n):
    blocks = []
    for j in range(-(-n // 128)):
        q, r = divmod(at + 128 * j, 128)
        blocks.append(merge(flat[q : q + 1, :], flat[q + 1 : q + 2, :], r))
    row = blocks[0] if len(blocks) == 1 else jnp.concatenate(blocks, 1)
    return row[:, :n]


def unpack_flat(blocks, flat, tmp, devices, share):
    rows = blocks.shape[1]
    lane = lanes((rows, 128))
    for d in range(devices):
        q, r = divmod(d * share, 128)
        block = blocks[d]
        if r == 0:
            flat[q : q + rows, :] = block
            continue
        slot = d % 4
        tmp[slot, 8 : 8 + rows, :] = pltpu.roll(block, r, 1)
        tmp[slot, 7:8, :] = flat[q : q + 1, :]
        flat[q : q + rows, :] = jnp.where(
            lane >= r, tmp[slot, 8 : 8 + rows, :], tmp[slot, 7 : 7 + rows, :]
        )


def unpack_pairs(flat, row, pairs, out, out_at):
    a = flat[pl.ds(row, pairs, stride=3), :]
    b = flat[pl.ds(row + 1, pairs, stride=3), :]
    c = flat[pl.ds(row + 2, pairs, stride=3), :]
    out[0, pl.ds(out_at, pairs, stride=2), :] = a
    out[1, pl.ds(out_at, pairs, stride=2), :] = b
    out[0, pl.ds(out_at + 1, pairs, stride=2), :] = merge(b, c, 64)
    out[1, pl.ds(out_at + 1, pairs, stride=2), :] = pltpu.roll(c, 64, 1)


def rows192(ref, at, n):
    return jnp.concatenate([ref[0, at : at + n, :], ref[1, at : at + n, 0:64]], 1)


def pack_pairs(src, src_at, flat, row, pairs):
    a = src[0, pl.ds(src_at, pairs, stride=2), :]
    b = src[1, pl.ds(src_at, pairs, stride=2), :]
    c = src[0, pl.ds(src_at + 1, pairs, stride=2), :]
    e = src[1, pl.ds(src_at + 1, pairs, stride=2), :]
    lane = lanes(a.shape)
    c = pltpu.roll(c, 64, 1)
    flat[pl.ds(row, pairs, stride=3), :] = a
    flat[pl.ds(row + 1, pairs, stride=3), :] = jnp.where(lane < 64, b, c)
    flat[pl.ds(row + 2, pairs, stride=3), :] = jnp.where(lane < 64, c, pltpu.roll(e, 64, 1))


def unpack_head(flat, out):
    lane = lanes((12, 128))
    for rho in range(16):
        for k in range(8):
            q, r = divmod(1000 * rho + 128 * k, 128)
            a = flat[pl.ds(HEAD_AT // 128 + q, 12, stride=125), :]
            b = flat[pl.ds(HEAD_AT // 128 + q + 1, 12, stride=125), :]
            block = merge(a, b, r)
            if k == 7:
                block = jnp.where(lane < CLASSES - 896, block, 0.0)
            out[k, pl.ds(rho, 12, stride=16), :] = block


def pack_head(src, out):
    lane = lanes((12, 128))
    for j in range(125):
        rho, c = divmod(128 * j, 1000)
        k, s = divmod(c, 128)
        a = src[k, pl.ds(rho, 12, stride=16), :]
        if s:
            b = a
            if k < 7:
                b = src[k + 1, pl.ds(rho, 12, stride=16), :]
            a = merge(a, b, s)
        left = 1000 - c
        if left < 128:
            nxt = src[0, pl.ds(rho + 1, 12, stride=16), :]
            a = jnp.where(lane < left, a, pltpu.roll(nxt, left, 1))
        out[pl.ds(j, 12, stride=125), :] = a


FACTOR_FLOW = 24
FACTOR_DLOGITS = 26
FACTOR_BLOCKS = 34
EXACT = 13
EXACT_ROWS = 16


def put_factor(ref, block, value, images):
    for k in range(-(-value.shape[1] // 128)):
        part = value[0:images, 128 * k : 128 * (k + 1)].astype(F32)
        at = EXACT_ROWS + (block + k) * images
        ref[at : at + images, 0 : part.shape[1]] = part


def put_entries(ref, shift_rows, at, row, n):
    lane = lanes((1, 128))
    done = 0
    while done < n:
        q, r = divmod(at + done, 128)
        q = q + shift_rows
        take = min(128 - r, n - done)
        block, off = divmod(done, 128)
        piece = row[:, 128 * block : 128 * (block + 1)]
        if off + take > 128:
            piece = merge(piece, row[:, 128 * (block + 1) : 128 * (block + 2)], off)
            off = 0
        shift = (r - off) % 128
        if shift:
            piece = pltpu.roll(piece, shift, 1)
        if take < 128:
            piece = jnp.where((lane >= r) & (lane < r + take), piece, ref[q : q + 1, :])
        ref[q : q + 1, :] = piece
        done += take


def image_rows(i):
    if isinstance(i, int):
        return pl.ds(i * TQ, TQ)
    return pl.ds(pl.multiple_of(i * TQ, 16), TQ)


def length_of(group):
    return jnp.where(group == 0, LEN_SHORT, jnp.where(group == 1, LEN_MID, SEQ))


def layer_vectors(flat, l):
    at = VEC_AT + l * VEC_LAYER
    six = [flat_vec(flat, at + k * D, D) for k in range(6)]
    return six, flat_vec(flat, at + 6 * D, FF)


def store_layer_grads(ref, parts):
    tails = []
    for at, g in parts:
        ref[at : at + g.shape[0], :] = g[:, 0:128]
        tails.append((at, g))
    half = ROWS_OUT // 2
    for at, g in tails:
        n = g.shape[0]
        low = max(0, min(n, half - at))
        if low > 0:
            ref[ROWS_OUT + at : ROWS_OUT + at + low, 0:64] = g[:low, 128:192]
        if low < n:
            start = at + low - half
            ref[ROWS_OUT + start : ROWS_OUT + start + n - low, 64:128] = g[low:, 128:192]


def half_rows(rows):
    return -(-rows // 8) * 8, -(-rows // 16) * 8


def unpack_weights(blocks, layers, column_width, row_width, asm, wt, dn):
    devices = blocks.shape[0]
    per_layer = column_width + row_width
    a_rows, h = half_rows(layers * per_layer)
    for l in range(layers):
        for d in range(devices):
            block = blocks[d].astype(F32)
            for at, n, to in (
                (l * per_layer, column_width, d * column_width),
                (l * per_layer + column_width, row_width, WIDE + d * row_width),
            ):
                asm[to : to + n, 0:128] = block[at : at + n]
                low = max(0, min(n, h - at))
                if low:
                    asm[to : to + low, 128:192] = block[a_rows + at : a_rows + at + low, 0:64]
                if low < n:
                    start = a_rows + at + low - h
                    asm[to + low : to + n, 128:192] = block[start : start + n - low, 64:128]
        wt[l] = asm[0:WIDE, :].astype(BF)
        dn[l] = asm[WIDE:ROWS_OUT, :].astype(BF)


def layer_forward(l, group, flat, wt, dn, gains, xin, xout, saved):
    mid, qs, ks, vs, probs, mixs, acts, gps = saved
    masks = [head_mask(h).astype(BF) for h in range(HEADS)]
    (gain1, shift1, out_bias, gain2, shift2, down_bias), up_bias = layer_vectors(flat, l)
    for k, value in enumerate((gain1, shift1, gain2, shift2)):
        gains[k : k + 1, :] = value

    def body(tq, tk):
        x = xin[0:tq, :]
        xhat, _ = norm_stats(x)
        n1 = (xhat * gain1 + shift1).astype(BF)
        q = (dot(n1, wt[0, 0:D, :], NT) * HD ** (-0.5)).astype(BF)
        k = dot(n1, wt[0, D : 2 * D, :], NT).astype(BF)
        v = dot(n1, wt[0, 2 * D : 3 * D, :], NT).astype(BF)
        qs[0:tq, :] = q
        ks[0, 0:tq, :] = k
        vs[0, 0:tq, :] = v
        ks[0, tq:tk, :] = jnp.zeros((tk - tq, D), BF)
        vs[0, tq:tk, :] = jnp.zeros((tk - tq, D), BF)
        valid = key_mask(length_of(group), tk)
        kk = ks[0, 0:tk, :]
        vv = vs[0, 0:tk, :]
        mix = None
        for h in range(HEADS):
            s = dot(q * masks[h], kk, NT)
            s = jnp.where(valid, s, MASKED)
            p = softmax_rows(s)
            p = p.astype(BF)
            probs[0, h, 0:tq, 0:tk] = p
            part = dot(p, vv * masks[h], NN)
            mix = part if mix is None else mix + part
        mix = mix.astype(BF)
        mixs[0:tq, :] = mix
        middle = x + dot(mix, wt[0, 3 * D : 4 * D, :], NT) + out_bias
        mid[0:tq, :] = middle
        xhat2, _ = norm_stats(middle)
        n2 = (xhat2 * gain2 + shift2).astype(BF)
        up = dot(n2, wt[0, 4 * D : WIDE, :], NT) + up_bias
        t = jnp.tanh(GELU_C * (up + GELU_K * (up * up * up)))
        half = 0.5 * (1.0 + t)
        act = (up * half).astype(BF)
        slope = half + 0.5 * up * (1.0 - t * t) * (GELU_C * (1.0 + 3.0 * GELU_K * (up * up)))
        gps[0:tq, :] = slope.astype(BF)
        acts[0:tq, :] = act
        xout[0:tq, :] = middle + dot(act, dn[0], NN) + down_bias
        if tq < TQ:
            xout[tq:TQ, :] = jnp.zeros((TQ - tq, D), F32)

    by_size(group, body)


def start_kernel(devices, share, column_width, row_width, places, n_pieces, groups, me, *refs):
    pieces, patches = refs[:n_pieces], refs[n_pieces]
    x0, mid, qs, ks, vs, probs, mixs, acts, gps, x1, gains, wt, dn, flat = refs[
        n_pieces + 1 : n_pieces + 15
    ]
    blocks, weights, asm, tmp, pw, pos, emb = refs[n_pieces + 15 :]
    image = pl.program_id(0)
    pl.when(image == 0)(
        lambda: unpack_start(
            devices, share, column_width, row_width, places, me[0], pieces, wt, dn, flat, blocks, weights,
            asm, tmp, pw, pos, emb,
        )
    )
    cls = flat_vec(flat, CLS_AT, D)
    patch_b = flat_vec(flat, PATCH_B_AT, D)
    e = dot(patches[0], emb[...], NN) + patch_b + rows192(pos, 8, PATCHES)
    x0[0:PATCH_AT, :] = jnp.concatenate(
        [cls + rows192(pos, 7, 1), jnp.zeros((PATCH_AT - 1, D), F32)], 0
    )
    x0[PATCH_AT : PATCH_AT + PATCHES, :] = e
    x0[PATCH_AT + PATCHES :, :] = jnp.zeros((TQ - PATCH_AT - PATCHES, D), F32)
    layer_forward(
        0, groups[image], flat, wt, dn, gains, x0, x1, (mid, qs, ks, vs, probs, mixs, acts, gps)
    )


def unpack_start(
    devices, share, column_width, row_width, places, me, pieces, wt, dn, flat, blocks, weights, asm, tmp,
    pw, pos, emb,
):
    inner_masks, outer_masks, top = places
    rows, weight_rows = blocks.shape[1], weights.shape[1]
    body = rows + weight_rows
    step = body if top is not None else body + rows
    for k, outer in enumerate(outer_masks):
        piece = pieces[k // pieces[0].shape[0]].at[k % pieces[0].shape[0]]
        for j, inner in enumerate(inner_masks):
            d = me ^ (outer | inner)
            at = j * step
            value = piece[at : at + rows, :].astype(F32)
            if top is None:
                value = value + piece[at + body : at + body + rows, :].astype(F32)
            blocks[d] = value
            weights[d] = piece[at + rows : at + body, :]
        if top is not None:
            d = top | ((me ^ outer) & 7)
            at = len(inner_masks) * step
            blocks[d] = blocks[d] + piece[at : at + rows, :].astype(F32)
    unpack_flat(blocks, flat, tmp, devices, share)
    unpack_weights(weights, 1, column_width, row_width, asm, wt, dn)
    unpack_pairs(flat, 0, PATCH_DIM // 2, pw, 0)
    unpack_pairs(flat, POS_AT // 128, SEQ // 2, pos, 7)
    last = flat_vec(flat, POS_AT + (SEQ - 1) * D, D)
    pos[0, 7 + SEQ - 1 : 7 + SEQ, :] = last[:, 0:128]
    pos[1, 7 + SEQ - 1 : 7 + SEQ, 0:64] = last[:, 128:192]
    emb[...] = rows192(pw, 0, PATCH_DIM).astype(BF)


def forward_kernel(
    total_images, images, column_width, row_width, masks, n_pieces, groups, labels, me, flat, x1, *refs
):
    pieces = refs[:n_pieces]
    mid, qs, ks, vs, probs, mixs, acts, gps, gains, *rest = refs[n_pieces:]
    gstream, kv, factors, small, wt_all, dn_all, weights, asm, hw, x2 = rest[:10]
    image = pl.program_id(0)

    @pl.when(image == 0)
    def _():
        inner = pieces[0].shape[0]
        for k in range(n_pieces):
            for j in range(inner):
                weights[me[0] ^ masks[k * inner + j]] = pieces[k][j]
        unpack_weights(weights, 2, column_width, row_width, asm, wt_all, dn_all)
        unpack_head(flat, hw)
        factors[...] = jnp.zeros_like(factors)

    layer_forward(
        1,
        groups[image],
        flat,
        wt_all,
        dn_all,
        gains,
        x1,
        x2.at[image_rows(image)],
        (mid, qs, ks, vs, probs, mixs, acts, gps),
    )
    pl.when(image == images - 1)(
        lambda: last_layer(
            total_images, images, groups, labels, flat, gstream, kv, factors, small, wt_all.at[1],
            dn_all.at[1], hw, x2, *rest[10:],
        )
    )


def last_layer(
    total_images, images, groups, labels, flat, gstream, kv, factors, small, wt, dn, hw, x2, kbuf, vbuf,
    dkbuf, dvbuf, clsbuf, qcls, mixcls, dmixcls, dqcls, midgrad, n1low,
):
    l = 2
    (gain1, shift1, out_bias, gain2, shift2, down_bias), up_bias = layer_vectors(flat, l)
    wk = wt[D : 2 * D, :]
    wv = wt[2 * D : 3 * D, :]
    clsbuf[...] = jnp.zeros_like(clsbuf)
    mixcls[...] = jnp.zeros_like(mixcls)
    kbuf[:, TQ:TK, :] = jnp.zeros((images, TK - TQ, D), BF)
    vbuf[:, TQ:TK, :] = jnp.zeros((images, TK - TQ, D), BF)

    def keys(i, carry):
        rows = image_rows(i)
        xhat, _ = norm_stats(x2[rows, :])
        n1 = (xhat * gain1 + shift1).astype(BF)
        kbuf[i, 0:TQ, :] = dot(n1, wk, NT).astype(BF)
        vbuf[i, 0:TQ, :] = dot(n1, wv, NT).astype(BF)
        clsbuf[pl.ds(i, 1), :] = x2[pl.ds(i * TQ + CLS_ROW, 1), :]
        return carry

    for i in range(images):
        keys(i, 0)
    xc = clsbuf[...]
    xhat1c, rstd1c = norm_stats(xc)
    n1c = (xhat1c * gain1 + shift1).astype(BF)
    qc = (dot(n1c, wt[0:D, :], NT) * HD ** (-0.5)).astype(BF)
    qcls[...] = qc.astype(F32)
    mask3 = jnp.concatenate([head_mask(h) for h in range(HEADS)] + [jnp.zeros((13, D), F32)], 0)

    def cls_probs(i):
        q3 = (qcls[pl.ds(i, 1), :] * mask3).astype(BF)
        s = dot(q3, kbuf[i], NT)
        s = jnp.where(key_mask(length_of(groups[i]), TK), s, MASKED)
        return q3, softmax_rows(s)

    def attend(i, carry):
        q3, p = cls_probs(i)
        m = dot(p.astype(BF), vbuf[i], NN)
        mixcls[pl.ds(i, 1), :] = colsum(m * mask3)
        return carry

    for i in range(images):
        attend(i, 0)
    mixc = mixcls[...].astype(BF)
    midc = xc + dot(mixc, wt[3 * D : 4 * D, :], NT) + out_bias
    xhat2c, rstd2c = norm_stats(midc)
    n2c = (xhat2c * gain2 + shift2).astype(BF)
    upc = dot(n2c, wt[4 * D : WIDE, :], NT) + up_bias
    tc = jnp.tanh(GELU_C * (upc + GELU_K * (upc * upc * upc)))
    halfc = 0.5 * (1.0 + tc)
    actc = (upc * halfc).astype(BF)
    gpc = halfc + 0.5 * upc * (1.0 - tc * tc) * (GELU_C * (1.0 + 3.0 * GELU_K * (upc * upc)))
    outc = midc + dot(actc, dn[...], NN) + down_bias

    fgain = flat_vec(flat, FINAL_AT, D)
    fshift = flat_vec(flat, FINAL_AT + D, D)
    head_b = jnp.concatenate(
        [flat_vec(flat, HEAD_B_AT, CLASSES), jnp.zeros((1, CLASSES_PAD - CLASSES), F32)], 1
    )
    row16 = lax.broadcasted_iota(jnp.int32, (16, 1), 0)
    real = (row16 < images).astype(F32)
    xhatf, rstdf = norm_stats(outc)
    flow = (xhatf * fgain + fshift).astype(BF)
    head_low = jnp.concatenate([hw[k, 0:D, :] for k in range(8)], 1).astype(BF)
    cls_lane = lanes((16, CLASSES_PAD))
    logits = dot(flow, head_low, NN) + head_b
    logits = jnp.where(cls_lane < CLASSES, logits, MASKED)
    top = jnp.max(logits, -1, keepdims=True)
    e = jnp.exp(logits - top)
    total = jnp.sum(e, -1, keepdims=True)
    label = jnp.zeros((16, 1), jnp.int32)
    for i in range(images):
        label = jnp.where(row16 == i, labels[i], label)
    onehot = (cls_lane == label).astype(F32)
    picked = jnp.sum(jnp.where(cls_lane == label, logits, 0.0), -1, keepdims=True)
    loss = jnp.sum((top + jnp.log(total) - picked) * real, 0, keepdims=True)
    dlogits = (e / total - onehot) * (real / total_images)
    dlow = dlogits.astype(BF)
    dflow = dot(dlow, head_low, NT)
    put_factor(factors, FACTOR_FLOW, flow, images)
    put_factor(factors, FACTOR_DLOGITS, dlow, images)
    small[...] = jnp.zeros_like(small)
    exact = [jnp.broadcast_to(loss, (1, 128))]
    head_bias_grad = colsum(dlogits)
    exact += [head_bias_grad[:, 128 * k : 128 * (k + 1)] for k in range(8)]
    for value in (colsum(dflow * xhatf), colsum(dflow)):
        value = jnp.concatenate([value, jnp.zeros((1, 64), F32)], 1)
        exact += [value[:, 0:128], value[:, 128:256]]
    for k, value in enumerate(exact):
        factors[k : k + 1, :] = value
    gout = norm_back(dflow, xhatf, rstdf, fgain) * real

    ol = gout.astype(BF)
    dact = dot(ol, dn[...], NT)
    dup = dact * gpc * real
    ul = dup.astype(BF)
    dn2 = dot(ul, wt[4 * D : WIDE, :], NN)
    dmid = norm_back(dn2, xhat2c, rstd2c, gain2) + gout
    ml = dmid.astype(BF)
    small[4:5, 0:FF] = colsum(dup)
    small[10:11, 0:D] = colsum(dmid)
    small[11:12, 0:D] = colsum(dn2 * xhat2c)
    small[12:13, 0:D] = colsum(dn2)
    small[13:14, 0:D] = colsum(gout)
    dmixcls[...] = dot(ml, wt[3 * D : 4 * D, :], NN).astype(BF).astype(F32)
    dqcls[...] = jnp.zeros_like(dqcls)

    def attend_back(i, carry):
        q3, p = cls_probs(i)
        dm3 = (dmixcls[pl.ds(i, 1), :] * mask3).astype(BF)
        dp = dot(dm3, vbuf[i], NT)
        dv = dot(p.astype(BF), dm3, TN)
        ds = (p * (dp - jnp.sum(p * dp, -1, keepdims=True))).astype(BF)
        dq = dot(ds, kbuf[i], NN)
        dk = dot(ds, q3, TN)
        rows = image_rows(i)
        dkbuf[rows, :] = dk[0:TQ].astype(BF)
        dvbuf[rows, :] = dv[0:TQ].astype(BF)
        dqcls[pl.ds(i, 1), :] = colsum(dq * mask3) * HD ** (-0.5)
        return carry

    for i in range(images):
        attend_back(i, 0)
    dql = dqcls[...].astype(BF)
    dn1c = dot(dql, wt[0:D, :], NN)
    midgrad[...] = dmid
    dqcls[...] = dn1c
    for k, value in enumerate((ol, n2c, ml, mixc, dql, n1c)):
        put_factor(factors, 2 * k, value, images)
    for k, value in enumerate((actc, ul)):
        put_factor(factors, 12 + 6 * k, value, images)

    def stream_back(i, carry):
        dgain, dshift = carry
        rows = image_rows(i)
        xhat, rstd = norm_stats(x2[rows, :])
        n1low[rows, :] = (xhat * gain1 + shift1).astype(BF)
        dkl = dkbuf[rows, :]
        dvl = dvbuf[rows, :]
        dn1 = dot(dkl, wk, NN) + dot(dvl, wv, NN)
        at_cls = lax.broadcasted_iota(jnp.int32, (TQ, 1), 0) == CLS_ROW
        dn1 = dn1 + jnp.where(at_cls, dqcls[pl.ds(i, 1), :], 0.0)
        gin = norm_back(dn1, xhat, rstd, gain1)
        gstream[rows, :] = gin + jnp.where(at_cls, midgrad[pl.ds(i, 1), :], 0.0)
        return (dgain + colsum(dn1 * xhat), dshift + colsum(dn1))

    zero_row = jnp.zeros((1, D), F32)
    dgain, dshift = zero_row, zero_row
    for i in range(images):
        dgain, dshift = stream_back(i, (dgain, dshift))
    dwk = dot(dkbuf[...], n1low[...], TN)
    dwv = dot(dvbuf[...], n1low[...], TN)
    small[8:9, 0:D] = dgain
    small[9:10, 0:D] = dshift
    kv[0:D, :] = dwk[:, 0:128]
    kv[D : 2 * D, :] = dwv[:, 0:128]
    kv[2 * D :, 0:64] = dwk[:, 128:192]
    kv[2 * D :, 64:128] = dwv[:, 128:192]


def layer_back(
    images,
    group,
    x,
    mid,
    qs,
    ks,
    vs,
    probs,
    mixs,
    acts,
    gps,
    gains,
    gout,
    wt,
    dn,
    gin,
    gt,
    vec,
    upb,
    olbuf,
    ulbuf,
    n2buf,
    mlbuf,
    n1buf,
    dqbuf,
    dkbuf,
    dvbuf,
    mixbuf,
    actbuf,
):
    gain1, shift1, gain2, shift2 = [gains[k : k + 1, :] for k in range(4)]
    masks = [head_mask(h).astype(BF) for h in range(HEADS)]
    image = pl.program_id(0)
    start = pl.multiple_of(image * TQ, 16)

    @pl.when(image == 0)
    def _():
        vec[...] = jnp.zeros_like(vec)
        upb[...] = jnp.zeros_like(upb)

    def body(tq, tk):
        rows = pl.ds(start, tq)
        go = gout[0:tq, :]
        ol = go.astype(BF)
        olbuf[rows, :] = ol
        actbuf[rows, :] = acts[0:tq, :]
        mixbuf[rows, :] = mixs[0:tq, :]
        dact = dot(ol, dn[0], NT)
        dup = dact * gps[0:tq, :].astype(F32)
        ul = dup.astype(BF)
        ulbuf[rows, :] = ul
        dn2 = dot(ul, wt[0, 4 * D : WIDE, :], NN)
        xhat2, rstd2 = norm_stats(mid[0:tq, :])
        n2buf[rows, :] = (xhat2 * gain2 + shift2).astype(BF)
        dmid = norm_back(dn2, xhat2, rstd2, gain2) + go
        ml = dmid.astype(BF)
        mlbuf[rows, :] = ml
        upb[0:1, :] += colsum(dup)
        vec[2:3, :] += colsum(dmid)
        vec[3:4, :] += colsum(dn2 * xhat2)
        vec[4:5, :] += colsum(dn2)
        vec[5:6, :] += colsum(go)
        dmix = dot(ml, wt[0, 3 * D : 4 * D, :], NN).astype(BF)
        q = qs[0:tq, :]
        kk = ks[0, 0:tk, :]
        vv = vs[0, 0:tk, :]
        dq = dk = dv = None
        for h in range(HEADS):
            qh = q * masks[h]
            dmh = dmix * masks[h]
            low = probs[0, h, 0:tq, 0:tk]
            p = low.astype(F32)
            dp = dot(dmh, vv, NT)
            t = p * dp
            ds = (t - p * jnp.sum(t, -1, keepdims=True)).astype(BF)
            dv_h = dot(low, dmh, TN)
            dq_h = dot(ds, kk * masks[h], NN)
            dk_h = dot(ds, qh, TN)
            dq, dk, dv = (dq_h, dk_h, dv_h) if dq is None else (dq + dq_h, dk + dk_h, dv + dv_h)
        dql = (dq * HD ** (-0.5)).astype(BF)
        dkl = dk[0:tq].astype(BF)
        dvl = dv[0:tq].astype(BF)
        dqbuf[rows, :] = dql
        dkbuf[rows, :] = dkl
        dvbuf[rows, :] = dvl
        dn1 = (
            dot(dql, wt[0, 0:D, :], NN)
            + dot(dkl, wt[0, D : 2 * D, :], NN)
            + dot(dvl, wt[0, 2 * D : 3 * D, :], NN)
        )
        xhat1, rstd1 = norm_stats(x[0:tq, :])
        n1buf[rows, :] = (xhat1 * gain1 + shift1).astype(BF)
        vec[0:1, :] += colsum(dn1 * xhat1)
        vec[1:2, :] += colsum(dn1)
        gin[0:tq, :] = norm_back(dn1, xhat1, rstd1, gain1) + dmid
        if tq < TQ:
            rest = pl.ds(start + tq, TQ - tq)
            gin[tq:TQ, :] = jnp.zeros((TQ - tq, D), F32)
            for ref in (olbuf, ulbuf, n2buf, mlbuf, n1buf, dqbuf, dkbuf, dvbuf, mixbuf, actbuf):
                ref[rest, :] = jnp.zeros((TQ - tq, ref.shape[1]), BF)

    by_size(group, body)

    @pl.when(image == images - 1)
    def _():
        store_layer_grads(
            gt,
            [
                (0, dot(dqbuf[...], n1buf[...], TN)),
                (D, dot(dkbuf[...], n1buf[...], TN)),
                (2 * D, dot(dvbuf[...], n1buf[...], TN)),
                (3 * D, dot(mlbuf[...], mixbuf[...], TN)),
                (4 * D, dot(ulbuf[...], n2buf[...], TN)),
                (WIDE, dot(actbuf[...], olbuf[...], TN)),
            ],
        )


def share_halves(gt, keep, send, mine):
    half = keep.shape[0]
    keep[...] = gt[pl.ds(pl.multiple_of(mine * half, 8), half), :]
    send[...] = gt[pl.ds(pl.multiple_of((1 - mine) * half, 8), half), :]


def middle_kernel(images, groups, me, *refs):
    inputs, (kv, small) = refs[:13], refs[13:15]
    gin, keep, send, vec, upb, gt, *buffers = refs[15:]
    image = pl.program_id(0)
    layer_back(images, groups[image], *inputs, gin, gt, vec, upb, *buffers)

    @pl.when(image == images - 1)
    def _():
        gt[PACKED:VEC_KEPT, :] = kv[...]
        gt[VEC_KEPT:, :] = jnp.zeros((MIDDLE_ROWS - VEC_KEPT, 128), F32)
        put = functools.partial(put_entries, gt, VEC_KEPT - VEC_ROW)
        put_vectors(put, 1, vec, upb[0:1, :])
        put_vectors(put, 2, small[8:14, :], small[4:5, 0:FF])
        share_halves(gt, keep, send, me[0] & 1)


def first_kernel(images, groups, me, *refs):
    inputs, patches = refs[:13], refs[13]
    keep, send, gt, gin, vec, upb, pgrad, posgrad, *buffers = refs[14:]
    image = pl.program_id(0)
    layer_back(images, groups[image], *inputs, gin, gt, vec, upb, *buffers)

    @pl.when(image == 0)
    def _():
        pgrad[...] = jnp.zeros_like(pgrad)
        posgrad[...] = jnp.zeros_like(posgrad)

    g = gin[...]
    used = PATCH_AT + PATCHES
    posgrad[0, 0:used, :] += g[0:used, 0:128]
    posgrad[1, 0:used, 0:64] += g[0:used, 128:192]
    pg = dot(patches[0], g[PATCH_AT:used].astype(BF), TN)
    pgrad[0] += pg[:, 0:128]
    pgrad[1, :, 0:64] += pg[:, 128:192]
    pl.when(image == images - 1)(
        lambda: pack_first(keep, send, gt, vec, upb, pgrad, posgrad, me[0] & 1)
    )


def put_vectors(put, l, six, up):
    at = VEC_AT + l * VEC_LAYER
    for k in range(6):
        row = jnp.concatenate([six[k : k + 1, 0:D], jnp.zeros((1, 64), F32)], 1)
        put(at + k * D, row, D)
    put(at + 6 * D, up, FF)


def pack_first(keep, send, gt, vec, upb, pgrad, posgrad, core):
    def pos_rows(at):
        return jnp.concatenate([posgrad[0, at : at + 1, :], posgrad[1, at : at + 1, :]], 1)

    cls_row = pos_rows(CLS_ROW)
    patch_b = jnp.concatenate(
        [colsum(posgrad[k, PATCH_AT : PATCH_AT + PATCHES, :]) for k in range(2)], 1
    )
    posgrad[0, 7:8, :] = cls_row[:, 0:128]
    posgrad[1, 7:8, :] = cls_row[:, 128:256]
    base = PACKED + PATCH_ROWS
    gt[base:, :] = jnp.zeros((FIRST_ROWS - base, 128), F32)
    pack_pairs(pgrad, 0, gt, PACKED, PATCH_DIM // 2)
    pack_pairs(posgrad, 7, gt, base + POS_AT // 128 - TAIL_ROW, SEQ // 2)
    put = functools.partial(put_entries, gt, base - TAIL_ROW)
    put(CLS_AT, cls_row, D)
    put(PATCH_B_AT, patch_b, D)
    put(POS_AT + (SEQ - 1) * D, pos_rows(7 + SEQ - 1), D)
    put_vectors(put, 0, vec, upb[0:1, :])
    share_halves(gt, keep, send, core)


def parts(a):
    high = a.astype(BF)
    return high, (a - high.astype(F32)).astype(BF)


def parts_dot(a, b, how):
    return dot(a[0], b[0], how) + (dot(a[0], b[1], how) + dot(a[1], b[0], how))


def split_dot(a, b, how):
    return parts_dot(parts(a), parts(b), how)


def own_rows(ref, l, at, width):
    if width % 8 == 0:
        return ref[l, pl.ds(pl.multiple_of(at, 8), width), :]
    rows = -(-(width + 7) // 8) * 8
    base = pl.multiple_of((at // 8) * 8, 8)
    x = ref[l, pl.ds(base, rows), :]
    return pltpu.roll(x, lax.rem(rows - (at - base), rows), 0)[:width]


def coefficient_kernel(devices, gathered, basis, exact, extra):
    total = gathered[0]
    for d in range(1, devices):
        total = total + gathered[d]
    exact[...] = total
    c = split_dot(jnp.broadcast_to(block_row(exact), (8, BLOCK_PAD)), basis[...], NT)[0:1, :]
    extra[...] = jnp.zeros_like(extra)
    for k in range(3):
        high = c.astype(BF).astype(F32)
        extra[k : k + 1, 0:BASIS] = high
        c = c - high


def late_kernel(devices, images, gathered, g2, headflat, hg):
    rows = gathered.shape[0] // devices

    def factor(block, count):
        columns = []
        for b in range(block, block + count):
            parts = [
                gathered[pl.ds(EXACT_ROWS + b * images + i, devices, stride=rows), :]
                for i in range(images)
            ]
            columns.append(jnp.concatenate(parts, 0))
        return jnp.concatenate(columns, 1).astype(BF)

    ol, n2, ml, mix, dq, n1 = [factor(2 * k, 2)[:, 0:D] for k in range(6)]
    act, ul = factor(12, 6), factor(18, 6)
    g2[0:D, :] = dot(dq, n1, TN)
    g2[3 * D : 4 * D, :] = dot(ml, mix, TN)
    g2[4 * D : WIDE, :] = dot(ul, n2, TN)
    g2[WIDE:, :] = dot(act, ol, TN)
    flow = factor(FACTOR_FLOW, 2)[:, 0:D]
    for k in range(8):
        hg[k, 0:D, :] = dot(flow, factor(FACTOR_DLOGITS + k, 1), TN)
    hg[:, D:, :] = jnp.zeros((8, HEAD_ROOM - D, 128), F32)
    pack_head(hg, headflat)


def block_row(exact):
    pieces = [
        jnp.concatenate([exact[at : at + 1, :], exact[at + 1 : at + 2, 0:64]], 1) for at in (9, 11)
    ]
    pieces += [exact[1 + k : 2 + k, :] for k in range(8)]
    return jnp.concatenate(pieces, 1)


def unpack_layer(src, out, l, which):
    half = ROWS_OUT // 2
    for c in range(18):
        out[l, c * 128 : (c + 1) * 128, 0:128] = src[c * 128 : (c + 1) * 128, :].astype(F32)
    for c in range(9):
        g = src[ROWS_OUT + c * 128 : ROWS_OUT + (c + 1) * 128, :].astype(F32)
        out[l, c * 128 : (c + 1) * 128, 128:192] = g[:, 0:64]
        out[l, half + c * 128 : half + (c + 1) * 128, 128:192] = g[:, 64:128]


def square_rows(ref, start, stop, acc):
    step = 64
    for at in range(start, stop, step):
        g = ref[at : min(at + step, stop), :].astype(F32)
        g = g * g
        for lane in range(0, g.shape[1], 128):
            part = g[:, lane : lane + 128]
            rows = part.shape[0]
            part = jnp.sum(part.reshape(rows // 8, 8, part.shape[1]), 0)
            if part.shape[1] < 128:
                part = jnp.concatenate([part, jnp.zeros((8, 128 - part.shape[1]), F32)], 1)
            acc = acc + part
    return acc


def total_of(x):
    return jnp.sum(jnp.sum(x, 0, keepdims=True), 1, keepdims=True)


def muon_kernel(column_width, row_width, n_pieces, place, *refs):
    pieces = refs[:n_pieces]
    (
        g2,
        headflat,
        exact,
        basis,
        mom_far,
        wide_w,
        wide_mom,
        down_w,
        down_mom,
    ) = refs[n_pieces : n_pieces + 9]
    (
        wide_new,
        wide_mom_new,
        wide_copy,
        down_new,
        down_mom_new,
        down_copy,
        share_grad,
        scal,
        flat,
        mid_rows,
        first_rows,
        coef,
        gfull,
        mats,
        powers,
        mom,
        mom_sem,
    ) = refs[n_pieces + 9 :]
    wide_at, down_at, mine = place[2], place[3], place[4]
    start = pl.multiple_of(place[0], 192)
    count = place[1]
    inner = pieces[0].shape[0]
    total_pieces = n_pieces * inner
    mr, fr = MIDDLE_ROWS // total_pieces, FIRST_ROWS // total_pieces

    mom_copies = [
        pltpu.make_async_copy(mom_far.at[:, l], mom.at[l], mom_sem.at[l]) for l in range(LAYERS)
    ]
    for copy in mom_copies:
        copy.start()

    for k in range(n_pieces):
        for z in range(inner):
            at = mine ^ (k * inner + z)
            mid_rows[pl.ds(pl.multiple_of(at * mr, 16), mr), :] = pieces[k][z, 0:mr, :]
            first_rows[pl.ds(pl.multiple_of(at * fr, 16), fr), :] = pieces[k][z, mr : mr + fr, :]
            coef[pl.ds(pl.multiple_of(at * 16, 16), 16), :] = pieces[k][
                z, mr + fr : mr + fr + 16, :
            ].astype(F32)
    unpack_layer(first_rows, gfull, 0, 0)
    unpack_layer(mid_rows, gfull, 1, 1)
    gfull[2, 0:D, :] = g2[0:D, :]
    gfull[2, 3 * D : ROWS_OUT, :] = g2[3 * D :, :]
    gfull[2, D : 3 * D, 0:128] = mid_rows[PACKED : PACKED + 2 * D, :].astype(F32)
    tail = mid_rows[PACKED + 2 * D : PACKED + 3 * D, :].astype(F32)
    gfull[2, D : 2 * D, 128:192] = tail[:, 0:64]
    gfull[2, 2 * D : 3 * D, 128:192] = tail[:, 64:128]

    base = PACKED + PATCH_ROWS
    flat[0:PATCH_ROWS, :] = first_rows[PACKED:base, :].astype(F32)
    flat[PATCH_ROWS : PATCH_ROWS + HEAD_ROWS, :] = headflat[0:HEAD_ROWS, :]
    tail = first_rows[base:FIRST_ROWS, :].astype(F32)
    vectors = mid_rows[VEC_KEPT : VEC_KEPT + 32, :].astype(F32)
    flat[TAIL_ROW:VEC_ROW, :] = tail[0 : TAIL_ROWS - 1]
    flat[VEC_ROW : VEC_ROW + 1, :] = tail[TAIL_ROWS - 1 : TAIL_ROWS] + vectors[0:1]
    flat[VEC_ROW + 1 : VEC_ROW + VEC_ROWS, :] = vectors[1:VEC_ROWS]
    used = VEC_ROW + VEC_ROWS
    flat[used:, :] = jnp.zeros((flat.shape[0] - used, 128), F32)
    block = block_row(exact)

    sums = jnp.zeros((16, 128), F32)
    for at in range(total_pieces):
        sums = sums + coef[16 * at : 16 * (at + 1), :]
    c = sums[0:1, :] + sums[1:2, :] + sums[2:3, :]
    acc = jnp.zeros((8, 128), F32)
    acc = square_rows(first_rows, 0, PACKED, acc)
    acc = square_rows(mid_rows, 0, VEC_KEPT, acc)
    acc = square_rows(g2, 0, D, acc)
    acc = square_rows(g2, 3 * D, ROWS_OUT, acc)
    acc = square_rows(flat, 0, flat.shape[0], acc)
    squares = total_of(acc) + total_of(jnp.where(lanes((1, BLOCK_PAD)) < 2 * D + CLASSES, block * block, 0.0))
    coef_square = jnp.sum(c * c, 1, keepdims=True)
    norm = jnp.sqrt(squares - coef_square)
    factor = CLIP_AT / jnp.maximum(norm, CLIP_AT)
    scal[...] = jnp.zeros_like(scal)
    for k, value in enumerate((norm, factor, jnp.sqrt(coef_square), exact[0:1, 0:1], c)):
        scal[k : k + 1, :] = jnp.broadcast_to(value, (1, 128))

    block = block - split_dot(
        jnp.broadcast_to(c[:, 0:BASIS], (8, BASIS)), basis[...], NN
    )[0:1, :]
    put_entries(flat, 0, FINAL_AT, block, 2 * D + CLASSES)
    rows = share_grad.shape[0]
    at, shift = place[5], place[6]
    base_row = pl.multiple_of((at // 8) * 8, 8)
    off = at - base_row
    window = flat[pl.ds(base_row, rows + 16), :]
    here = pltpu.roll(window, lax.rem(rows + 16 - off, rows + 16), 0)
    there = pltpu.roll(window, lax.rem(rows + 15 - off, rows + 16), 0)[0:rows]
    here = here[0:rows]
    back = lax.rem(128 - shift, 128)
    g = jnp.where(
        lanes((rows, 128)) < 128 - shift, pltpu.roll(here, back, 1), pltpu.roll(there, back, 1)
    )
    share_grad[...] = g * factor

    row = lax.broadcasted_iota(jnp.int32, (FF, 1), 0)
    sizes = []
    eye = (
        lax.broadcasted_iota(jnp.int32, (D, D), 0) == lax.broadcasted_iota(jnp.int32, (D, D), 1)
    ).astype(F32)
    own = []
    for k in range(2 * LAYERS):
        l, which = divmod(k, 2)
        if which == 0:
            mom_copies[l].wait()
            m = mom[l, pl.ds(start // column_width, FF // column_width), 0:column_width, :]
            m = BETA_ONE * m.reshape(FF, D) + factor * gfull[l, pl.ds(start, FF), :]
            m = jnp.where(row < count, m, 0.0)
            kept = BETA_ONE * wide_mom[l] + factor * own_rows(gfull, l, wide_at, column_width)
            wide_mom_new[l] = kept
        else:
            m = BETA_ONE * mom[l, :, column_width:, :].reshape(FF, D)
            m = m + factor * gfull[l, WIDE:ROWS_OUT, :]
            kept = BETA_ONE * down_mom[l] + factor * own_rows(gfull, l, down_at, row_width)
            down_mom_new[l] = kept
        size = 1.0 / (jnp.sqrt(total_of(m * m)) + SHAPE_EPS)
        high, low = parts(m * size)
        cross = dot(high, low, TN)
        mats[k] = dot(high, high, TN) + (cross + cross.T)
        n = kept.shape[0]
        if n < powers.shape[1]:
            powers[k] = jnp.zeros(powers.shape[1:], F32)
        powers[k, 0:n, :] = kept * size

    def polynomial(k):
        a = parts(mats[k])
        cross = dot(a[0], a[1], NN)
        b = dot(a[0], a[0], NN) + (cross + cross.T)
        return a, 3.4445 * eye - 4.775 * mats[k] + 2.0315 * b

    def step(it, carry):
        polys = [polynomial(k) for k in range(2 * LAYERS)]
        ps = [parts(p) for _, p in polys]
        ts = [parts_dot(p, a, NN) for (a, _), p in zip(polys, ps)]
        for k in range(2 * LAYERS):
            both = parts_dot(parts(jnp.concatenate([ts[k], powers[k]], 0)), ps[k], NN)
            mats[k] = both[0:D]
            powers[k] = both[D:]
        return carry

    lax.fori_loop(0, 4, step, 0)
    side = jnp.where(count == 4 * D, 768.0, jnp.where(count == 3 * D, 576.0, 192.0))
    rate = jnp.sqrt(jnp.full((1, 1), 1.0, F32) * side) * (MUON_RATE * 0.2)
    for k in range(2 * LAYERS):
        l, which = divmod(k, 2)
        _, p = polynomial(k)
        update = parts_dot(parts(powers[k]), parts(p), NN)
        if which == 0:
            new = wide_w[l] - rate * update[0:column_width]
            wide_new[l] = new
            wide_copy[l] = new.astype(BF)
        else:
            new = down_w[l] - (MUON_RATE * 0.2 * FF**0.5) * update[0:row_width]
            down_new[l] = new
            down_copy[l] = new.astype(BF)


def cost(micros):
    return pl.CostEstimate(
        flops=int(micros * 1.15e9), bytes_accessed=int(micros * 1e6), transcendentals=0
    )


def pad_rows(x, rows):
    return jnp.pad(x, (0, rows * 128 - x.shape[0])).reshape(rows, 128)


def pack_shard(wide_t, down):
    rows = jnp.concatenate([wide_t, down], 1)
    rows = rows.reshape(-1, D).astype(BF)
    a_rows, h = half_rows(rows.shape[0])
    head = jnp.pad(rows[:, :128], ((0, a_rows - rows.shape[0]), (0, 0)))
    tail = jnp.pad(rows[:, 128:], ((0, 2 * h - rows.shape[0]), (0, 0)))
    tail = jnp.concatenate([tail[:h], tail[h:]], 1)
    fill = -(a_rows + h) % 16
    return jnp.concatenate([head, tail] + ([jnp.zeros((fill, 128), BF)] if fill else []), 0)


def stage_masks(stages):
    masks = [0]
    for low, width in reversed(stages):
        masks = [a ^ (m << low) for m in range(1 << width) for a in masks]
    return masks


def gather_stages(arrays, stages, devices, apart=2):
    for depth in reversed(range(len(stages))):
        low, width = stages[depth]
        got = [swap(x, m << low, devices) for m in range(1, 1 << width) for x in arrays]
        arrays = arrays + got
        if depth >= apart:
            arrays = [jnp.concatenate(arrays, 0)]
    return arrays


def combine_kernel(spot, middle_keep, middle_got, first_keep, first_got, own, one, two, three):
    mine = spot[0]
    at = 0
    for keep, got in ((middle_keep, middle_got), (first_keep, first_got)):
        n = keep.shape[0] // 4
        for m, out in enumerate((own, one, two, three)):
            rows = pl.ds(pl.multiple_of((mine ^ m) * n, 16), n)
            out[at : at + n, :] = (keep[rows, :] + got[rows, :]).astype(out.dtype)
        at += n


def swap(x, mask, devices):
    return lax.ppermute(x, AXES, [(i, i ^ mask) for i in range(devices)])


def local(
    patches,
    groups,
    labels,
    wide_w,
    down_w,
    plain,
    wide_mom,
    down_mom,
    plain_first,
    plain_second,
    basis_plain,
):
    devices = lax.axis_size(AXES)
    bits = devices.bit_length() - 1
    me = lax.axis_index(AXES).astype(jnp.int32)
    images = patches.shape[0]
    share = plain.shape[0]
    column_width = wide_w.shape[2]
    row_width = down_w.shape[1]
    vmem = pl.BlockSpec(memory_space=pltpu.VMEM)
    smem = pl.BlockSpec(memory_space=pltpu.SMEM)
    params = pltpu.CompilerParams(vmem_limit_bytes=VMEM_LIMIT)
    S = jax.ShapeDtypeStruct

    number_of = [(0, 1), (1, 2), (3, 2)]
    stages = number_of + ([(5, 2), (7, 1)] if bits == 8 else [(b, 1) for b in range(5, bits)])

    wide_t = jnp.transpose(wide_w, (0, 2, 1))
    plain_rows = -(-(share + 127) // 2048) * 16
    rows = plain_rows
    plain_block = pad_rows(plain, plain_rows)
    high = lax.reduce_precision(plain_block, 8, 7)
    low_half = (plain_block - high).astype(BF)
    weights_one = pack_shard(wide_t[:1], down_w[:1])
    shard_one = jnp.concatenate([high.astype(BF), weights_one, low_half], 0)
    shard_two = pack_shard(wide_t[1:], down_w[1:])
    weight_rows = weights_one.shape[0]

    one = gather_stages([shard_one[None]], stages[2:], devices, 0)[0]
    two = gather_stages([shard_two[None]], stages[2:], devices, 0)
    first_masks = stage_masks(stages[2:])
    top = 3 * devices // 4
    compact = bits == 5 and top * share <= CLS_AT
    body = rows + weight_rows
    if compact:
        low_top = lax.dynamic_index_in_dim(one[:, body:], (me >> 3) ^ 3, 0, keepdims=False)
        one = jnp.concatenate([one[:, :body].reshape(-1, 128), low_top], 0)
    else:
        one = one.reshape(-1, 128)
    one = gather_stages([one[None]], stages[1:2], devices)
    one[0] = one[0] + 0.0 * jnp.max(two[0][:, 0, 0])
    pieces_one = gather_stages([jnp.concatenate(one, 0)], stages[:1], devices)
    two = gather_stages(two, stages[1:2], devices)
    places = (first_masks, stage_masks(stages[:2]), top if compact else None)

    lead = jnp.clip(FINAL_AT - me * share + BLOCK_PAD, 0, share + BLOCK_PAD)
    basis_block = lax.dynamic_slice(
        jnp.pad(basis_plain, ((0, 0), (BLOCK_PAD, BLOCK_PAD))), (0, lead), (BASIS, BLOCK_PAD)
    )

    number = me[None]
    groups = groups.astype(jnp.int32)
    labels = labels.astype(jnp.int32)
    flat_rows = -(-((devices - 1) * share // 128 + rows + 8) // 8) * 8
    n = images * TQ
    saved = [
        S((n, D), F32),
        S((n, D), BF),
        S((images, TK, D), BF),
        S((images, TK, D), BF),
        S((images, HEADS, TQ, TK), BF),
        S((n, D), BF),
        S((n, FF), BF),
        S((n, FF), BF),
    ]
    rows_spec = pl.BlockSpec((TQ, D), lambda i: (i, 0))
    wide_spec = pl.BlockSpec((TQ, FF), lambda i: (i, 0))
    key_spec = pl.BlockSpec((1, TK, D), lambda i: (i, 0, 0))
    patch_spec = pl.BlockSpec((1, PATCHES, PATCH_DIM), lambda i: (i, 0, 0))
    saved_specs = [
        rows_spec,
        rows_spec,
        key_spec,
        key_spec,
        pl.BlockSpec((1, HEADS, TQ, TK), lambda i: (i, 0, 0, 0)),
        rows_spec,
        wide_spec,
        wide_spec,
    ]
    factor_rows = EXACT_ROWS + -(-FACTOR_BLOCKS * images // 8) * 8
    x0, *saved0, x1, gains0, wt0, dn0, flat = pl.pallas_call(
        functools.partial(
            start_kernel, devices, share, column_width, row_width, places, len(pieces_one)
        ),
        grid=(images,),
        out_shape=[S((n, D), F32)]
        + saved
        + [
            S((n, D), F32),
            S((8, D), F32),
            S((1, WIDE, D), BF),
            S((1, FF, D), BF),
            S((flat_rows, 128), F32),
        ],
        in_specs=[smem] * 2 + [vmem] * len(pieces_one) + [patch_spec],
        out_specs=[rows_spec] + saved_specs + [rows_spec] + [vmem] * 4,
        scratch_shapes=[
            pltpu.VMEM((devices, rows, 128), F32),
            pltpu.VMEM((devices, weight_rows, 128), BF),
            pltpu.VMEM((ROWS_OUT, D), F32),
            pltpu.VMEM((4, rows + 8, 128), F32),
            pltpu.VMEM((2, PATCH_DIM, 128), F32),
            pltpu.VMEM((2, TQ + 8, 128), F32),
            pltpu.VMEM((PATCH_DIM, D), BF),
        ],
        compiler_params=params,
        cost_estimate=cost(20),
        name="start",
    )(groups, number, *pieces_one, patches)

    two, x1 = lax.optimization_barrier((two, x1))
    pieces_two = gather_stages(two, stages[:1], devices)
    *saved1, gains1, gstream, kv, factors, small, wt12, dn12 = pl.pallas_call(
        functools.partial(
            forward_kernel,
            float(images * devices),
            images,
            column_width,
            row_width,
            stage_masks(stages),
            len(pieces_two),
        ),
        grid=(images,),
        out_shape=saved
        + [
            S((8, D), F32),
            S((n, D), F32),
            S((3 * D, 128), F32),
            S((factor_rows, 128), F32),
            S((16, CLASSES_PAD), F32),
            S((2, WIDE, D), BF),
            S((2, FF, D), BF),
        ],
        in_specs=[smem] * 3 + [vmem, rows_spec] + [vmem] * len(pieces_two),
        out_specs=saved_specs + [vmem] * 7,
        scratch_shapes=[
            pltpu.VMEM((devices, shard_two.shape[0], 128), BF),
            pltpu.VMEM((ROWS_OUT, D), F32),
            pltpu.VMEM((8, HEAD_ROOM, 128), F32),
            pltpu.VMEM((n, D), F32),
            pltpu.VMEM((images, TK, D), BF),
            pltpu.VMEM((images, TK, D), BF),
            pltpu.VMEM((n, D), BF),
            pltpu.VMEM((n, D), BF),
        ]
        + [pltpu.VMEM((16, D), F32)] * 6
        + [pltpu.VMEM((n, D), BF)],
        compiler_params=params,
        cost_estimate=cost(30),
        name="forward",
    )(groups, labels, number, flat, x1, *pieces_two)

    mom_shard = jnp.concatenate([jnp.transpose(wide_mom, (0, 2, 1)), down_mom], 1)
    mom_all = lax.all_gather(mom_shard, AXES, axis=0)
    factors, mom_all = lax.optimization_barrier((factors, mom_all))
    gstream, factors = lax.optimization_barrier((gstream, factors))
    factors_all = lax.all_gather(factors, AXES, axis=0)
    back_scratch = [
        pltpu.VMEM((n, D), BF),
        pltpu.VMEM((n, FF), BF),
        pltpu.VMEM((n, D), BF),
        pltpu.VMEM((n, D), BF),
        pltpu.VMEM((n, D), BF),
        pltpu.VMEM((n, D), BF),
        pltpu.VMEM((n, D), BF),
        pltpu.VMEM((n, D), BF),
        pltpu.VMEM((n, D), BF),
        pltpu.VMEM((n, FF), BF),
    ]
    gstream1, middle_keep, middle_send = pl.pallas_call(
        functools.partial(middle_kernel, images),
        out_shape=[
            S((n, D), F32),
            S((MIDDLE_ROWS // 2, 128), F32),
            S((MIDDLE_ROWS // 2, 128), F32),
        ],
        grid=(images,),
        in_specs=[smem] * 2 + [rows_spec] + saved_specs + [vmem, rows_spec] + [vmem] * 4,
        out_specs=[rows_spec] + [vmem] * 2,
        scratch_shapes=[
            pltpu.VMEM((8, D), F32),
            pltpu.VMEM((8, FF), F32),
            pltpu.VMEM((MIDDLE_ROWS, 128), F32),
        ]
        + back_scratch,
        compiler_params=params,
        cost_estimate=cost(23),
        name="middle",
    )(groups, number, x1, *saved1, gains1, gstream, wt12, dn12, kv, small)

    first_keep, first_send = pl.pallas_call(
        functools.partial(first_kernel, images),
        out_shape=[S((FIRST_ROWS // 2, 128), F32)] * 2,
        grid=(images,),
        in_specs=[smem] * 2
        + [rows_spec]
        + saved_specs
        + [vmem, rows_spec]
        + [vmem] * 2
        + [patch_spec],
        out_specs=[vmem] * 2,
        scratch_shapes=[
            pltpu.VMEM((FIRST_ROWS, 128), F32),
            pltpu.VMEM((TQ, D), F32),
            pltpu.VMEM((8, D), F32),
            pltpu.VMEM((8, FF), F32),
            pltpu.VMEM((2, PATCH_DIM, 128), F32),
            pltpu.VMEM((2, TQ + 16, 128), F32),
        ]
        + back_scratch,
        compiler_params=params,
        cost_estimate=cost(25),
        name="first",
    )(groups, number, x0, *saved0, gains0, gstream1, wt0, dn0, patches)

    late_params = pltpu.CompilerParams(
        vmem_limit_bytes=12 * 1024 * 1024 + 1024 * devices * factor_rows
    )
    exact, extra = pl.pallas_call(
        functools.partial(coefficient_kernel, devices),
        grid=(1,),
        out_shape=[S((EXACT_ROWS, 128), F32), S((16, 128), F32)],
        in_specs=[pl.BlockSpec((devices, EXACT_ROWS, 128), lambda i: (0, 0, 0)), vmem],
        out_specs=[vmem] * 2,
        compiler_params=late_params,
        cost_estimate=cost(2),
        name="coefficients",
    )(factors_all, basis_block)

    g2, headflat = pl.pallas_call(
        functools.partial(late_kernel, devices, images),
        out_shape=[S((ROWS_OUT, D), F32), S((HEAD_FLAT_ROOM, 128), F32)],
        in_specs=[vmem],
        out_specs=[vmem] * 2,
        scratch_shapes=[pltpu.VMEM((8, HEAD_ROOM, 128), F32)],
        compiler_params=late_params,
        cost_estimate=cost(4),
        name="late",
    )(factors_all.reshape(devices * factor_rows, 128))

    split_bits = 5
    for bit in range(split_bits, bits):
        extra = extra + swap(extra, 1 << bit, devices)
    if bits > split_bits:
        c = extra[0] + extra[1] + extra[2]
        split = []
        for k in range(3):
            split.append(lax.reduce_precision(c, 8, 7))
            c = c - split[-1]
        extra = jnp.concatenate([jnp.stack(split), extra[3:]], 0)
    quarter = (MIDDLE_ROWS + FIRST_ROWS) // 8
    small_params = pltpu.CompilerParams(vmem_limit_bytes=16 * 1024 * 1024)
    total, *sends = pl.pallas_call(
        combine_kernel,
        out_shape=[S((quarter, 128), F32)] + [S((quarter, 128), BF)] * 3,
        in_specs=[smem] + [vmem] * 4,
        out_specs=[vmem] * 4,
        compiler_params=small_params,
        cost_estimate=cost(2),
        name="combine",
    )(
        ((me >> 1) & 3)[None],
        middle_keep,
        swap(middle_send, 1, devices),
        first_keep,
        swap(first_send, 1, devices),
    )
    for m in range(1, 4):
        total = total + swap(sends[m - 1], m << 1, devices).astype(F32)
    mr, fr = MIDDLE_ROWS // 8, FIRST_ROWS // 8
    kept = jnp.concatenate(
        [total[:mr].reshape(4, mr // 4, 128), total[mr:].reshape(4, fr // 4, 128)], 1
    )
    mine = (me >> 3) & 3
    total = lax.dynamic_index_in_dim(kept, mine, 0, keepdims=False)
    for m in range(1, 4):
        send = lax.dynamic_index_in_dim(kept, mine ^ m, 0, keepdims=False)
        if m == 3:
            send = send + 0.0 * extra[0, 0]
        total = total + swap(send.astype(BF), m << 3, devices).astype(F32)
    kept = total
    for bit in range(split_bits, bits):
        small_part = kept.astype(BF)
        kept = small_part.astype(F32) + swap(small_part, 1 << bit, devices).astype(F32)
    piece = jnp.concatenate([kept, extra], 0).astype(BF)[None]
    piece = gather_stages([piece], number_of[2:], devices, 0)[0]
    pieces = [piece] + [swap(piece, m << 1, devices) for m in range(1, 3)]
    pieces = pieces + [swap(piece + (0.0 * g2[0, 0]).astype(BF), 3 << 1, devices)]
    pieces = pieces + [swap(p, 1, devices) for p in pieces]

    first_column = me * column_width
    in_q = first_column < 3 * D
    in_o = first_column < 4 * D
    start = jnp.where(in_q, 0, jnp.where(in_o, 3 * D, 4 * D))
    count = jnp.where(in_q, 3 * D, jnp.where(in_o, D, FF))
    piece_number = ((me & 1) << 4) | (((me >> 1) & 3) << 2) | ((me >> 3) & 3)
    at = me * share
    spots = jnp.stack(
        [start, count, first_column, WIDE + me * row_width, piece_number, at // 128, at % 128]
    )
    wide_shape = (LAYERS, column_width, D)
    down_shape = (LAYERS, row_width, D)
    flat_rows = -(-((devices - 1) * share // 128 + rows + 24) // 8) * 8
    (
        wide_new,
        wide_mom_new,
        wide_copy,
        down_new,
        down_mom_new,
        down_copy,
        share_grad,
        scal,
    ) = pl.pallas_call(
        functools.partial(muon_kernel, column_width, row_width, len(pieces)),
        out_shape=[
            S(wide_shape, F32),
            S(wide_shape, F32),
            S(wide_shape, BF),
            S(down_shape, F32),
            S(down_shape, F32),
            S(down_shape, BF),
            S((rows, 128), F32),
            S((8, 128), F32),
        ],
        in_specs=[smem]
        + [vmem] * (len(pieces) + 4)
        + [pl.BlockSpec(memory_space=pltpu.HBM)]
        + [vmem] * 4,
        out_specs=[vmem] * 8,
        scratch_shapes=[
            pltpu.VMEM((flat_rows, 128), F32),
            pltpu.VMEM((MIDDLE_ROWS, 128), BF),
            pltpu.VMEM((FIRST_ROWS, 128), BF),
            pltpu.VMEM((16 * 32, 128), F32),
            pltpu.VMEM((LAYERS, ROWS_OUT + 16, D), F32),
            pltpu.VMEM((2 * LAYERS, D, D), F32),
            pltpu.VMEM((2 * LAYERS, -(-max(column_width, row_width) // 8) * 8, D), F32),
            pltpu.VMEM((LAYERS, devices, column_width + row_width, D), F32),
            pltpu.SemaphoreType.DMA((LAYERS,)),
        ],
        compiler_params=pltpu.CompilerParams(vmem_limit_bytes=48 * 1024 * 1024),
        cost_estimate=cost(20),
        name="muon",
    )(
        spots.astype(jnp.int32),
        *pieces,
        g2,
        headflat,
        exact,
        basis_block,
        mom_all,
        wide_t,
        jnp.transpose(wide_mom, (0, 2, 1)),
        down_w,
        down_mom,
    )
    grad_norm, _, removed_norm, loss_sum = [scal[k, 0] for k in range(4)]
    clipped = share_grad.reshape(-1)[:share]
    first_new = BETA_ONE * plain_first + (1.0 - BETA_ONE) * clipped
    second_new = BETA_TWO * plain_second + (1.0 - BETA_TWO) * clipped * clipped
    first_hat = first_new / (1.0 - BETA_ONE**STEP)
    second_hat = second_new / (1.0 - BETA_TWO**STEP)
    plain_new = plain - ADAM_RATE * (
        first_hat / (jnp.sqrt(second_hat) + ADAM_EPS) + DECAY_RATE * plain
    )
    plain_copy = plain_new.astype(BF)
    return (
        loss_sum,
        removed_norm,
        grad_norm,
        *[jnp.transpose(x, (0, 2, 1)) for x in (wide_new, wide_mom_new, wide_copy)],
        down_new,
        down_mom_new,
        down_copy,
        plain_new,
        first_new,
        second_new,
        plain_copy,
    )


def solution(mesh):
    placed = (
        P(AXES, None, None),
        P(AXES),
        P(AXES),
        P(None, None, AXES),
        P(None, AXES, None),
        P(AXES),
        P(None, None, AXES),
        P(None, AXES, None),
        P(AXES),
        P(AXES),
        P(None, AXES),
    )
    return jax.shard_map(
        local,
        mesh=mesh,
        in_specs=placed,
        out_specs=(
            P(),
            P(),
            P(),
            P(None, None, AXES),
            P(None, None, AXES),
            P(None, None, AXES),
            P(None, AXES, None),
            P(None, AXES, None),
            P(None, AXES, None),
            P(AXES),
            P(AXES),
            P(AXES),
            P(AXES),
        ),
        check_vma=False,
    )
```
